32 devices in a mesh: tm: 2 (over y), lat: 16 (over z, x, core).
Axes of the slice: x: 2, y: 2, z: 4, core: 2. Of those that a mesh axis runs over, the one named last changes fastest.
Arguments:
- background: bfloat16 [4, 2, 256, 2048], P('tm', None, 'lat'), may hold values from -12 to 12
- conv_weight: bfloat16 [32, 90], replicated, may hold values from -0.625 to 0.625
- conv_bias: float32 [32], replicated, may hold values from -3 to 3
- mix_weight: bfloat16 [32, 32], replicated, may hold values from -1 to 1
- mix_bias: float32 [32], replicated, may hold values from -3 to 3
- out_weight: bfloat16 [2, 32], replicated, may hold values from -0.1875 to 0.1875
- out_bias: float32 [2], replicated, may hold values from -0.3 to 0.3
- drift_east: float32 [256, 2048], P('lat', 'tm'), may hold values from -0.2 to 0.2
- drift_north: float32 [256, 2048], P('lat', 'tm'), may hold values from -0.2 to 0.2
- diffusivity: float32 [256, 2048], P('lat', 'tm'), may hold values from 0.1 to 0.24
- sensors: int32 [4, 16, 2, 128], P(None, 'lat', 'tm'), may hold values from 0 to 16383, as said below
- observations: float32 [4, 16, 2, 2, 128], P(None, 'lat', 'tm'), may hold values from -6 to 6
Outputs:
- total_score: float32 [4, 2, 256, 2048], P('tm', None, 'lat')
The draws below stay inside these ranges and needn't reach their ends.
Inputs may be any that keep to these rules, and one draw needn't show every extreme that they name: `sensors`: each entry is a cell of its tile counted row by row over 16 rows of 1024 cells; cells may repeat.
All inputs are finite; a program needn't handle non-finite values.
Results may differ from the reference program's by a relative error of at most 0.0039.
Values may be sent and summed in bfloat16 or wider, within the bound.
No kernel may reach another device: no remote copies, remote signals or barrier semaphores. Data moves between devices by JAX's collectives and lax.ppermute only.
A program may use at most 128 MiB of HBM per device.

```python
import jax
import jax.numpy as jnp
from jax import lax

LAT_DEV = 16
LON = 2048
VARS = 2
HID = 32
KT = 5
SUB = 3
SENS = 128
TAPS = 90
FRAMES = 4
LAT = 256
TILE = 1024
N_TM = 2
N_LAT = 16


def draw_sensors(key, part):
    shape = (FRAMES, N_LAT, N_TM, SENS)
    keys = jax.random.split(key, 6)
    side = jax.random.randint(keys[0], shape, 0, 4)
    depth = jax.random.randint(keys[1], shape, 0, 2)
    along_row = jax.random.randint(keys[2], shape, 0, TILE)
    along_col = jax.random.randint(keys[3], shape, 0, LAT_DEV)
    picker = jax.random.randint(keys[4], shape, 0, 8)
    anywhere = jax.random.randint(keys[5], shape, 0, LAT_DEV * TILE)
    cell_row = jnp.where(side == 0, depth, jnp.where(side == 1, LAT_DEV - 1 - depth, along_col))
    cell_col = jnp.where(side == 2, depth, jnp.where(side == 3, TILE - 1 - depth, along_row))
    rim_cell = cell_row * TILE + cell_col
    return jnp.where(picker < 7, rim_cell, anywhere).astype(jnp.int32)


def steps_of(rng, extent, pieces, least, high):
    gain, own = 1.0, jax.random.fold_in(rng, 6)
    for position, parts in pieces:
        draws = jnp.exp(jax.random.uniform(jax.random.fold_in(own, position), (parts,), jnp.float32, least / len(pieces), high / len(pieces)))
        gain = gain * jnp.repeat(draws, extent[position] // parts).reshape([-1 if axis == position else 1 for axis in range(len(extent))])
    return gain


def gaussian(stream_key, dims, width, reach, cuts=(), held_as=jnp.bfloat16):
    array = width * jax.random.normal(stream_key, dims, jnp.float32)
    if cuts:
        array = array * steps_of(stream_key, dims, cuts, -0.22, 0.18)
    return jnp.clip(array, -reach, reach).astype(held_as)


def setup_inputs(seed: int = 0) -> dict:
    streams_of = jax.random.split(jax.random.key(seed), 13)
    background = gaussian(streams_of[0], (FRAMES, VARS, LAT, LON), 2.0, 12.0, ((0, 2), (2, 16)))
    conv_weight = gaussian(streams_of[1], (HID, TAPS), TAPS ** -0.5, 0.625)
    conv_bias = gaussian(streams_of[2], (HID,), 0.5, 3.0, (), jnp.float32)
    mix_weight = gaussian(streams_of[3], (HID, HID), HID ** -0.5, 1.0)
    mix_bias = gaussian(streams_of[4], (HID,), 0.5, 3.0, (), jnp.float32)
    out_weight = gaussian(streams_of[5], (VARS, HID), (32 * HID) ** -0.5, 0.1875)
    out_bias = gaussian(streams_of[6], (VARS,), 0.05, 0.3, (), jnp.float32)
    drift_east = jnp.clip(jax.random.uniform(streams_of[7], (LAT, LON), jnp.float32, -0.2, 0.2) * steps_of(streams_of[7], (LAT, LON), ((0, 16), (1, 2)), -0.4, 0.0), -0.2, 0.2)
    drift_north = jnp.clip(jax.random.uniform(streams_of[8], (LAT, LON), jnp.float32, -0.2, 0.2) * steps_of(streams_of[8], (LAT, LON), ((0, 16), (1, 2)), -0.4, 0.0), -0.2, 0.2)
    diffusivity = jnp.clip(0.1 + 0.13999999 * jax.random.uniform(streams_of[9], (LAT, LON), jnp.float32) ** steps_of(streams_of[9], (LAT, LON), ((0, 16), (1, 2)), -0.2, 0.2), 0.1, 0.24)
    sensors = draw_sensors(jax.random.fold_in(streams_of[12], 71), 0)
    observations = gaussian(streams_of[11], (FRAMES, N_LAT, N_TM, VARS, SENS), 1.0, 6.0, ((1, 16), (2, 2)), jnp.float32)
    return {"background": background, "conv_weight": conv_weight, "conv_bias": conv_bias, "mix_weight": mix_weight, "mix_bias": mix_bias, "out_weight": out_weight, "out_bias": out_bias, "drift_east": drift_east, "drift_north": drift_north, "diffusivity": diffusivity, "sensors": sensors, "observations": observations}


def lon_shifted(values, offset):
    return jnp.roll(values, -offset, axis=-1)


def conv_frame(window, conv_weight, conv_bias, mix_weight, mix_bias, out_weight, out_bias):
    row_count = window.shape[2] - 2
    tap_list = []
    for channel in range(window.shape[1]):
        for time_lag in range(window.shape[0]):
            for row_offset in range(3):
                for col_offset in range(3):
                    tap_list.append(lon_shifted(window[time_lag, channel, row_offset:row_offset + row_count], col_offset - 1))
    patches = jnp.stack(tap_list)
    hidden_one = jnp.einsum("hk,kyx->hyx", conv_weight, patches, preferred_element_type=jnp.float32) + conv_bias[:, None, None]
    hidden_one = jax.nn.gelu(hidden_one).astype(jnp.bfloat16)
    hidden_two = jnp.einsum("gh,hyx->gyx", mix_weight, hidden_one, preferred_element_type=jnp.float32) + mix_bias[:, None, None]
    hidden_two = jax.nn.gelu(hidden_two).astype(jnp.bfloat16)
    return jnp.einsum("ch,hyx->cyx", out_weight, hidden_two, preferred_element_type=jnp.float32) + out_bias[:, None, None]


def advance_one_step(values, coefficients):
    center_cell = values[..., 1:-1, 1:-1]
    east_cell = values[..., 1:-1, 2:]
    west_cell = values[..., 1:-1, :-2]
    north_cell = values[..., 2:, 1:-1]
    south_cell = values[..., :-2, 1:-1]
    drift_a = coefficients[0, 0, 1:-1, 1:-1]
    drift_b = coefficients[1, 0, 1:-1, 1:-1]
    diff_k = coefficients[2, 0, 1:-1, 1:-1]
    return (center_cell - drift_a * (east_cell - west_cell) * 0.5 - drift_b * (north_cell - south_cell) * 0.5
            + diff_k * (east_cell + west_cell + north_cell + south_cell - 4.0 * center_cell))


def adjoint_step(values, coefficients):
    drift_a = coefficients[0, 0]
    drift_b = coefficients[1, 0]
    diff_k = coefficients[2, 0]
    from_west = values * (diff_k - 0.5 * drift_a)
    from_east = values * (diff_k + 0.5 * drift_a)
    from_south = values * (diff_k - 0.5 * drift_b)
    from_north = values * (diff_k + 0.5 * drift_b)
    center_cell = values[..., 1:-1, 1:-1]
    return ((1.0 - 4.0 * diff_k[1:-1, 1:-1]) * center_cell + from_west[..., 1:-1, :-2] + from_east[..., 1:-1, 2:]
            + from_south[..., :-2, 1:-1] + from_north[..., 2:, 1:-1])


def pad_field(values, border_width):
    tall_field = jnp.pad(values, [(0, 0)] * (values.ndim - 2) + [(border_width, border_width), (0, 0)])
    return jnp.concatenate([tall_field[..., -border_width:], tall_field, tall_field[..., :border_width]], axis=-1)


def reference(background, conv_weight, conv_bias, mix_weight, mix_bias, out_weight, out_bias,
              drift_east, drift_north, diffusivity, sensors, observations):
    coefficients = jnp.stack([drift_east, drift_north, diffusivity])[:, None]
    widened_coefficients = pad_field(coefficients, 1)
    padded = jnp.pad(background, ((2, 2), (0, 0), (1, 1), (0, 0)))
    tile_cols = LON // N_TM
    tile_row = jnp.arange(N_LAT, dtype=jnp.int32)[None, :, None, None]
    tile_col = jnp.arange(N_TM, dtype=jnp.int32)[None, None, :, None]
    global_row = tile_row * LAT_DEV + sensors // tile_cols
    global_col = tile_col * tile_cols + sensors % tile_cols
    cell_index = (global_row * LON + global_col).reshape(FRAMES, -1)
    obs_rows = observations.transpose(0, 3, 1, 2, 4).reshape(FRAMES, VARS, -1)

    def one_frame(frame_index):
        window = lax.dynamic_slice_in_dim(padded, frame_index, KT, 0)
        prior_score = conv_frame(window, conv_weight, conv_bias, mix_weight, mix_bias, out_weight, out_bias)
        present_values = lax.dynamic_index_in_dim(background, frame_index, 0, False).astype(jnp.float32)
        for step_count in range(SUB):
            present_values = advance_one_step(pad_field(present_values, 1), widened_coefficients)
        flattened_field = present_values.reshape(VARS, -1)
        frame_cells = lax.dynamic_index_in_dim(cell_index, frame_index, 0, False)
        frame_obs = lax.dynamic_index_in_dim(obs_rows, frame_index, 0, False)
        misfit = flattened_field[:, frame_cells] - frame_obs
        diffusion_spread = jnp.zeros_like(flattened_field).at[:, frame_cells].add(misfit).reshape(VARS, LAT, LON)
        for step_count in range(SUB):
            diffusion_spread = adjoint_step(pad_field(diffusion_spread, 1), widened_coefficients)
        return prior_score - diffusion_spread

    return lax.map(one_frame, jnp.arange(FRAMES, dtype=jnp.int32))
```

```python
import functools

import jax
import jax.numpy as jnp
import numpy as np
from jax import lax
from jax.experimental import pallas as pl
from jax.experimental.pallas import tpu as pltpu
from jax.sharding import PartitionSpec as P

KT = 5
SUB = 3
K_MID = 0.17
HALO = 2 * SUB
CROWS = 2 * SUB - 1
BF = jnp.bfloat16
F32 = jnp.float32
VMEM_BYTES = 48 * 1024 * 1024
GELU_1 = 2.0 * float(np.sqrt(2.0 / np.pi))
GELU_2 = 8.0 * 0.044715 * float(np.sqrt(2.0 / np.pi))


def dot(a, b):
    return jnp.dot(a, b, preferred_element_type=F32)


def dot_t(a, b):
    return lax.dot_general(a, b, (((1,), (1,)), ((), ())), preferred_element_type=F32)


def split2(x):
    high = x.astype(BF)
    return high, (x - high.astype(F32)).astype(BF)


def pack_table(rows, fields):
    table = np.zeros((2, 2, 96, 128), np.float32)
    coef_row = fields * rows
    for parity in range(2):
        for side in range(2):
            for message in range(4):
                far, diagonal = message % 2, message // 2
                bottom = (far == 0) == (parity == 0)
                base = 64 + 16 * far if diagonal else 32 * far
                height = 16 if diagonal else 32
                out = table[parity, side]
                if diagonal:
                    for field in range(fields):
                        out[base + field, field * rows + (rows - 1 if bottom else 0)] = 1
                else:
                    for field in range(fields):
                        for e in range(HALO):
                            row = rows - HALO + e if bottom else e
                            out[base + field * HALO + e, field * rows + row] = 1
                for slot in range(8):
                    j = side * 8 + slot
                    target = base + height - 8 + slot
                    if j < 3 * CROWS:
                        c, e = divmod(j, CROWS)
                        row = rows - CROWS + e if bottom else e
                        out[target, coef_row + c * rows + row] = 1
                    else:
                        out[target, coef_row + 3 * rows + (15 if diagonal else 14)] = 1
    return table


def near_far(case):
    parity = case in (1, 3)
    top_ok = case != 2
    bottom_ok = case not in (3, 4)
    top_slot = 0 if parity else 1
    return top_slot, 1 - top_slot, top_ok, bottom_ok


def model_tables(rows, frames, variables, quarters):
    lanes = quarters * variables
    own = np.zeros((rows * lanes, quarters * variables * rows), np.float32)
    coef = np.zeros((rows * lanes, quarters * rows), np.float32)
    out = np.zeros((lanes * rows, rows * lanes), np.float32)
    for r in range(rows):
        for q in range(quarters):
            for v in range(variables):
                own[r * lanes + q * variables + v, (q * variables + v) * rows + r] = 1
                coef[r * lanes + q * variables + v, q * rows + r] = 1
                out[(q * variables + v) * rows + r, r * lanes + q * variables + v] = 1
    halo = np.zeros((5, frames, 2 * HALO * lanes, quarters * 64), np.float32)
    chalo = np.zeros((5, 3 * 2 * CROWS * lanes, quarters * 64), np.float32)
    for case in range(5):
        top_slot, bottom_slot, top_ok, bottom_ok = near_far(case)
        for q in range(quarters):
            for v in range(variables):
                lane = q * variables + v
                for half, slot, ok in ((0, top_slot, top_ok), (1, bottom_slot, bottom_ok)):
                    if not ok:
                        continue
                    for t in range(frames):
                        for e in range(HALO):
                            local = (t * variables + v) * HALO + e
                            halo[case, t, (half * HALO + e) * lanes + lane, q * 64 + slot * 32 + local] = 1
                    for c in range(3):
                        for e in range(CROWS):
                            j = c * CROWS + e
                            column = q * 64 + slot * 32 + (j // 8) * 16 + 8 + j % 8
                            row = ((c * 2 + half) * CROWS + e) * lanes + lane
                            chalo[case, row, column] = 1.0 if c == 2 else 0.5
    return own, coef, out, halo, chalo


def conv_table(rows, frames, others, variables, group):
    channels = (frames + others) * variables
    tall = group + 2
    own_rows = frames * variables * rows
    oth_rows = others * variables * rows
    table = np.zeros((5, rows // group * tall * channels, own_rows + oth_rows + 96), np.float32)
    for case in range(5):
        top_slot, bottom_slot, top_ok, bottom_ok = near_far(case)
        for g in range(rows // group):
            for yy in range(tall):
                y = g * group + yy - 1
                for f in range(frames + others):
                    for v in range(variables):
                        target = (g * tall + yy) * channels + f * variables + v
                        own = f < frames
                        field = (f if own else f - frames) * variables + v
                        if 0 <= y < rows:
                            table[case, target, (0 if own else own_rows) + field * rows + y] = 1
                            continue
                        slot, ok = (top_slot, top_ok) if y < 0 else (bottom_slot, bottom_ok)
                        if not ok:
                            continue
                        if own:
                            column = own_rows + oth_rows + slot * 32
                            column += field * HALO + (HALO - 1 if y < 0 else 0)
                        else:
                            column = own_rows + oth_rows + 64 + slot * 16 + field
                        table[case, target, column] = 1
    return table


def tap_table(offsets, frames, variables, group, depth):
    channels = len(offsets) * variables
    tall = group + 2
    table = np.full((frames * group, depth), -1, np.int32)
    for t in range(frames):
        for y in range(group):
            for s in range(3):
                for yy in range(tall):
                    for f, offset in enumerate(offsets):
                        for v in range(variables):
                            lag, i = offset - t + KT // 2, yy - y
                            if 0 <= lag < KT and 0 <= i < 3:
                                k = s * tall * channels + yy * channels + f * variables + v
                                table[t * group + y, k] = ((v * KT + lag) * 3 + i) * 3 + s
            for part in range(3):
                table[t * group + y, 3 * tall * channels + part] = 3 * 3 * KT * variables + part
    return table


def case_of(parity, index, count):
    return jnp.where(index == 0, 2, jnp.where(index == count - 1, jnp.where(parity == 1, 3, 4), parity))


def pack_kernel(bg, east, north, diff, sensors, obs, table, p0, near, far, dnear, dfar, *, frames):
    me_t = lax.axis_index("tm")
    parity = lax.axis_index("lat") % 2
    fields = bg.shape[0] * bg.shape[1]
    rows, lon = bg.shape[2], bg.shape[3]
    half = lon // 2
    fields_2d = bg[...].reshape(fields * rows, lon)
    a, b = east[...].astype(BF), north[...].astype(BF)
    k = (diff[...] - K_MID).astype(BF)

    def described(first, low):
        pieces = []
        for t in range(frames):
            cells = sensors[first + t, 0]
            if not low:
                pieces += [(cells >> 8).astype(F32), (cells & 255).astype(F32)]
            for v in range(obs.shape[3]):
                value = obs[first + t, 0, 0, v : v + 1]
                high = value.astype(BF).astype(F32)
                pieces.append(value - high if low else high)
        row = jnp.concatenate(pieces, axis=1)
        if row.shape[1] < half:
            row = jnp.concatenate([row, jnp.zeros((1, half - row.shape[1]), F32)], axis=1)
        return row

    mine, theirs = me_t * frames, (1 - me_t) * frames
    extra = jnp.concatenate(
        [
            jnp.zeros((12, half), F32),
            described(mine, True),
            described(theirs, True),
            described(mine, False),
            described(theirs, False),
        ],
        axis=0,
    ).astype(BF)
    split = fields * rows
    p0[0:split, :] = fields_2d
    p0[split : split + rows, 0:half] = a
    p0[split + rows : split + 2 * rows, 0:half] = b
    p0[split : split + rows, half:lon] = k
    p0[split + rows : split + 2 * rows, half:lon] = extra
    for side in range(2):
        cut = slice(side * half, (side + 1) * half)
        source = jnp.concatenate([fields_2d[:, cut], a, b, k, extra], axis=0)
        message = dot(table[parity, side], source).astype(BF)
        near[:, cut] = message[0:32]
        far[:, cut] = message[32:64]
        dnear[:, cut] = message[64:80]
        dfar[:, cut] = message[80:96]


def prep_kernel(conv_w, conv_b, mix_w, mix_b, out_w, out_b, taps, w1, w2, w3, b2, b3, *, group, i_of):
    hid = mix_w.shape[0]
    table = taps[i_of()]

    def column(row):
        n = row.shape[1]
        here = lax.broadcasted_iota(jnp.int32, (n, n), 0) == lax.broadcasted_iota(jnp.int32, (n, n), 1)
        return jnp.sum(jnp.where(here, jnp.broadcast_to(row, (n, n)), 0.0), axis=1, keepdims=True)

    bias = 0.5 * column(conv_b[...])
    pieces = []
    for _ in range(3):
        piece = bias.astype(BF)
        bias = bias - piece.astype(F32)
        pieces.append(piece.astype(F32))
    ntap = conv_w.shape[1]
    padded = 128
    weights = jnp.concatenate(
        [0.5 * conv_w[...].astype(F32)] + pieces + [jnp.zeros((hid, padded - ntap - 3), F32)], axis=1
    ).astype(BF)
    tap_id = lax.broadcasted_iota(jnp.int32, (padded, table.shape[1]), 0)
    for ty in range(table.shape[0]):
        chosen = jnp.where(tap_id == table[ty : ty + 1, :], 1.0, 0.0).astype(BF)
        w1[ty * hid : (ty + 1) * hid, :] = dot(weights, chosen).astype(BF)
    tall = group * hid
    row = lax.broadcasted_iota(jnp.int32, (tall, hid), 0) & (hid - 1)
    up = jnp.where(row == lax.broadcasted_iota(jnp.int32, (tall, hid), 1), 1.0, 0.0).astype(BF)
    mixed = dot_t(dot(up, (0.5 * mix_w[...].astype(F32)).astype(BF)).astype(BF), up)
    shift = hid.bit_length() - 1
    rows2 = lax.broadcasted_iota(jnp.int32, (tall, tall), 0) >> shift
    cols2 = lax.broadcasted_iota(jnp.int32, (tall, tall), 1) >> shift
    w2[...] = jnp.where(rows2 == cols2, mixed, 0.0).astype(BF)
    variables = out_w.shape[0]
    spread = dot_t(out_w[...], up)
    parts, parts_b = [], []
    for v in range(variables):
        here = lax.broadcasted_iota(jnp.int32, (group, tall), 0) == (
            lax.broadcasted_iota(jnp.int32, (group, tall), 1) >> shift
        )
        parts.append(jnp.where(here, jnp.broadcast_to(spread[v : v + 1], (group, tall)), 0.0))
        parts_b.append(jnp.broadcast_to(out_b[:, v : v + 1], (group, 128)))
    w3[...] = jnp.concatenate(parts, axis=0).astype(BF)
    b3[...] = jnp.concatenate(parts_b, axis=0)
    mixed_bias = jnp.broadcast_to(0.5 * column(mix_b[...]), (hid, 128))
    b2[...] = jnp.concatenate([mixed_bias] * group, axis=0)


def model_kernel(
    p0, r0, near, far, dnear, dfar, *rest,
    rows, frames, variables, own_bg, oth_bg, tile_cols, n_sens, paired, i_of, parity_of,
):
    sens = None if paired else rest[0]
    p_own, p_coef, p_out, p_halo, p_chalo, out, field_a, field_b, coefs = rest[-9:]
    lon = p0.shape[1]
    half = lon // 2
    quarters = 8 // variables
    width = half // quarters
    me_l, count = lax.axis_index("lat"), lax.axis_size("lat")
    parity = parity_of()
    me_t = i_of()
    case = case_of(parity, me_l, count)
    top_ok, bottom_ok = me_l > 0, me_l < count - 1
    tall = rows + 2 * HALO

    for t in range(frames):
        for h in range(2):
            g = t * 2 + h
            body, rim = [], []
            for q in range(quarters):
                cut = slice(h * half + q * width, h * half + (q + 1) * width)
                body.append(p0[t * variables * rows : (t + 1) * variables * rows, cut])
                rim += [near[:, cut], far[:, cut]]
            field_a[g, HALO : HALO + rows] = dot(p_own[...], jnp.concatenate(body, axis=0)).reshape(rows, 8, width)
            edges = dot(p_halo[case, t], jnp.concatenate(rim, axis=0)).reshape(2 * HALO, 8, width)
            field_a[g, 0:HALO] = edges[0:HALO]
            field_a[g, HALO + rows : tall] = edges[HALO:]

    ctall = rows + 2 * CROWS
    for source in range(2):
        big, at = (p0, own_bg) if source == 0 else (r0, oth_bg)
        spot = me_t if source == 0 else 1 - me_t
        m_near, m_far = (near, far) if source == 0 else (dnear, dfar)
        last = m_near.shape[0]
        pieces = []
        for side in range(2):
            for c_row in range(2):
                stack = []
                for q in range(quarters):
                    cut = slice(side * half + q * width, side * half + (q + 1) * width)
                    stack.append(big[at + c_row * rows : at + (c_row + 1) * rows, cut])
                pieces.append(jnp.concatenate(stack, axis=0))
        scaled = p_coef[...]
        ha = (0.5 * dot(scaled, pieces[0])).reshape(rows, 8, width)
        hb = (0.5 * dot(scaled, pieces[1])).reshape(rows, 8, width)
        kk = dot(scaled, pieces[2]).reshape(rows, 8, width) + K_MID
        rim = []
        for q in range(quarters):
            for message in (m_near, m_far):
                for side in range(2):
                    cut = slice(side * half + q * width, side * half + (q + 1) * width)
                    rim.append(message[last - 16 : last, cut])
        edges = dot(p_chalo[case], jnp.concatenate(rim, axis=0)).reshape(3, 2, CROWS, 8, width)
        k_top = edges[2, 0] + jnp.where(top_ok, K_MID, 0.0)
        k_bottom = edges[2, 1] + jnp.where(bottom_ok, K_MID, 0.0)
        for start, size, xa, xb, xk in (
            (0, CROWS, edges[0, 0], edges[1, 0], k_top),
            (CROWS, rows, ha, hb, kk),
            (CROWS + rows, CROWS, edges[0, 1], edges[1, 1], k_bottom),
        ):
            span = slice(start, start + size)
            coefs[spot, 0, span] = xk - xa
            coefs[spot, 1, span] = xk + xa
            coefs[spot, 2, span] = xk - xb
            coefs[spot, 3, span] = xk + xb
            coefs[spot, 4, span] = 1.0 - 4.0 * xk

    lane = lax.broadcasted_iota(jnp.int32, (8, 128), 1)
    sub_q = lax.broadcasted_iota(jnp.int32, (8, 128), 0) >> (variables.bit_length() - 1)
    first_lane, last_lane = lane == 0, lane == 127
    first_q, last_q = sub_q == 0, sub_q == quarters - 1
    tiles = width // 128

    def cut_tiles(x):
        return [x[:, n * 128 : (n + 1) * 128] for n in range(tiles)]

    def from_west(x0, x1):
        both = [[pltpu.roll(part, 1, 1) for part in cut_tiles(x)] for x in (x0, x1)]
        result = []
        for h in range(2):
            wrapped = jnp.where(last_q, both[1 - h][-1], both[h][-1])
            carry = pltpu.roll(wrapped, variables, 0)
            parts = []
            for n in range(tiles):
                parts.append(jnp.where(first_lane, carry if n == 0 else both[h][n - 1], both[h][n]))
            result.append(jnp.concatenate(parts, axis=1))
        return result

    def from_east(x0, x1):
        both = [[pltpu.roll(part, 127, 1) for part in cut_tiles(x)] for x in (x0, x1)]
        result = []
        for h in range(2):
            wrapped = jnp.where(first_q, both[1 - h][0], both[h][0])
            carry = pltpu.roll(wrapped, 8 - variables, 0)
            parts = []
            for n in range(tiles):
                parts.append(
                    jnp.where(last_lane, carry if n == tiles - 1 else both[h][n + 1], both[h][n])
                )
            result.append(jnp.concatenate(parts, axis=1))
        return result

    def forward(source, target, low, high):
        def row_step(r, _):
            cr = r - (HALO - CROWS)
            for t in range(frames):
                center = [source[t * 2 + h, r] for h in range(2)]
                west, east = from_west(*center), from_east(*center)
                for h in range(2):
                    g = t * 2 + h
                    target[g, r] = (
                        (coefs[h, 4, cr] * center[h] + coefs[h, 0, cr] * east[h])
                        + (coefs[h, 1, cr] * west[h] + coefs[h, 2, cr] * source[g, r + 1])
                        + coefs[h, 3, cr] * source[g, r - 1]
                    )
            return 0

        lax.fori_loop(low, high, row_step, 0, unroll=2)

    def backward(source, target, low, high):
        def row_step(r, _):
            cr = r - (HALO - CROWS)
            for t in range(frames):
                center = [source[t * 2 + h, r] for h in range(2)]
                west = from_west(*[coefs[h, 0, cr] * center[h] for h in range(2)])
                east = from_east(*[coefs[h, 1, cr] * center[h] for h in range(2)])
                for h in range(2):
                    g = t * 2 + h
                    target[g, r] = (
                        (coefs[h, 4, cr] * center[h] + west[h])
                        + (east[h] + coefs[h, 2, cr - 1] * source[g, r - 1])
                        + coefs[h, 3, cr + 1] * source[g, r + 1]
                    )
            return 0

        lax.fori_loop(low, high, row_step, 0, unroll=2)

    buffers = [field_a, field_b]
    for step in range(SUB):
        forward(buffers[step % 2], buffers[(step + 1) % 2], step + 1, tall - step - 1)
    forecast, spread = buffers[SUB % 2], buffers[(SUB + 1) % 2]

    def kinds(row, t):
        base = t * (2 + variables) * n_sens
        return [row[:, base + n * n_sens : base + (n + 1) * n_sens] for n in range(2 + variables)]

    def sensor_rows(h, band):
        if not paired:
            count = sens.shape[0] // 8
            first = (h * 4 + band) * count
            return [sens[...].astype(F32)[first + n : first + n + 1] for n in range(count)]
        if band in (1, 3):
            at = slice(own_bg + rows, own_bg + rows + 16)
            mine, other = p0[at, half:lon].astype(F32), r0[at, half:lon].astype(F32)
            n = 14 if band == 1 else 12
            return [jnp.where(me_t == h, mine[n : n + 1], other[n + 1 : n + 2])]
        from_far = parity == (0 if band == 0 else 1)
        found = []
        for x, y in ((near, far), (dnear, dfar)):
            last = x.shape[0]
            pair = [m[last - 16 : last, half:lon].astype(F32)[15:16] for m in (x, y)]
            found.append(jnp.where(from_far, pair[1], pair[0]))
        return [jnp.where(me_t == h, found[0], found[1])]

    row_bits = tile_cols.bit_length() - 1
    width_bits = width.bit_length() - 1

    def located(h, band, t):
        found = []
        for n, row in enumerate(sensor_rows(h, band)):
            high, low, *values = kinds(row, t)
            cell = (high * 256.0 + low).astype(jnp.int32)
            column = (cell & (tile_cols - 1)) + n * tile_cols
            found.append([cell >> row_bits, column >> width_bits, column & (width - 1)] + list(values))
        if band == 1:
            for n, row in enumerate(sensor_rows(h, 3)):
                for v in range(variables):
                    found[n][3 + v] = found[n][3 + v] + row[:, (t * variables + v) * n_sens : (t * variables + v + 1) * n_sens]
        return [jnp.concatenate([f[n] for f in found], axis=1) for n in range(3 + variables)]

    def assimilate(g, row_list, where_row, quarter, lane_of, values):
        total = where_row.shape[1]
        onehot = jnp.where(
            lax.broadcasted_iota(jnp.int32, (width, total), 0) == lane_of, 1.0, 0.0
        ).astype(BF)
        stack = jnp.concatenate([forecast[g, HALO + r] for r in row_list], axis=0)
        high, low = split2(stack)
        picked = dot(high, onehot) + dot(low, onehot)
        shape = (8, total)
        here_q = (lax.broadcasted_iota(jnp.int32, shape, 0) >> (variables.bit_length() - 1)) == quarter
        variable = lax.broadcasted_iota(jnp.int32, shape, 0) & (variables - 1)
        misfit = jnp.zeros(shape, F32)
        for n, r in enumerate(row_list):
            misfit = misfit + jnp.where(where_row == r, picked[n * 8 : (n + 1) * 8], 0.0)
        target = jnp.broadcast_to(values[0], shape)
        for v in range(1, variables):
            target = jnp.where(variable == v, values[v], target)
        misfit = jnp.where(here_q, misfit - target, 0.0)
        weighted = jnp.concatenate([jnp.where(where_row == r, misfit, 0.0) for r in row_list], axis=0)
        high, low = split2(weighted)
        return (dot_t(high, onehot) + dot_t(low, onehot)).reshape(len(row_list), 8, width)

    far_away = -(1 << 20)
    for t in range(frames):
        for h in range(2):
            g = t * 2 + h
            row, quarter, lane_of, *values = located(h, 1, t)
            spread[g, HALO : HALO + rows] = assimilate(g, list(range(rows)), row, quarter, lane_of, values)
            above, below = located(h, 0, t), located(h, 2, t)
            above[0] = jnp.where(top_ok, above[0] - rows, far_away)
            below[0] = jnp.where(bottom_ok, below[0] + rows, far_away)
            merged = [jnp.concatenate([x, y], axis=1) for x, y in zip(above, below)]
            rim_rows = list(range(-SUB, 0)) + list(range(rows, rows + SUB))
            rim = assimilate(g, rim_rows, merged[0], merged[1], merged[2], merged[3:])
            spread[g, HALO - SUB : HALO] = rim[0:SUB]
            spread[g, HALO + rows : HALO + rows + SUB] = rim[SUB:]

    buffers = [spread, forecast]
    for step in range(SUB):
        low = HALO - SUB + step + 1
        backward(buffers[step % 2], buffers[(step + 1) % 2], low, tall - low)
    result = buffers[SUB % 2]

    for t in range(frames):
        for h in range(2):
            high, low = split2(result[t * 2 + h, HALO : HALO + rows].reshape(rows * 8, width))
            back = dot(p_out[...], high) + dot(p_out[...], low)
            for q in range(quarters):
                cut = slice(h * half + q * width, h * half + (q + 1) * width)
                for v in range(variables):
                    base = (q * variables + v) * rows
                    out[t, v, :, cut] = back[base : base + rows]


def conv_kernel(
    p0, r0, near, far, dnear, dfar, adjoint, table, w1, w2, w3, b2, b3, out, window,
    *, rows, frames, variables, own_bg, oth_bg, group, chunk, parity_of,
):
    lon = p0.shape[1]
    me_l, count = lax.axis_index("lat"), lax.axis_size("lat")
    case = case_of(parity_of(), me_l, count)
    groups = rows // group
    tall = table.shape[1] // groups
    depth = window.shape[1]
    stack = jnp.concatenate(
        [p0[0:own_bg], r0[0:oth_bg], near[...], far[...], dnear[...], dfar[...]], axis=0
    )
    chosen = dot(table[case], stack)
    for g in range(groups):
        center = chosen[g * tall : (g + 1) * tall]
        window[g, 0:tall] = pltpu.roll(center, 1, 1).astype(BF)
        window[g, tall : 2 * tall] = center.astype(BF)
        window[g, 2 * tall : 3 * tall] = pltpu.roll(center, lon - 1, 1).astype(BF)
        left = depth - 3 * tall
        ones = lax.broadcasted_iota(jnp.int32, (left, lon), 0) < 3
        window[g, 3 * tall : depth] = jnp.where(ones, 1.0, 0.0).astype(BF)

    def gelu(y):
        inner = y * (GELU_1 + GELU_2 * (y * y))
        return (y + y * jnp.tanh(inner)).astype(BF)

    hidden = w2.shape[0]
    bias2 = jnp.concatenate([b2[...]] * (chunk // 128), axis=1)
    bias3 = jnp.concatenate([b3[...]] * (chunk // 128), axis=1)

    def columns(n, _):
        cut = pl.ds(pl.multiple_of(n * chunk, chunk), chunk)
        for g in range(groups):
            taps = window[g, :, cut]
            for t in range(frames):
                one = gelu(dot(w1[t * hidden : (t + 1) * hidden], taps))
                two = gelu(dot(w2[...], one) + bias2)
                score = dot(w3[...], two) + bias3
                for v in range(variables):
                    span = slice(g * group, (g + 1) * group)
                    out[t, v, span, cut] = score[v * group : (v + 1) * group] - adjoint[t, v, span, cut]
        return 0

    lax.fori_loop(0, lon // chunk, columns, 0)


def call(body, out_shape, scratch, *args):
    whole = pl.BlockSpec(memory_space=pltpu.VMEM)
    several = isinstance(out_shape, (list, tuple))
    return pl.pallas_call(
        body,
        out_shape=out_shape,
        in_specs=[whole] * len(args),
        out_specs=[whole] * len(out_shape) if several else whole,
        scratch_shapes=scratch,
        compiler_params=pltpu.CompilerParams(vmem_limit_bytes=VMEM_BYTES),
    )(*args)


def struct(shape, dtype):
    return jax.ShapeDtypeStruct(shape, dtype)


def swap_pairs(tiles, bands):
    def at(t, j):
        return t * bands + j

    def far(j):
        return j + 1 if j % 2 else j - 1

    cells = [(t, j) for t in range(tiles) for j in range(bands)]
    inner = lambda j: 0 <= far(j) < bands
    return (
        [(at(t, j), at(1 - t, j)) for t, j in cells],
        [(at(t, j), at(t, j ^ 1)) for t, j in cells],
        [(at(t, j), at(t, far(j)) if inner(j) else at(1 - t, j)) for t, j in cells],
        [(at(t, j), at(1 - t, j ^ 1)) for t, j in cells],
        [(at(t, j), at(1 - t, far(j)) if inner(j) else at(1 - t, j)) for t, j in cells],
    )


def exchange_pairs(background, east, north, diff, sensors, observations):
    frames, variables, rows, lon = background.shape
    fields = frames * variables
    bands = lax.axis_size("lat")
    table = jnp.asarray(pack_table(rows, fields), BF)
    big = struct((fields * rows + 2 * rows, lon), BF)
    lat_message, diagonal = struct((32, lon), BF), struct((16, lon), BF)
    with jax.named_scope("pack"):
        p0, near, far, dnear, dfar = call(
            functools.partial(pack_kernel, frames=frames),
            [big, lat_message, lat_message, diagonal, diagonal],
            [],
            background, east, north, diff, sensors, observations, table,
        )
    axes = ("tm", "lat")
    across, on_chip, next_chip, diag_near, diag_far = swap_pairs(lax.axis_size("tm"), bands)
    r0 = lax.ppermute(p0, axes, across)
    r_dfar = lax.ppermute(dfar, axes, diag_far)
    r_far = lax.ppermute(far, axes, next_chip)
    r_dnear = lax.ppermute(dnear, axes, diag_near)
    r_near = lax.ppermute(near, axes, on_chip)
    return p0, r0, r_near, r_far, r_dnear, r_dfar


def exchange_gathered(background, east, north, diff, sensors, observations):
    frames, variables, rows, lon = background.shape
    fields = frames * variables
    half = lon // 2
    tiles, bands = lax.axis_size("tm"), lax.axis_size("lat")
    down = [(j, j + 1) for j in range(bands - 1)]
    up = [(j + 1, j) for j in range(bands - 1)]
    later = [(t, t + 1) for t in range(tiles - 1)]
    earlier = [(t + 1, t) for t in range(tiles - 1)]
    coefs = jnp.stack([east, north, diff - K_MID]).astype(BF)
    coefs = lax.all_gather(coefs, "tm", axis=2, tiled=True)
    around = jnp.concatenate(
        [lax.ppermute(background, "tm", later), lax.ppermute(background, "tm", earlier)], axis=0
    )
    cells = lax.all_to_all(sensors, "tm", split_axis=0, concat_axis=2, tiled=True)[:, 0]
    obs = lax.all_to_all(observations, "tm", split_axis=0, concat_axis=2, tiled=True)[:, 0]
    cells = jnp.moveaxis(cells, 1, 0)
    obs = jnp.transpose(obs, (1, 0, 2, 3))
    obs_high = obs.astype(BF).astype(F32)
    digits = jnp.stack([(cells >> 8).astype(F32), (cells & 255).astype(F32)], axis=2)
    described = jnp.concatenate([digits, obs_high], axis=2).reshape(tiles, -1).astype(BF)
    low = (obs - obs_high).astype(BF).reshape(tiles, -1)
    low = jnp.pad(low, ((0, 0), (0, described.shape[1] - low.shape[1])))
    bands_of = [
        lax.ppermute(described, "lat", down), described, lax.ppermute(described, "lat", up), low
    ]
    sens = jnp.stack([x.reshape(2, tiles // 2, -1) for x in bands_of], axis=1)
    sens = sens.reshape(-1, described.shape[1])

    def block(fields_3d, h):
        part = coefs[:, :, h * half : (h + 1) * half]
        blank = jnp.zeros_like(part[0])
        return jnp.concatenate(
            [
                fields_3d.reshape(-1, lon),
                jnp.concatenate([part[0], part[2]], axis=1),
                jnp.concatenate([part[1], blank], axis=1),
            ],
            axis=0,
        )

    def message(fields_4d, depth, h, bottom, height):
        height_rows = fields_4d.shape[2]
        edge = fields_4d[:, :, height_rows - depth :] if bottom else fields_4d[:, :, :depth]
        edge = edge.reshape(-1, lon)
        part = coefs[:, :, h * half : (h + 1) * half]
        part = part[:, rows - CROWS :] if bottom else part[:, :CROWS]
        part = jnp.pad(part.reshape(3 * CROWS, half), ((0, 16 - 3 * CROWS), (0, 0)))
        part = jnp.concatenate([part[:8], part[8:]], axis=1)
        blank = jnp.zeros((height - 8 - edge.shape[0], lon), BF)
        return jnp.concatenate([edge, blank, part], axis=0)

    p0, r0 = block(background, 0), block(around, 1)
    near = lax.ppermute(message(background, HALO, 0, False, 32), "lat", up)
    far = lax.ppermute(message(background, HALO, 0, True, 32), "lat", down)
    dnear = lax.ppermute(message(around, 1, 1, False, 16), "lat", up)
    dfar = lax.ppermute(message(around, 1, 1, True, 16), "lat", down)
    return p0, r0, near, far, dnear, dfar, sens


def shards(
    background, conv_weight, conv_bias, mix_weight, mix_bias, out_weight, out_bias,
    drift_east, drift_north, diffusivity, sensors, observations,
):
    frames, variables, rows, lon = background.shape
    tiles, bands = lax.axis_size("tm"), lax.axis_size("lat")
    paired = tiles == 2 and bands % 2 == 0
    group = 8
    hid = mix_weight.shape[0]
    fields = frames * variables
    arrays = (background, drift_east, drift_north, diffusivity, sensors, observations)
    if paired:
        received, sens = exchange_pairs(*arrays), ()
        offsets = [[*range(2 * frames)], [*range(frames), *range(-frames, 0)]]
        i_of = lambda: lax.axis_index("tm")
        parity_of = lambda: lax.axis_index("lat") % 2
    else:
        *received, sens = exchange_gathered(*arrays)
        sens = (sens,)
        offsets = [[*range(frames), *range(-frames, 0), *range(frames, 2 * frames)]]
        i_of = lambda: 0
        parity_of = lambda: 0
    others = len(offsets[0]) - frames
    own_bg, oth_bg = fields * rows, others * variables * rows

    need = 3 * (group + 2) * (frames + others) * variables + 3
    depth = -(-need // 128) * 128
    taps = jnp.asarray(np.stack([tap_table(o, frames, variables, group, depth) for o in offsets]))
    with jax.named_scope("weights"):
        weights = call(
            functools.partial(prep_kernel, group=group, i_of=i_of),
            [
                struct((frames * group * hid, depth), BF),
                struct((group * hid, group * hid), BF),
                struct((variables * group, group * hid), BF),
                struct((group * hid, 128), F32),
                struct((variables * group, 128), F32),
            ],
            [],
            conv_weight, conv_bias.reshape(1, -1), mix_weight, mix_bias.reshape(1, -1),
            out_weight, out_bias.reshape(1, -1), taps,
        )
    quarters = 8 // variables
    width = lon // 8
    tables = [jnp.asarray(x, BF) for x in model_tables(rows, frames, variables, quarters)]
    tall, ctall = rows + 2 * HALO, rows + 2 * CROWS
    with jax.named_scope("model"):
        adjoint = call(
            functools.partial(
                model_kernel, rows=rows, frames=frames, variables=variables, own_bg=own_bg,
                oth_bg=oth_bg, tile_cols=drift_east.shape[1], n_sens=sensors.shape[3],
                paired=paired, i_of=i_of, parity_of=parity_of,
            ),
            struct(background.shape, F32),
            [
                pltpu.VMEM((2 * frames, tall, 8, width), F32),
                pltpu.VMEM((2 * frames, tall, 8, width), F32),
                pltpu.VMEM((2, 5, ctall, 8, width), F32),
            ],
            *received, *sens, *tables,
        )
    table = jnp.asarray(conv_table(rows, frames, others, variables, group), BF)
    with jax.named_scope("prior"):
        return call(
            functools.partial(
                conv_kernel, rows=rows, frames=frames, variables=variables, own_bg=own_bg,
                oth_bg=oth_bg, group=group, chunk=256, parity_of=parity_of,
            ),
            struct(background.shape, F32),
            [pltpu.VMEM((rows // group, depth, lon), BF)],
            *received, adjoint, table, *weights,
        )


def solution(mesh):
    placed = (
        P("tm", None, "lat", None),
        P(),
        P(),
        P(),
        P(),
        P(),
        P(),
        P("lat", "tm"),
        P("lat", "tm"),
        P("lat", "tm"),
        P(None, "lat", "tm", None),
        P(None, "lat", "tm", None, None),
    )
    return jax.shard_map(
        shards, mesh=mesh, in_specs=placed, out_specs=P("tm", None, "lat", None), check_vma=False
    )
```

```python
import functools

import jax
import jax.numpy as jnp
import numpy as np
from jax import lax
from jax.experimental import pallas as pl
from jax.experimental.pallas import tpu as pltpu
from jax.sharding import PartitionSpec as P

KT = 5
SUB = 3
K_MID = 0.17
HALO = 2 * SUB
CROWS = 2 * SUB - 1
BF = jnp.bfloat16
F32 = jnp.float32
VMEM_BYTES = 48 * 1024 * 1024
COST = 60 * 10**6
PACK_BYTES = 64 * 1024 * 1024 - 1024 * 1024
GELU_1 = 2.0 * float(np.sqrt(2.0 / np.pi))
GELU_2 = 8.0 * 0.044715 * float(np.sqrt(2.0 / np.pi))


def dot(a, b):
    return jnp.dot(a, b, preferred_element_type=F32)


def dot_t(a, b):
    return lax.dot_general(a, b, (((1,), (1,)), ((), ())), preferred_element_type=F32)


def split2(x):
    high = x.astype(BF)
    return high, (x - high.astype(F32)).astype(BF)


def fetch(pairs, sems):
    copies = [pltpu.make_async_copy(source, target, sems.at[n]) for n, (source, target) in enumerate(pairs)]
    for copy in copies:
        copy.start()
    for copy in copies:
        copy.wait()


def pack_table(rows, fields):
    table = np.zeros((2, 2, 80, 128), np.float32)
    coef_row = fields * rows
    for parity in range(2):
        for side in range(2):
            for message in range(4):
                far, diagonal = message % 2, message // 2
                bottom = (far == 0) == (parity == 0)
                out = table[parity, side]
                if diagonal:
                    base = 64 + 8 * far
                    for field in range(fields):
                        out[base + field, field * rows + (rows - 1 if bottom else 0)] = 1
                    if side == 0:
                        out[base + fields, coef_row + 3 * rows + 15] = 1
                    continue
                base = 32 * far
                for field in range(fields):
                    for e in range(HALO):
                        row = rows - HALO + e if bottom else e
                        out[base + field * HALO + e, field * rows + row] = 1
                for slot in range(8):
                    j = side * 8 + slot
                    target = base + 24 + slot
                    if j < 3 * CROWS:
                        c, e = divmod(j, CROWS)
                        row = rows - CROWS + e if bottom else e
                        out[target, coef_row + c * rows + row] = 1
                    else:
                        out[target, coef_row + 3 * rows + 14] = 1
    return table


def near_far(case):
    parity = case in (1, 3)
    top_ok = case != 2
    bottom_ok = case not in (3, 4)
    top_slot = 0 if parity else 1
    return top_slot, 1 - top_slot, top_ok, bottom_ok


def model_tables(rows, frames, variables, quarters):
    lanes = quarters * variables
    own = np.zeros((rows * lanes, quarters * variables * rows), np.float32)
    coef = np.zeros((rows * lanes, quarters * rows), np.float32)
    out = np.zeros((lanes * rows, rows * lanes), np.float32)
    for r in range(rows):
        for q in range(quarters):
            for v in range(variables):
                own[r * lanes + q * variables + v, (q * variables + v) * rows + r] = 1
                coef[r * lanes + q * variables + v, q * rows + r] = 1
                out[(q * variables + v) * rows + r, r * lanes + q * variables + v] = 1
    halo = np.zeros((5, frames, 2 * HALO * lanes, quarters * 64), np.float32)
    chalo = np.zeros((5, 3 * 2 * CROWS * lanes, quarters * 64), np.float32)
    ohalo = np.zeros((5, 3 * 2 * CROWS * lanes, quarters * 32), np.float32)
    for case in range(5):
        top_slot, bottom_slot, top_ok, bottom_ok = near_far(case)
        for q in range(quarters):
            for v in range(variables):
                lane = q * variables + v
                for half, slot, ok in ((0, top_slot, top_ok), (1, bottom_slot, bottom_ok)):
                    if not ok:
                        continue
                    for t in range(frames):
                        for e in range(HALO):
                            local = (t * variables + v) * HALO + e
                            halo[case, t, (half * HALO + e) * lanes + lane, q * 64 + slot * 32 + local] = 1
                    for c in range(3):
                        for e in range(CROWS):
                            j = c * CROWS + e
                            column = q * 64 + slot * 32 + (j // 8) * 16 + 8 + j % 8
                            row = ((c * 2 + half) * CROWS + e) * lanes + lane
                            chalo[case, row, column] = 1
                            column = q * 32 + (j // 8) * 16 + slot * 8 + j % 8
                            ohalo[case, row, column] = 1
    return own, coef, out, halo, chalo, ohalo


def round16(n):
    return -(-n // 16) * 16


def conv_table(rows, frames, others, variables, group):
    channels = (frames + others) * variables
    tall = round16((group + 2) * channels)
    own_rows = frames * variables * rows
    oth_rows = others * variables * rows
    table = np.zeros((5, rows // group * tall, own_rows + oth_rows + 80), np.float32)
    for case in range(5):
        top_slot, bottom_slot, top_ok, bottom_ok = near_far(case)
        for g in range(rows // group):
            for yy in range(group + 2):
                y = g * group + yy - 1
                for f in range(frames + others):
                    for v in range(variables):
                        target = g * tall + yy * channels + f * variables + v
                        own = f < frames
                        field = (f if own else f - frames) * variables + v
                        if 0 <= y < rows:
                            table[case, target, (0 if own else own_rows) + field * rows + y] = 1
                            continue
                        slot, ok = (top_slot, top_ok) if y < 0 else (bottom_slot, bottom_ok)
                        if not ok:
                            continue
                        column = own_rows + oth_rows
                        if own:
                            column += slot * 32 + field * HALO + (HALO - 1 if y < 0 else 0)
                        else:
                            column += 64 + slot * 8 + field
                        table[case, target, column] = 1
    return table


def tap_table(offsets, frames, variables, group, depth):
    channels = len(offsets) * variables
    tall = round16((group + 2) * channels)
    table = np.full((8, depth), -1, np.int32)
    for t in range(frames):
        for s in range(3):
            for i in range(3):
                for f, offset in enumerate(offsets):
                    lag = offset - t + KT // 2
                    for v in range(variables):
                        if 0 <= lag < KT:
                            k = s * tall + i * channels + f * variables + v
                            table[t, k] = ((v * KT + lag) * 3 + i) * 3 + s
    table[frames, 3 * tall : 3 * tall + 3] = 3 * 3 * KT * variables + np.arange(3)
    return table


def index_rows(tables, lanes):
    out = np.full((8, lanes), -1, np.int32)
    for n, table in enumerate(tables):
        out[n, : table.shape[0]] = np.where(table.any(1), table.argmax(1), -1)
    return out


def case_of(parity, index, count):
    return jnp.where(index == 0, 2, jnp.where(index == count - 1, jnp.where(parity == 1, 3, 4), parity))


def pack_kernel(
    bg_in, east_in, north_in, diff_in, sensors_in, obs_in, table_in, p_c, near, far, dnear, dfar,
    bg, east, north, diff, sensors, obs, table, sems, *, frames,
):
    me_t = lax.axis_index("tm")
    parity = lax.axis_index("lat") % 2
    fetch(
        [
            (bg_in, bg), (east_in, east), (north_in, north), (diff_in, diff),
            (sensors_in, sensors), (obs_in, obs), (table_in.at[parity], table),
        ],
        sems,
    )
    fields = bg.shape[0] * bg.shape[1]
    rows, lon = bg.shape[2], bg.shape[3]
    half = lon // 2
    fields_2d = bg[...].reshape(fields * rows, lon)
    a, b = east[...].astype(BF), north[...].astype(BF)
    k = (diff[...] - K_MID).astype(BF)

    def described(first, low):
        pieces = []
        for t in range(frames):
            cells = sensors[first + t, 0]
            if not low:
                pieces += [(cells >> 8).astype(F32), (cells & 255).astype(F32)]
            for v in range(obs.shape[3]):
                value = obs[first + t, 0, 0, v : v + 1]
                high = value.astype(BF).astype(F32)
                pieces.append(value - high if low else high)
        row = jnp.concatenate(pieces, axis=1)
        if row.shape[1] < half:
            row = jnp.concatenate([row, jnp.zeros((1, half - row.shape[1]), F32)], axis=1)
        return row

    mine, theirs = me_t * frames, (1 - me_t) * frames
    extra = jnp.concatenate(
        [
            jnp.zeros((12, half), F32),
            described(mine, True),
            described(theirs, True),
            described(mine, False),
            described(theirs, False),
        ],
        axis=0,
    ).astype(BF)
    p_c[0:rows, 0:half] = a
    p_c[rows : 2 * rows, 0:half] = b
    p_c[0:rows, half:lon] = k
    p_c[rows : 2 * rows, half:lon] = extra
    for side in range(2):
        cut = slice(side * half, (side + 1) * half)
        source = jnp.concatenate([fields_2d[:, cut], a, b, k, extra], axis=0)
        message = dot(table[side], source).astype(BF)
        near[:, cut] = message[0:32]
        far[:, cut] = message[32:64]
        dnear[:, cut] = message[64:72]
        dfar[:, cut] = message[72:80]


def prep_kernel(*refs, group, channels, relay, i_of, parity_of):
    sources, rest = refs[:8], refs[8:]
    if relay:
        p_c, near, far, q_c, *rest = rest
    w1, w2, w3, b2, b3, p_conv, p_own, p_coef, p_out, p_halo, p_chalo, p_ohalo = rest[:12]
    conv_w, conv_b, mix_w, mix_b, out_w, out_b, taps, index, sems = rest[12:]
    hid = mix_w.shape[0]
    case = case_of(parity_of(), lax.axis_index("lat"), lax.axis_size("lat"))
    moves = [*zip(sources[:6], (conv_w, conv_b, mix_w, mix_b, out_w, out_b))]
    moves += [(sources[6].at[i_of()], taps), (sources[7].at[case], index)]
    if relay:
        moves.append((p_c, q_c.at[0:32]))
        q_c[32:40, :] = near[24:32, :]
        q_c[40:48, :] = far[24:32, :]
    fetch(moves, sems)
    columns = index[...].astype(F32).T

    def select(n, shape):
        lanes = lax.broadcasted_iota(jnp.int32, shape, 1).astype(F32)
        return jnp.where(lanes == columns[0 : shape[0], n : n + 1], 1.0, 0.0)

    frames = p_halo.shape[0]
    p_conv[...] = select(0, p_conv.shape).astype(BF)
    for t in range(frames):
        p_halo[t] = select(1 + t, p_halo.shape[1:]).astype(BF)
    for n, target in ((1 + frames, p_chalo), (5 + frames, p_ohalo)):
        halved = lax.broadcasted_iota(jnp.int32, target.shape, 0) < target.shape[0] // 3 * 2
        target[...] = (select(n, target.shape) * jnp.where(halved, 0.5, 1.0)).astype(BF)
    p_own[...] = select(2 + frames, p_own.shape).astype(BF)
    p_coef[...] = select(3 + frames, p_coef.shape).astype(BF)
    p_out[...] = select(4 + frames, p_out.shape).astype(BF)
    table = taps[...]

    def column(row):
        n = row.shape[1]
        here = lax.broadcasted_iota(jnp.int32, (n, n), 0) == lax.broadcasted_iota(jnp.int32, (n, n), 1)
        return jnp.sum(jnp.where(here, jnp.broadcast_to(row, (n, n)), 0.0), axis=1, keepdims=True)

    bias = 0.5 * column(conv_b[...])
    pieces = []
    for _ in range(3):
        piece = bias.astype(BF)
        bias = bias - piece.astype(F32)
        pieces.append(piece.astype(F32))
    ntap = conv_w.shape[1]
    padded = 128
    weights = jnp.concatenate(
        [0.5 * conv_w[...].astype(F32)] + pieces + [jnp.zeros((hid, padded - ntap - 3), F32)], axis=1
    ).astype(BF)
    tap_id = lax.broadcasted_iota(jnp.int32, (padded, table.shape[1]), 0)

    def chosen(n):
        return dot(weights, jnp.where(tap_id == table[n : n + 1, :], 1.0, 0.0).astype(BF))

    biased = chosen(frames)
    for t in range(frames):
        first = chosen(t)
        for y in range(group):
            start = (t * group + y) * hid
            moved = pltpu.roll(first, y * channels, 1) if y else first
            w1[start : start + hid, :] = (moved + biased).astype(BF)
    tall = group * hid
    row = lax.broadcasted_iota(jnp.int32, (tall, hid), 0) & (hid - 1)
    up = jnp.where(row == lax.broadcasted_iota(jnp.int32, (tall, hid), 1), 1.0, 0.0).astype(BF)
    mixed = dot_t(dot(up, (0.5 * mix_w[...].astype(F32)).astype(BF)).astype(BF), up)
    shift = hid.bit_length() - 1
    rows2 = lax.broadcasted_iota(jnp.int32, (tall, tall), 0) >> shift
    cols2 = lax.broadcasted_iota(jnp.int32, (tall, tall), 1) >> shift
    w2[...] = jnp.where(rows2 == cols2, mixed, 0.0).astype(BF)
    variables = out_w.shape[0]
    wide = dot_t(out_w[...], up)
    y = lax.broadcasted_iota(jnp.int32, (group, tall), 0)
    here = y == lax.broadcasted_iota(jnp.int32, (group, tall), 1) >> shift
    w3[...] = jnp.concatenate(
        [jnp.where(here, jnp.broadcast_to(wide[v : v + 1], (group, tall)), 0.0) for v in range(variables)],
        axis=0,
    ).astype(BF)
    b3[...] = jnp.concatenate(
        [jnp.broadcast_to(out_b[:, v : v + 1], (group, 128)) for v in range(variables)], axis=0
    )
    mixed_bias = jnp.broadcast_to(0.5 * column(mix_b[...]), (hid, 128))
    b2[...] = jnp.concatenate([mixed_bias] * group, axis=0)


def model_kernel(
    p_bg, q_c, r_c, near, far, dnear, dfar, *rest,
    rows, frames, variables, tile_cols, n_sens, paired, i_of, parity_of,
):
    sens = None if paired else rest[0]
    first = 0 if paired else 1
    prior, p_own, p_coef, p_out, p_halo, p_chalo, p_ohalo = rest[first : first + 7]
    out, field_a, field_b, coefs = rest[first + 7 :]
    lon = p_bg.shape[1]
    half = lon // 2
    quarters = 8 // variables
    width = half // quarters
    me_l, count = lax.axis_index("lat"), lax.axis_size("lat")
    parity = parity_of()
    me_t = i_of()
    top_ok, bottom_ok = me_l > 0, me_l < count - 1
    tall = rows + 2 * HALO

    for t in range(frames):
        for h in range(2):
            g = t * 2 + h
            body, rim = [], []
            for q in range(quarters):
                cut = slice(h * half + q * width, h * half + (q + 1) * width)
                body.append(p_bg[t * variables * rows : (t + 1) * variables * rows, cut])
                rim += [near[:, cut], far[:, cut]]
            field_a[g, HALO : HALO + rows] = dot(p_own[...], jnp.concatenate(body, axis=0)).reshape(rows, 8, width)
            edges = dot(p_halo[t], jnp.concatenate(rim, axis=0)).reshape(2 * HALO, 8, width)
            field_a[g, 0:HALO] = edges[0:HALO]
            field_a[g, HALO + rows : tall] = edges[HALO:]

    ctall = rows + 2 * CROWS
    for source in range(2):
        big = q_c if source == 0 else r_c
        spot = me_t if source == 0 else 1 - me_t
        pieces = []
        for side in range(2):
            for c_row in range(2):
                stack = []
                for q in range(quarters):
                    cut = slice(side * half + q * width, side * half + (q + 1) * width)
                    stack.append(big[c_row * rows : (c_row + 1) * rows, cut])
                pieces.append(jnp.concatenate(stack, axis=0))
        scaled = p_coef[...]
        ha = (0.5 * dot(scaled, pieces[0])).reshape(rows, 8, width)
        hb = (0.5 * dot(scaled, pieces[1])).reshape(rows, 8, width)
        kk = dot(scaled, pieces[2]).reshape(rows, 8, width) + K_MID
        rim = []
        for q in range(quarters):
            for message in (near[16:32], far[16:32]) if source == 0 else (r_c[32:48],):
                for side in range(2):
                    cut = slice(side * half + q * width, side * half + (q + 1) * width)
                    rim.append(message[:, cut])
        edges = dot((p_ohalo if source else p_chalo)[...], jnp.concatenate(rim, axis=0))
        edges = edges.reshape(3, 2, CROWS, 8, width)
        k_top = edges[2, 0] + jnp.where(top_ok, K_MID, 0.0)
        k_bottom = edges[2, 1] + jnp.where(bottom_ok, K_MID, 0.0)
        for start, size, xa, xb, xk in (
            (0, CROWS, edges[0, 0], edges[1, 0], k_top),
            (CROWS, rows, ha, hb, kk),
            (CROWS + rows, CROWS, edges[0, 1], edges[1, 1], k_bottom),
        ):
            span = slice(start, start + size)
            coefs[spot, 0, span] = xk - xa
            coefs[spot, 1, span] = xk + xa
            coefs[spot, 2, span] = xk - xb
            coefs[spot, 3, span] = xk + xb
            coefs[spot, 4, span] = 1.0 - 4.0 * xk

    lane = lax.broadcasted_iota(jnp.int32, (8, 128), 1)
    sub_q = lax.broadcasted_iota(jnp.int32, (8, 128), 0) >> (variables.bit_length() - 1)
    first_lane, last_lane = lane == 0, lane == 127
    first_q, last_q = sub_q == 0, sub_q == quarters - 1
    tiles = width // 128

    def cut_tiles(x):
        return [x[:, n * 128 : (n + 1) * 128] for n in range(tiles)]

    def from_west(x0, x1):
        both = [[pltpu.roll(part, 1, 1) for part in cut_tiles(x)] for x in (x0, x1)]
        result = []
        for h in range(2):
            wrapped = jnp.where(last_q, both[1 - h][-1], both[h][-1])
            carry = pltpu.roll(wrapped, variables, 0)
            parts = []
            for n in range(tiles):
                parts.append(jnp.where(first_lane, carry if n == 0 else both[h][n - 1], both[h][n]))
            result.append(jnp.concatenate(parts, axis=1))
        return result

    def from_east(x0, x1):
        both = [[pltpu.roll(part, 127, 1) for part in cut_tiles(x)] for x in (x0, x1)]
        result = []
        for h in range(2):
            wrapped = jnp.where(first_q, both[1 - h][0], both[h][0])
            carry = pltpu.roll(wrapped, 8 - variables, 0)
            parts = []
            for n in range(tiles):
                parts.append(
                    jnp.where(last_lane, carry if n == tiles - 1 else both[h][n + 1], both[h][n])
                )
            result.append(jnp.concatenate(parts, axis=1))
        return result

    def forward(source, target, low, high):
        for r in range(low, high):
            cr = r - (HALO - CROWS)
            for t in range(frames):
                center = [source[t * 2 + h, r] for h in range(2)]
                west, east = from_west(*center), from_east(*center)
                for h in range(2):
                    g = t * 2 + h
                    target[g, r] = (
                        (coefs[h, 4, cr] * center[h] + coefs[h, 0, cr] * east[h])
                        + (coefs[h, 1, cr] * west[h] + coefs[h, 2, cr] * source[g, r + 1])
                        + coefs[h, 3, cr] * source[g, r - 1]
                    )

    def backward(source, target, low, high):
        for r in range(low, high):
            cr = r - (HALO - CROWS)
            for t in range(frames):
                center = [source[t * 2 + h, r] for h in range(2)]
                west = from_west(*[coefs[h, 0, cr] * center[h] for h in range(2)])
                east = from_east(*[coefs[h, 1, cr] * center[h] for h in range(2)])
                for h in range(2):
                    g = t * 2 + h
                    target[g, r] = (
                        (coefs[h, 4, cr] * center[h] + west[h])
                        + (east[h] + coefs[h, 2, cr - 1] * source[g, r - 1])
                        + coefs[h, 3, cr + 1] * source[g, r + 1]
                    )

    buffers = [field_a, field_b]
    for step in range(SUB):
        forward(buffers[step % 2], buffers[(step + 1) % 2], step + 1, tall - step - 1)
    forecast, spread = buffers[SUB % 2], buffers[(SUB + 1) % 2]

    def kinds(row, t):
        base = t * (2 + variables) * n_sens
        return [row[:, base + n * n_sens : base + (n + 1) * n_sens] for n in range(2 + variables)]

    def sensor_rows(h, band):
        if not paired:
            count = sens.shape[0] // 8
            first = (h * 4 + band) * count
            return [sens[...].astype(F32)[first + n : first + n + 1] for n in range(count)]
        if band in (1, 3):
            at = slice(rows, rows + 16)
            mine, other = q_c[at, half:lon].astype(F32), r_c[at, half:lon].astype(F32)
            n = 14 if band == 1 else 12
            return [jnp.where(me_t == h, mine[n : n + 1], other[n + 1 : n + 2])]
        from_far = parity == (0 if band == 0 else 1)
        pair = [m[16:32, half:lon].astype(F32)[15:16] for m in (near, far)]
        row = frames * variables
        pair += [m[:, 0:half].astype(F32)[row : row + 1] for m in (dnear, dfar)]
        found = [jnp.where(from_far, pair[n + 1], pair[n]) for n in (0, 2)]
        return [jnp.where(me_t == h, found[0], found[1])]

    row_bits = tile_cols.bit_length() - 1
    width_bits = width.bit_length() - 1

    def located(h, band, t):
        found = []
        for n, row in enumerate(sensor_rows(h, band)):
            high, low, *values = kinds(row, t)
            cell = (high * 256.0 + low).astype(jnp.int32)
            column = (cell & (tile_cols - 1)) + n * tile_cols
            found.append([cell >> row_bits, column >> width_bits, column & (width - 1)] + list(values))
        if band == 1:
            for n, row in enumerate(sensor_rows(h, 3)):
                for v in range(variables):
                    found[n][3 + v] = found[n][3 + v] + row[:, (t * variables + v) * n_sens : (t * variables + v + 1) * n_sens]
        return [jnp.concatenate([f[n] for f in found], axis=1) for n in range(3 + variables)]

    def assimilate(g, row_list, where_row, quarter, lane_of, values):
        total = where_row.shape[1]
        lanes_bf = lax.broadcasted_iota(jnp.int32, (width, total), 0).astype(F32).astype(BF)
        onehot = jnp.where(lanes_bf == lane_of.astype(F32).astype(BF), BF(1), BF(0))
        stack = jnp.concatenate([forecast[g, HALO + r] for r in row_list], axis=0)
        high, low = split2(stack)
        picked = dot(high, onehot) + dot(low, onehot)
        shape = (8, total)
        here_q = (lax.broadcasted_iota(jnp.int32, shape, 0) >> (variables.bit_length() - 1)) == quarter
        variable = lax.broadcasted_iota(jnp.int32, shape, 0) & (variables - 1)
        misfit = jnp.zeros(shape, F32)
        for n, r in enumerate(row_list):
            misfit = misfit + jnp.where(where_row == r, picked[n * 8 : (n + 1) * 8], 0.0)
        target = jnp.broadcast_to(values[0], shape)
        for v in range(1, variables):
            target = jnp.where(variable == v, values[v], target)
        misfit = jnp.where(here_q, misfit - target, 0.0)
        row_f = where_row.astype(F32)
        weighted = jnp.concatenate([jnp.where(row_f == float(r), misfit, 0.0) for r in row_list], axis=0)
        high, low = split2(weighted)
        return (dot_t(high, onehot) + dot_t(low, onehot)).reshape(len(row_list), 8, width)

    far_away = -(1 << 20)
    for t in range(frames):
        for h in range(2):
            g = t * 2 + h
            row, quarter, lane_of, *values = located(h, 1, t)
            spread[g, HALO : HALO + rows] = assimilate(g, list(range(rows)), row, quarter, lane_of, values)
            above, below = located(h, 0, t), located(h, 2, t)
            above[0] = jnp.where(top_ok, above[0] - rows, far_away)
            below[0] = jnp.where(bottom_ok, below[0] + rows, far_away)
            merged = [jnp.concatenate([x, y], axis=1) for x, y in zip(above, below)]
            rim_rows = list(range(-SUB, 0)) + list(range(rows, rows + SUB))
            rim = assimilate(g, rim_rows, merged[0], merged[1], merged[2], merged[3:])
            spread[g, HALO - SUB : HALO] = rim[0:SUB]
            spread[g, HALO + rows : HALO + rows + SUB] = rim[SUB:]

    buffers = [spread, forecast]
    for step in range(SUB):
        low = HALO - SUB + step + 1
        backward(buffers[step % 2], buffers[(step + 1) % 2], low, tall - low)
    result = buffers[SUB % 2]

    for t in range(frames):
        for h in range(2):
            high, low = split2(result[t * 2 + h, HALO : HALO + rows].reshape(rows * 8, width))
            back = dot(p_out[...], high) + dot(p_out[...], low)
            for q in range(quarters):
                cut = slice(h * half + q * width, h * half + (q + 1) * width)
                for v in range(variables):
                    base = (q * variables + v) * rows
                    out[t, v, :, cut] = prior[t, v, :, cut] - back[base : base + rows]


def gelu(y):
    inner = y * (GELU_1 + GELU_2 * (y * y))
    return (y + y * jnp.tanh(inner)).astype(BF)


def shifted(chosen, window, depth):
    tall, lon = chosen.shape
    window[0:tall] = pltpu.roll(chosen, 1, 1).astype(BF)
    window[tall : 2 * tall] = chosen.astype(BF)
    window[2 * tall : 3 * tall] = pltpu.roll(chosen, lon - 1, 1).astype(BF)
    ones = lax.broadcasted_iota(jnp.int32, (depth - 3 * tall, lon), 0) < 3
    window[3 * tall : depth] = jnp.where(ones, 1.0, 0.0).astype(BF)


def widen(column, chunk):
    return jnp.concatenate([column] * (chunk // 128), axis=1)


def conv_kernel(
    p_bg, r_bg, near, far, dnear, dfar, w1, w2, w3, b2, b3, select, out, window,
    *, frames, variables, group, chunk,
):
    groups, depth, lon = window.shape
    fields = jnp.concatenate([x[...] for x in (p_bg, r_bg, near, far, dnear, dfar)], axis=0)
    chosen = dot(select[...], fields)
    tall = chosen.shape[0] // groups
    for g in range(groups):
        shifted(chosen[g * tall : (g + 1) * tall], window.at[g], depth)
    hidden = w2.shape[0]
    bias2, bias3 = widen(b2[...], chunk), widen(b3[...], chunk)
    pending = []
    for n in range(lon // chunk):
        cut = slice(n * chunk, (n + 1) * chunk)
        for g in range(groups):
            first = dot(w1[...], window[g, :, cut])
            for t in range(frames):
                one = gelu(first[t * hidden : (t + 1) * hidden])
                pending.append((t, g, cut, gelu(dot(w2[...], one) + bias2)))
    for t, g, cut, two in pending:
        score = dot(w3[...], two) + bias3
        for v in range(variables):
            out[t, v, g * group : (g + 1) * group, cut] = score[v * group : (v + 1) * group]


def call(body, out_shape, scratch, *args, fetched=(), limit=VMEM_BYTES, cost=None):
    whole = pl.BlockSpec(memory_space=pltpu.VMEM)
    given = pl.BlockSpec(memory_space=pltpu.HBM)
    several = isinstance(out_shape, (list, tuple))
    if cost is not None:
        cost = pl.CostEstimate(flops=10**8, bytes_accessed=cost, transcendentals=0)
    return pl.pallas_call(
        body,
        out_shape=out_shape,
        in_specs=[given if n in fetched else whole for n in range(len(args))],
        out_specs=[whole] * len(out_shape) if several else whole,
        scratch_shapes=scratch,
        compiler_params=pltpu.CompilerParams(vmem_limit_bytes=limit),
        cost_estimate=cost,
    )(*args)


def struct(shape, dtype):
    return jax.ShapeDtypeStruct(shape, dtype)


def swap_pairs(tiles, bands):
    def at(t, j):
        return t * bands + j

    def far(j):
        return j + 1 if j % 2 else j - 1

    cells = [(t, j) for t in range(tiles) for j in range(bands)]
    inner = lambda j: 0 <= far(j) < bands
    return (
        [(at(t, j), at(1 - t, j)) for t, j in cells],
        [(at(t, j), at(t, j ^ 1)) for t, j in cells],
        [(at(t, j), at(t, far(j)) if inner(j) else at(1 - t, j)) for t, j in cells],
        [(at(t, j), at(1 - t, j ^ 1)) for t, j in cells],
        [(at(t, j), at(1 - t, far(j)) if inner(j) else at(1 - t, j)) for t, j in cells],
    )


def exchange_pairs(background, east, north, diff, sensors, observations):
    frames, variables, rows, lon = background.shape
    fields = frames * variables
    bands = lax.axis_size("lat")
    table = jnp.asarray(pack_table(rows, fields), BF)
    arrays = (background, east, north, diff, sensors, observations)
    lat_message, diagonal = struct((32, lon), BF), struct((8, lon), BF)
    with jax.named_scope("pack"):
        p_c, near, far, dnear, dfar = call(
            functools.partial(pack_kernel, frames=frames),
            [struct((2 * rows, lon), BF), lat_message, lat_message, diagonal, diagonal],
            [pltpu.VMEM(x.shape, x.dtype) for x in arrays]
            + [pltpu.VMEM(table.shape[1:], BF), pltpu.SemaphoreType.DMA((7,))],
            *arrays, table, fetched=range(7), limit=PACK_BYTES,
        )
    axes = ("tm", "lat")
    across, on_chip, next_chip, diag_near, diag_far = swap_pairs(lax.axis_size("tm"), bands)
    p_bg = background.reshape(fields * rows, lon)
    r_bg = lax.ppermute(p_bg, axes, across)
    r_dfar = lax.ppermute(dfar, axes, diag_far)
    r_far = lax.ppermute(far, axes, next_chip)
    r_dnear = lax.ppermute(dnear, axes, diag_near)
    r_near = lax.ppermute(near, axes, on_chip)
    return p_bg, r_bg, p_c, r_near, r_far, r_dnear, r_dfar


def exchange_gathered(background, east, north, diff, sensors, observations):
    frames, variables, rows, lon = background.shape
    fields = frames * variables
    half = lon // 2
    tiles, bands = lax.axis_size("tm"), lax.axis_size("lat")
    down = [(j, j + 1) for j in range(bands - 1)]
    up = [(j + 1, j) for j in range(bands - 1)]
    later = [(t, t + 1) for t in range(tiles - 1)]
    earlier = [(t + 1, t) for t in range(tiles - 1)]
    coefs = jnp.stack([east, north, diff - K_MID]).astype(BF)
    coefs = lax.all_gather(coefs, "tm", axis=2, tiled=True)
    around = jnp.concatenate(
        [lax.ppermute(background, "tm", later), lax.ppermute(background, "tm", earlier)], axis=0
    )
    cells = lax.all_to_all(sensors, "tm", split_axis=0, concat_axis=2, tiled=True)[:, 0]
    obs = lax.all_to_all(observations, "tm", split_axis=0, concat_axis=2, tiled=True)[:, 0]
    cells = jnp.moveaxis(cells, 1, 0)
    obs = jnp.transpose(obs, (1, 0, 2, 3))
    obs_high = obs.astype(BF).astype(F32)
    digits = jnp.stack([(cells >> 8).astype(F32), (cells & 255).astype(F32)], axis=2)
    described = jnp.concatenate([digits, obs_high], axis=2).reshape(tiles, -1).astype(BF)
    low = (obs - obs_high).astype(BF).reshape(tiles, -1)
    low = jnp.pad(low, ((0, 0), (0, described.shape[1] - low.shape[1])))
    bands_of = [
        lax.ppermute(described, "lat", down), described, lax.ppermute(described, "lat", up), low
    ]
    sens = jnp.stack([x.reshape(2, tiles // 2, -1) for x in bands_of], axis=1)
    sens = sens.reshape(-1, described.shape[1])

    def block(h):
        part = coefs[:, :, h * half : (h + 1) * half]
        blank = jnp.zeros_like(part[0])
        return jnp.concatenate(
            [jnp.concatenate([part[0], part[2]], axis=1), jnp.concatenate([part[1], blank], axis=1)],
            axis=0,
        )

    def edge_fields(fields_4d, depth, bottom):
        first = rows - depth if bottom else 0
        return fields_4d[:, :, first : first + depth].reshape(-1, lon)

    def edge_coefs(h, bottom):
        first = rows - CROWS if bottom else 0
        part = coefs[:, first : first + CROWS, h * half : (h + 1) * half]
        part = jnp.pad(part.reshape(3 * CROWS, half), ((0, 16 - 3 * CROWS), (0, 0)))
        return jnp.concatenate([part[:8], part[8:]], axis=1)

    received = []
    for bottom, pairs in ((False, up), (True, down)):
        message = [edge_fields(background, HALO, bottom), edge_coefs(0, bottom)]
        message = lax.ppermute(jnp.concatenate(message, axis=0), "lat", pairs)
        diagonal = lax.ppermute(edge_fields(around, 1, bottom), "lat", pairs)
        received.append((message, diagonal, lax.ppermute(edge_coefs(1, bottom), "lat", pairs)))
    (near, dnear, c_near), (far, dfar, c_far) = received
    r_c = jnp.concatenate([block(1), c_near, c_far], axis=0)
    p_bg, r_bg = background.reshape(-1, lon), around.reshape(-1, lon)
    return p_bg, r_bg, block(0), r_c, near, far, dnear, dfar, sens


def shards(
    background, conv_weight, conv_bias, mix_weight, mix_bias, out_weight, out_bias,
    drift_east, drift_north, diffusivity, sensors, observations,
):
    frames, variables, rows, lon = background.shape
    tiles, bands = lax.axis_size("tm"), lax.axis_size("lat")
    paired = tiles == 2 and bands % 2 == 0
    group = rows // 2
    hid = mix_weight.shape[0]
    fields = frames * variables
    arrays = (background, drift_east, drift_north, diffusivity, sensors, observations)
    if paired:
        p_bg, r_bg, p_c, near, far, dnear, dfar = exchange_pairs(*arrays)
        offsets = [[*range(2 * frames)], [*range(frames), *range(-frames, 0)]]
        i_of = lambda: lax.axis_index("tm")
        parity_of = lambda: lax.axis_index("lat") % 2
        near, far, r_bg = lax.optimization_barrier((near, far, r_bg))
        relayed, sens = (p_c, near, far), ()
    else:
        p_bg, r_bg, q_c, r_c, near, far, dnear, dfar, sens = exchange_gathered(*arrays)
        offsets = [[*range(frames), *range(-frames, 0), *range(frames, 2 * frames)]]
        i_of = lambda: 0
        parity_of = lambda: 0
        relayed, sens = (), (sens,)
    others = len(offsets[0]) - frames

    channels = (frames + others) * variables
    depth = -(-(3 * round16((group + 2) * channels) + 3) // 128) * 128
    quarters = 8 // variables
    width = lon // 8
    taps = jnp.asarray(np.stack([tap_table(o, frames, variables, group, depth) for o in offsets]))
    own, coef, back, halo, chalo, ohalo = model_tables(rows, frames, variables, quarters)
    gather = conv_table(rows, frames, others, variables, group)
    index = np.stack(
        [index_rows([gather[c], *halo[c], chalo[c], own, coef, back, ohalo[c]], 256) for c in range(5)]
    )
    tables = [gather[0], own, coef, back, halo[0], chalo[0], ohalo[0]]
    small = [conv_weight, conv_bias.reshape(1, -1), mix_weight, mix_bias.reshape(1, -1)]
    small += [out_weight, out_bias.reshape(1, -1)]
    with jax.named_scope("weights"):
        weights = call(
            functools.partial(
                prep_kernel, group=group, channels=channels, relay=paired, i_of=i_of,
                parity_of=parity_of,
            ),
            [struct((48, lon), BF)] * len(relayed[:1])
            + [
                struct((frames * group * hid, depth), BF),
                struct((group * hid, group * hid), BF),
                struct((variables * group, group * hid), BF),
                struct((group * hid, 128), F32),
                struct((variables * group, 128), F32),
            ]
            + [struct(x.shape, BF) for x in tables],
            [pltpu.VMEM(x.shape, x.dtype) for x in small]
            + [pltpu.VMEM(taps.shape[1:], jnp.int32), pltpu.VMEM(index.shape[1:], jnp.int32)]
            + [pltpu.SemaphoreType.DMA((9,))],
            *small, taps, jnp.asarray(index), *relayed, fetched=range(9),
        )
    if paired:
        q_c, *weights = weights
        pairs = swap_pairs(tiles, bands)[0]
        late, dnear, dfar = lax.optimization_barrier((q_c, dnear, dfar))
        r_c = lax.ppermute(late, ("tm", "lat"), pairs)
    *w_conv, p_conv = weights[:6]
    p_model = weights[6:]
    with jax.named_scope("prior"):
        prior = call(
            functools.partial(
                conv_kernel, frames=frames, variables=variables, group=group, chunk=256
            ),
            struct(background.shape, F32),
            [pltpu.VMEM((rows // group, depth, lon), BF)],
            p_bg, r_bg, near, far, dnear, dfar, *w_conv, p_conv,
            cost=COST,
        )
    tall, ctall = rows + 2 * HALO, rows + 2 * CROWS
    with jax.named_scope("model"):
        return call(
            functools.partial(
                model_kernel, rows=rows, frames=frames, variables=variables,
                tile_cols=drift_east.shape[1], n_sens=sensors.shape[3],
                paired=paired, i_of=i_of, parity_of=parity_of,
            ),
            struct(background.shape, F32),
            [
                pltpu.VMEM((2 * frames, tall, 8, width), F32),
                pltpu.VMEM((2 * frames, tall, 8, width), F32),
                pltpu.VMEM((2, 5, ctall, 8, width), F32),
            ],
            p_bg, q_c, r_c, near, far, dnear, dfar, *sens, prior, *p_model,
        )


def solution(mesh):
    placed = (
        P("tm", None, "lat", None),
        P(),
        P(),
        P(),
        P(),
        P(),
        P(),
        P("lat", "tm"),
        P("lat", "tm"),
        P("lat", "tm"),
        P(None, "lat", "tm", None),
        P(None, "lat", "tm", None, None),
    )
    return jax.shard_map(
        shards, mesh=mesh, in_specs=placed, out_specs=P("tm", None, "lat", None), check_vma=False
    )
```

```python
import functools

import jax
import jax.numpy as jnp
import numpy as np
from jax import lax
from jax.experimental import pallas as pl
from jax.experimental.pallas import tpu as pltpu
from jax.sharding import PartitionSpec as P

KT = 5
SUB = 3
K_MID = 0.17
HALO = 2 * SUB
CROWS = 2 * SUB - 1
BF = jnp.bfloat16
F32 = jnp.float32
VMEM_BYTES = 48 * 1024 * 1024
COST = 60 * 10**6
PACK_BYTES = 64 * 1024 * 1024 - 1024 * 1024
GELU_1 = 2.0 * float(np.sqrt(2.0 / np.pi))
GELU_2 = 8.0 * 0.044715 * float(np.sqrt(2.0 / np.pi))


def dot(a, b):
    return jnp.dot(a, b, preferred_element_type=F32)


def dot_t(a, b):
    return lax.dot_general(a, b, (((1,), (1,)), ((), ())), preferred_element_type=F32)


def split2(x):
    high = x.astype(BF)
    return high, (x - high.astype(F32)).astype(BF)


def fetch(pairs, sems):
    copies = [pltpu.make_async_copy(source, target, sems.at[n]) for n, (source, target) in enumerate(pairs)]
    for copy in copies:
        copy.start()
    for copy in copies:
        copy.wait()


def pack_table(rows, fields):
    table = np.zeros((2, 2, 80, 128), np.float32)
    coef_row = fields * rows
    for parity in range(2):
        for side in range(2):
            for message in range(4):
                far, diagonal = message % 2, message // 2
                bottom = (far == 0) == (parity == 0)
                out = table[parity, side]
                if diagonal:
                    base = 64 + 8 * far
                    for field in range(fields):
                        out[base + field, field * rows + (rows - 1 if bottom else 0)] = 1
                    if side == 0:
                        out[base + fields, coef_row + 3 * rows + 15] = 1
                    continue
                base = 32 * far
                for field in range(fields):
                    for e in range(HALO):
                        row = rows - HALO + e if bottom else e
                        out[base + field * HALO + e, field * rows + row] = 1
                for slot in range(8):
                    j = side * 8 + slot
                    target = base + 24 + slot
                    if j < 3 * CROWS:
                        c, e = divmod(j, CROWS)
                        row = rows - CROWS + e if bottom else e
                        out[target, coef_row + c * rows + row] = 1
                    else:
                        out[target, coef_row + 3 * rows + 14] = 1
    return table


def near_far(case):
    parity = case in (1, 3)
    top_ok = case != 2
    bottom_ok = case not in (3, 4)
    top_slot = 0 if parity else 1
    return top_slot, 1 - top_slot, top_ok, bottom_ok


def model_tables(rows, frames, variables, quarters):
    lanes = quarters * variables
    own = np.zeros((rows * lanes, quarters * variables * rows), np.float32)
    coef = np.zeros((rows * lanes, quarters * rows), np.float32)
    out = np.zeros((lanes * rows, rows * lanes), np.float32)
    for r in range(rows):
        for q in range(quarters):
            for v in range(variables):
                own[r * lanes + q * variables + v, (q * variables + v) * rows + r] = 1
                coef[r * lanes + q * variables + v, q * rows + r] = 1
                out[(q * variables + v) * rows + r, r * lanes + q * variables + v] = 1
    halo = np.zeros((5, frames, 2 * HALO * lanes, quarters * 64), np.float32)
    chalo = np.zeros((5, 3 * 2 * CROWS * lanes, quarters * 64), np.float32)
    ohalo = np.zeros((5, 3 * 2 * CROWS * lanes, quarters * 32), np.float32)
    for case in range(5):
        top_slot, bottom_slot, top_ok, bottom_ok = near_far(case)
        for q in range(quarters):
            for v in range(variables):
                lane = q * variables + v
                for half, slot, ok in ((0, top_slot, top_ok), (1, bottom_slot, bottom_ok)):
                    if not ok:
                        continue
                    for t in range(frames):
                        for e in range(HALO):
                            local = (t * variables + v) * HALO + e
                            halo[case, t, (half * HALO + e) * lanes + lane, q * 64 + slot * 32 + local] = 1
                    for c in range(3):
                        for e in range(CROWS):
                            j = c * CROWS + e
                            column = q * 64 + slot * 32 + (j // 8) * 16 + 8 + j % 8
                            row = ((c * 2 + half) * CROWS + e) * lanes + lane
                            chalo[case, row, column] = 1
                            column = q * 32 + (j // 8) * 16 + slot * 8 + j % 8
                            ohalo[case, row, column] = 1
    return own, coef, out, halo, chalo, ohalo


def round16(n):
    return -(-n // 16) * 16


def conv_table(rows, frames, others, variables, group):
    channels = (frames + others) * variables
    tall = round16((group + 2) * channels)
    own_rows = frames * variables * rows
    oth_rows = others * variables * rows
    table = np.zeros((5, rows // group * tall, own_rows + oth_rows + 80), np.float32)
    for case in range(5):
        top_slot, bottom_slot, top_ok, bottom_ok = near_far(case)
        for g in range(rows // group):
            for yy in range(group + 2):
                y = g * group + yy - 1
                for f in range(frames + others):
                    for v in range(variables):
                        target = g * tall + yy * channels + f * variables + v
                        own = f < frames
                        field = (f if own else f - frames) * variables + v
                        if 0 <= y < rows:
                            table[case, target, (0 if own else own_rows) + field * rows + y] = 1
                            continue
                        slot, ok = (top_slot, top_ok) if y < 0 else (bottom_slot, bottom_ok)
                        if not ok:
                            continue
                        column = own_rows + oth_rows
                        if own:
                            column += slot * 32 + field * HALO + (HALO - 1 if y < 0 else 0)
                        else:
                            column += 64 + slot * 8 + field
                        table[case, target, column] = 1
    return table


def tap_table(offsets, frames, variables, group, depth):
    channels = len(offsets) * variables
    tall = round16((group + 2) * channels)
    table = np.full((8, depth), -1, np.int32)
    for t in range(frames):
        for s in range(3):
            for i in range(3):
                for f, offset in enumerate(offsets):
                    lag = offset - t + KT // 2
                    for v in range(variables):
                        if 0 <= lag < KT:
                            k = s * tall + i * channels + f * variables + v
                            table[t, k] = ((v * KT + lag) * 3 + i) * 3 + s
    table[frames, 3 * tall : 3 * tall + 3] = 3 * 3 * KT * variables + np.arange(3)
    return table


def index_rows(tables, lanes):
    out = np.full((8, lanes), -1, np.int32)
    for n, table in enumerate(tables):
        out[n, : table.shape[0]] = np.where(table.any(1), table.argmax(1), -1)
    return out


def case_of(parity, index, count):
    return jnp.where(index == 0, 2, jnp.where(index == count - 1, jnp.where(parity == 1, 3, 4), parity))


def pack_kernel(
    bg_in, east_in, north_in, diff_in, sensors_in, obs_in, table_in, p_c, near, far, dnear, dfar,
    bg, east, north, diff, sensors, obs, table, sems, *, frames,
):
    me_t = lax.axis_index("tm")
    parity = lax.axis_index("lat") % 2
    fetch(
        [
            (bg_in, bg), (east_in, east), (north_in, north), (diff_in, diff),
            (sensors_in, sensors), (obs_in, obs), (table_in.at[parity], table),
        ],
        sems,
    )
    fields = bg.shape[0] * bg.shape[1]
    rows, lon = bg.shape[2], bg.shape[3]
    half = lon // 2
    fields_2d = bg[...].reshape(fields * rows, lon)
    a, b = east[...].astype(BF), north[...].astype(BF)
    k = (diff[...] - K_MID).astype(BF)

    def described(first, low):
        pieces = []
        for t in range(frames):
            cells = sensors[first + t, 0]
            if not low:
                pieces += [(cells >> 8).astype(F32), (cells & 255).astype(F32)]
            for v in range(obs.shape[3]):
                value = obs[first + t, 0, 0, v : v + 1]
                high = value.astype(BF).astype(F32)
                pieces.append(value - high if low else high)
        row = jnp.concatenate(pieces, axis=1)
        if row.shape[1] < half:
            row = jnp.concatenate([row, jnp.zeros((1, half - row.shape[1]), F32)], axis=1)
        return row

    mine, theirs = me_t * frames, (1 - me_t) * frames
    extra = jnp.concatenate(
        [
            jnp.zeros((12, half), F32),
            described(mine, True),
            described(theirs, True),
            described(mine, False),
            described(theirs, False),
        ],
        axis=0,
    ).astype(BF)
    p_c[0:rows, 0:half] = a
    p_c[rows : 2 * rows, 0:half] = b
    p_c[0:rows, half:lon] = k
    p_c[rows : 2 * rows, half:lon] = extra
    for side in range(2):
        cut = slice(side * half, (side + 1) * half)
        source = jnp.concatenate([fields_2d[:, cut], a, b, k, extra], axis=0)
        message = dot(table[side], source).astype(BF)
        near[:, cut] = message[0:32]
        far[:, cut] = message[32:64]
        dnear[:, cut] = message[64:72]
        dfar[:, cut] = message[72:80]


def relay_kernel(near, far, out):
    edge = near.shape[0] - 8
    out[0:8, :] = near[edge : edge + 8, :]
    out[8:16, :] = far[edge : edge + 8, :]


def prep_kernel(*refs, group, channels, i_of, parity_of):
    sources, rest = refs[:8], refs[8:]
    w1, w2, w3, b2, b3, p_conv, p_own, p_coef, p_out, p_halo, p_chalo, p_ohalo = rest[:12]
    conv_w, conv_b, mix_w, mix_b, out_w, out_b, taps, index, sems = rest[12:]
    hid = mix_w.shape[0]
    case = case_of(parity_of(), lax.axis_index("lat"), lax.axis_size("lat"))
    moves = [*zip(sources[:6], (conv_w, conv_b, mix_w, mix_b, out_w, out_b))]
    moves += [(sources[6].at[i_of()], taps), (sources[7].at[case], index)]
    fetch(moves, sems)
    columns = index[...].astype(F32).T

    def select(n, shape):
        lanes = lax.broadcasted_iota(jnp.int32, shape, 1).astype(F32)
        return jnp.where(lanes == columns[0 : shape[0], n : n + 1], 1.0, 0.0)

    frames = p_halo.shape[0]
    p_conv[...] = select(0, p_conv.shape).astype(BF)
    for t in range(frames):
        p_halo[t] = select(1 + t, p_halo.shape[1:]).astype(BF)
    for n, target in ((1 + frames, p_chalo), (5 + frames, p_ohalo)):
        halved = lax.broadcasted_iota(jnp.int32, target.shape, 0) < target.shape[0] // 3 * 2
        target[...] = (select(n, target.shape) * jnp.where(halved, 0.5, 1.0)).astype(BF)
    p_own[...] = select(2 + frames, p_own.shape).astype(BF)
    p_coef[...] = select(3 + frames, p_coef.shape).astype(BF)
    p_out[...] = select(4 + frames, p_out.shape).astype(BF)
    table = taps[...]

    def column(row):
        n = row.shape[1]
        here = lax.broadcasted_iota(jnp.int32, (n, n), 0) == lax.broadcasted_iota(jnp.int32, (n, n), 1)
        return jnp.sum(jnp.where(here, jnp.broadcast_to(row, (n, n)), 0.0), axis=1, keepdims=True)

    bias = 0.5 * column(conv_b[...])
    pieces = []
    for _ in range(3):
        piece = bias.astype(BF)
        bias = bias - piece.astype(F32)
        pieces.append(piece.astype(F32))
    ntap = conv_w.shape[1]
    padded = 128
    weights = jnp.concatenate(
        [0.5 * conv_w[...].astype(F32)] + pieces + [jnp.zeros((hid, padded - ntap - 3), F32)], axis=1
    ).astype(BF)
    tap_id = lax.broadcasted_iota(jnp.int32, (padded, table.shape[1]), 0)

    def chosen(n):
        return dot(weights, jnp.where(tap_id == table[n : n + 1, :], 1.0, 0.0).astype(BF))

    biased = chosen(frames)
    for t in range(frames):
        first = chosen(t)
        for y in range(group):
            start = (t * group + y) * hid
            moved = pltpu.roll(first, y * channels, 1) if y else first
            w1[start : start + hid, :] = (moved + biased).astype(BF)
    tall = group * hid
    row = lax.broadcasted_iota(jnp.int32, (tall, hid), 0) & (hid - 1)
    up = jnp.where(row == lax.broadcasted_iota(jnp.int32, (tall, hid), 1), 1.0, 0.0).astype(BF)
    mixed = dot_t(dot(up, (0.5 * mix_w[...].astype(F32)).astype(BF)).astype(BF), up)
    shift = hid.bit_length() - 1
    rows2 = lax.broadcasted_iota(jnp.int32, (tall, tall), 0) >> shift
    cols2 = lax.broadcasted_iota(jnp.int32, (tall, tall), 1) >> shift
    w2[...] = jnp.where(rows2 == cols2, mixed, 0.0).astype(BF)
    variables = out_w.shape[0]
    wide = dot_t(out_w[...], up)
    y = lax.broadcasted_iota(jnp.int32, (group, tall), 0)
    here = y == lax.broadcasted_iota(jnp.int32, (group, tall), 1) >> shift
    w3[...] = jnp.concatenate(
        [jnp.where(here, jnp.broadcast_to(wide[v : v + 1], (group, tall)), 0.0) for v in range(variables)],
        axis=0,
    ).astype(BF)
    b3[...] = jnp.concatenate(
        [jnp.broadcast_to(out_b[:, v : v + 1], (group, 128)) for v in range(variables)], axis=0
    )
    mixed_bias = jnp.broadcast_to(0.5 * column(mix_b[...]), (hid, 128))
    b2[...] = jnp.concatenate([mixed_bias] * group, axis=0)


def model_kernel(
    p_bg, p_c, r_c, r_e, near, far, dnear, dfar, *rest,
    rows, frames, variables, tile_cols, n_sens, paired, i_of, parity_of,
):
    sens = None if paired else rest[0]
    first = 0 if paired else 1
    prior, p_own, p_coef, p_out, p_halo, p_chalo, p_ohalo = rest[first : first + 7]
    out, field_a, field_b, coefs = rest[first + 7 :]
    lon = p_bg.shape[1]
    half = lon // 2
    quarters = 8 // variables
    width = half // quarters
    me_l, count = lax.axis_index("lat"), lax.axis_size("lat")
    parity = parity_of()
    me_t = i_of()
    top_ok, bottom_ok = me_l > 0, me_l < count - 1
    tall = rows + 2 * HALO

    for t in range(frames):
        for h in range(2):
            g = t * 2 + h
            body, rim = [], []
            for q in range(quarters):
                cut = slice(h * half + q * width, h * half + (q + 1) * width)
                body.append(p_bg[t * variables * rows : (t + 1) * variables * rows, cut])
                rim += [near[:, cut], far[:, cut]]
            field_a[g, HALO : HALO + rows] = dot(p_own[...], jnp.concatenate(body, axis=0)).reshape(rows, 8, width)
            edges = dot(p_halo[t], jnp.concatenate(rim, axis=0)).reshape(2 * HALO, 8, width)
            field_a[g, 0:HALO] = edges[0:HALO]
            field_a[g, HALO + rows : tall] = edges[HALO:]

    ctall = rows + 2 * CROWS
    for source in range(2):
        big = p_c if source == 0 else r_c
        spot = me_t if source == 0 else 1 - me_t
        pieces = []
        for side in range(2):
            for c_row in range(2):
                stack = []
                for q in range(quarters):
                    cut = slice(side * half + q * width, side * half + (q + 1) * width)
                    stack.append(big[c_row * rows : (c_row + 1) * rows, cut])
                pieces.append(jnp.concatenate(stack, axis=0))
        scaled = p_coef[...]
        ha = (0.5 * dot(scaled, pieces[0])).reshape(rows, 8, width)
        hb = (0.5 * dot(scaled, pieces[1])).reshape(rows, 8, width)
        kk = dot(scaled, pieces[2]).reshape(rows, 8, width) + K_MID
        rim = []
        for q in range(quarters):
            for message in (near[16:32], far[16:32]) if source == 0 else (r_e,):
                for side in range(2):
                    cut = slice(side * half + q * width, side * half + (q + 1) * width)
                    rim.append(message[:, cut])
        edges = dot((p_ohalo if source else p_chalo)[...], jnp.concatenate(rim, axis=0))
        edges = edges.reshape(3, 2, CROWS, 8, width)
        k_top = edges[2, 0] + jnp.where(top_ok, K_MID, 0.0)
        k_bottom = edges[2, 1] + jnp.where(bottom_ok, K_MID, 0.0)
        for start, size, xa, xb, xk in (
            (0, CROWS, edges[0, 0], edges[1, 0], k_top),
            (CROWS, rows, ha, hb, kk),
            (CROWS + rows, CROWS, edges[0, 1], edges[1, 1], k_bottom),
        ):
            span = slice(start, start + size)
            coefs[spot, 0, span] = xk - xa
            coefs[spot, 1, span] = xk + xa
            coefs[spot, 2, span] = xk - xb
            coefs[spot, 3, span] = xk + xb
            coefs[spot, 4, span] = 1.0 - 4.0 * xk

    lane = lax.broadcasted_iota(jnp.int32, (8, 128), 1)
    sub_q = lax.broadcasted_iota(jnp.int32, (8, 128), 0) >> (variables.bit_length() - 1)
    first_lane, last_lane = lane == 0, lane == 127
    first_q, last_q = sub_q == 0, sub_q == quarters - 1
    tiles = width // 128

    def cut_tiles(x):
        return [x[:, n * 128 : (n + 1) * 128] for n in range(tiles)]

    def from_west(x0, x1):
        both = [[pltpu.roll(part, 1, 1) for part in cut_tiles(x)] for x in (x0, x1)]
        result = []
        for h in range(2):
            wrapped = jnp.where(last_q, both[1 - h][-1], both[h][-1])
            carry = pltpu.roll(wrapped, variables, 0)
            parts = []
            for n in range(tiles):
                parts.append(jnp.where(first_lane, carry if n == 0 else both[h][n - 1], both[h][n]))
            result.append(jnp.concatenate(parts, axis=1))
        return result

    def from_east(x0, x1):
        both = [[pltpu.roll(part, 127, 1) for part in cut_tiles(x)] for x in (x0, x1)]
        result = []
        for h in range(2):
            wrapped = jnp.where(first_q, both[1 - h][0], both[h][0])
            carry = pltpu.roll(wrapped, 8 - variables, 0)
            parts = []
            for n in range(tiles):
                parts.append(
                    jnp.where(last_lane, carry if n == tiles - 1 else both[h][n + 1], both[h][n])
                )
            result.append(jnp.concatenate(parts, axis=1))
        return result

    def forward(source, target, low, high):
        for r in range(low, high):
            cr = r - (HALO - CROWS)
            for t in range(frames):
                center = [source[t * 2 + h, r] for h in range(2)]
                west, east = from_west(*center), from_east(*center)
                for h in range(2):
                    g = t * 2 + h
                    target[g, r] = (
                        (coefs[h, 4, cr] * center[h] + coefs[h, 0, cr] * east[h])
                        + (coefs[h, 1, cr] * west[h] + coefs[h, 2, cr] * source[g, r + 1])
                        + coefs[h, 3, cr] * source[g, r - 1]
                    )

    def backward(source, target, low, high):
        for r in range(low, high):
            cr = r - (HALO - CROWS)
            for t in range(frames):
                center = [source[t * 2 + h, r] for h in range(2)]
                west = from_west(*[coefs[h, 0, cr] * center[h] for h in range(2)])
                east = from_east(*[coefs[h, 1, cr] * center[h] for h in range(2)])
                for h in range(2):
                    g = t * 2 + h
                    target[g, r] = (
                        (coefs[h, 4, cr] * center[h] + west[h])
                        + (east[h] + coefs[h, 2, cr - 1] * source[g, r - 1])
                        + coefs[h, 3, cr + 1] * source[g, r + 1]
                    )

    buffers = [field_a, field_b]
    for step in range(SUB):
        forward(buffers[step % 2], buffers[(step + 1) % 2], step + 1, tall - step - 1)
    forecast, spread = buffers[SUB % 2], buffers[(SUB + 1) % 2]

    def kinds(row, t):
        base = t * (2 + variables) * n_sens
        return [row[:, base + n * n_sens : base + (n + 1) * n_sens] for n in range(2 + variables)]

    def sensor_rows(h, band):
        if not paired:
            count = sens.shape[0] // 8
            first = (h * 4 + band) * count
            return [sens[...].astype(F32)[first + n : first + n + 1] for n in range(count)]
        if band in (1, 3):
            at = slice(rows, rows + 16)
            mine, other = p_c[at, half:lon].astype(F32), r_c[at, half:lon].astype(F32)
            n = 14 if band == 1 else 12
            return [jnp.where(me_t == h, mine[n : n + 1], other[n + 1 : n + 2])]
        from_far = parity == (0 if band == 0 else 1)
        pair = [m[16:32, half:lon].astype(F32)[15:16] for m in (near, far)]
        row = frames * variables
        pair += [m[:, 0:half].astype(F32)[row : row + 1] for m in (dnear, dfar)]
        found = [jnp.where(from_far, pair[n + 1], pair[n]) for n in (0, 2)]
        return [jnp.where(me_t == h, found[0], found[1])]

    row_bits = tile_cols.bit_length() - 1
    width_bits = width.bit_length() - 1

    def located(h, band, t):
        found = []
        for n, row in enumerate(sensor_rows(h, band)):
            high, low, *values = kinds(row, t)
            cell = (high * 256.0 + low).astype(jnp.int32)
            column = (cell & (tile_cols - 1)) + n * tile_cols
            found.append([cell >> row_bits, column >> width_bits, column & (width - 1)] + list(values))
        if band == 1:
            for n, row in enumerate(sensor_rows(h, 3)):
                for v in range(variables):
                    found[n][3 + v] = found[n][3 + v] + row[:, (t * variables + v) * n_sens : (t * variables + v + 1) * n_sens]
        return [jnp.concatenate([f[n] for f in found], axis=1) for n in range(3 + variables)]

    def assimilate(g, row_list, where_row, quarter, lane_of, values):
        total = where_row.shape[1]
        lanes_bf = lax.broadcasted_iota(jnp.int32, (width, total), 0).astype(F32).astype(BF)
        onehot = jnp.where(lanes_bf == lane_of.astype(F32).astype(BF), BF(1), BF(0))
        stack = jnp.concatenate([forecast[g, HALO + r] for r in row_list], axis=0)
        high, low = split2(stack)
        picked = dot(high, onehot) + dot(low, onehot)
        shape = (8, total)
        here_q = (lax.broadcasted_iota(jnp.int32, shape, 0) >> (variables.bit_length() - 1)) == quarter
        variable = lax.broadcasted_iota(jnp.int32, shape, 0) & (variables - 1)
        misfit = jnp.zeros(shape, F32)
        for n, r in enumerate(row_list):
            misfit = misfit + jnp.where(where_row == r, picked[n * 8 : (n + 1) * 8], 0.0)
        target = jnp.broadcast_to(values[0], shape)
        for v in range(1, variables):
            target = jnp.where(variable == v, values[v], target)
        misfit = jnp.where(here_q, misfit - target, 0.0)
        row_f = where_row.astype(F32)
        weighted = jnp.concatenate([jnp.where(row_f == float(r), misfit, 0.0) for r in row_list], axis=0)
        high, low = split2(weighted)
        return (dot_t(high, onehot) + dot_t(low, onehot)).reshape(len(row_list), 8, width)

    far_away = -(1 << 20)
    for t in range(frames):
        for h in range(2):
            g = t * 2 + h
            row, quarter, lane_of, *values = located(h, 1, t)
            spread[g, HALO : HALO + rows] = assimilate(g, list(range(rows)), row, quarter, lane_of, values)
            above, below = located(h, 0, t), located(h, 2, t)
            above[0] = jnp.where(top_ok, above[0] - rows, far_away)
            below[0] = jnp.where(bottom_ok, below[0] + rows, far_away)
            merged = [jnp.concatenate([x, y], axis=1) for x, y in zip(above, below)]
            rim_rows = list(range(-SUB, 0)) + list(range(rows, rows + SUB))
            rim = assimilate(g, rim_rows, merged[0], merged[1], merged[2], merged[3:])
            spread[g, HALO - SUB : HALO] = rim[0:SUB]
            spread[g, HALO + rows : HALO + rows + SUB] = rim[SUB:]

    buffers = [spread, forecast]
    for step in range(SUB):
        low = HALO - SUB + step + 1
        backward(buffers[step % 2], buffers[(step + 1) % 2], low, tall - low)
    result = buffers[SUB % 2]

    for t in range(frames):
        for h in range(2):
            high, low = split2(result[t * 2 + h, HALO : HALO + rows].reshape(rows * 8, width))
            back = dot(p_out[...], high) + dot(p_out[...], low)
            for q in range(quarters):
                cut = slice(h * half + q * width, h * half + (q + 1) * width)
                for v in range(variables):
                    base = (q * variables + v) * rows
                    out[t, v, :, cut] = prior[t, v, :, cut] - back[base : base + rows]


def gelu(y):
    inner = y * (GELU_1 + GELU_2 * (y * y))
    return (y + y * jnp.tanh(inner)).astype(BF)


def shifted(chosen, window, depth):
    tall, lon = chosen.shape
    window[0:tall] = pltpu.roll(chosen, 1, 1).astype(BF)
    window[tall : 2 * tall] = chosen.astype(BF)
    window[2 * tall : 3 * tall] = pltpu.roll(chosen, lon - 1, 1).astype(BF)
    ones = lax.broadcasted_iota(jnp.int32, (depth - 3 * tall, lon), 0) < 3
    window[3 * tall : depth] = jnp.where(ones, 1.0, 0.0).astype(BF)


def widen(column, chunk):
    return jnp.concatenate([column] * (chunk // 128), axis=1)


def conv_kernel(
    p_bg, r_bg, near, far, dnear, dfar, w1, w2, w3, b2, b3, select, out, window,
    *, frames, variables, group, chunk,
):
    groups, depth, lon = window.shape
    fields = jnp.concatenate([x[...] for x in (p_bg, r_bg, near, far, dnear, dfar)], axis=0)
    chosen = dot(select[...], fields)
    tall = chosen.shape[0] // groups
    for g in range(groups):
        shifted(chosen[g * tall : (g + 1) * tall], window.at[g], depth)
    hidden = w2.shape[0]
    bias2, bias3 = widen(b2[...], chunk), widen(b3[...], chunk)
    pending = []
    wide2 = jnp.concatenate([bias2] * frames, axis=1)
    for n in range(lon // chunk):
        cut = slice(n * chunk, (n + 1) * chunk)
        for g in range(groups):
            first = dot(w1[...], window[g, :, cut])
            one = [gelu(first[t * hidden : (t + 1) * hidden]) for t in range(frames)]
            pending.append((g, cut, gelu(dot(w2[...], jnp.concatenate(one, axis=1)) + wide2)))
    for g, cut, two in pending:
        scores = dot(w3[...], two)
        for t in range(frames):
            score = scores[:, t * chunk : (t + 1) * chunk] + bias3
            for v in range(variables):
                out[t, v, g * group : (g + 1) * group, cut] = score[v * group : (v + 1) * group]


def call(body, out_shape, scratch, *args, fetched=(), limit=VMEM_BYTES, cost=None):
    whole = pl.BlockSpec(memory_space=pltpu.VMEM)
    given = pl.BlockSpec(memory_space=pltpu.HBM)
    several = isinstance(out_shape, (list, tuple))
    if cost is not None:
        cost = pl.CostEstimate(flops=10**8, bytes_accessed=cost, transcendentals=0)
    return pl.pallas_call(
        body,
        out_shape=out_shape,
        in_specs=[given if n in fetched else whole for n in range(len(args))],
        out_specs=[whole] * len(out_shape) if several else whole,
        scratch_shapes=scratch,
        compiler_params=pltpu.CompilerParams(vmem_limit_bytes=limit),
        cost_estimate=cost,
    )(*args)


def struct(shape, dtype):
    return jax.ShapeDtypeStruct(shape, dtype)


def swap_pairs(tiles, bands):
    def at(t, j):
        return t * bands + j

    def far(j):
        return j + 1 if j % 2 else j - 1

    cells = [(t, j) for t in range(tiles) for j in range(bands)]
    inner = lambda j: 0 <= far(j) < bands
    return (
        [(at(t, j), at(1 - t, j)) for t, j in cells],
        [(at(t, j), at(t, j ^ 1)) for t, j in cells],
        [(at(t, j), at(t, far(j)) if inner(j) else at(1 - t, j)) for t, j in cells],
        [(at(t, j), at(1 - t, j ^ 1)) for t, j in cells],
        [(at(t, j), at(1 - t, far(j)) if inner(j) else at(1 - t, j)) for t, j in cells],
    )


def exchange_pairs(background, east, north, diff, sensors, observations):
    frames, variables, rows, lon = background.shape
    fields = frames * variables
    bands = lax.axis_size("lat")
    table = jnp.asarray(pack_table(rows, fields), BF)
    arrays = (background, east, north, diff, sensors, observations)
    lat_message, diagonal = struct((32, lon), BF), struct((8, lon), BF)
    with jax.named_scope("pack"):
        p_c, near, far, dnear, dfar = call(
            functools.partial(pack_kernel, frames=frames),
            [struct((2 * rows, lon), BF), lat_message, lat_message, diagonal, diagonal],
            [pltpu.VMEM(x.shape, x.dtype) for x in arrays]
            + [pltpu.VMEM(table.shape[1:], BF), pltpu.SemaphoreType.DMA((7,))],
            *arrays, table, fetched=range(7), limit=PACK_BYTES,
        )
    axes = ("tm", "lat")
    across, on_chip, next_chip, diag_near, diag_far = swap_pairs(lax.axis_size("tm"), bands)
    p_bg = background.reshape(fields * rows, lon)
    r_bg = lax.ppermute(p_bg, axes, across)
    r_dfar = lax.ppermute(dfar, axes, diag_far)
    r_far = lax.ppermute(far, axes, next_chip)
    r_dnear = lax.ppermute(dnear, axes, diag_near)
    r_near = lax.ppermute(near, axes, on_chip)
    return p_bg, r_bg, p_c, r_near, r_far, r_dnear, r_dfar


def exchange_gathered(background, east, north, diff, sensors, observations):
    frames, variables, rows, lon = background.shape
    fields = frames * variables
    half = lon // 2
    tiles, bands = lax.axis_size("tm"), lax.axis_size("lat")
    down = [(j, j + 1) for j in range(bands - 1)]
    up = [(j + 1, j) for j in range(bands - 1)]
    later = [(t, t + 1) for t in range(tiles - 1)]
    earlier = [(t + 1, t) for t in range(tiles - 1)]
    coefs = jnp.stack([east, north, diff - K_MID]).astype(BF)
    coefs = lax.all_gather(coefs, "tm", axis=2, tiled=True)
    around = jnp.concatenate(
        [lax.ppermute(background, "tm", later), lax.ppermute(background, "tm", earlier)], axis=0
    )
    cells = lax.all_to_all(sensors, "tm", split_axis=0, concat_axis=2, tiled=True)[:, 0]
    obs = lax.all_to_all(observations, "tm", split_axis=0, concat_axis=2, tiled=True)[:, 0]
    cells = jnp.moveaxis(cells, 1, 0)
    obs = jnp.transpose(obs, (1, 0, 2, 3))
    obs_high = obs.astype(BF).astype(F32)
    digits = jnp.stack([(cells >> 8).astype(F32), (cells & 255).astype(F32)], axis=2)
    described = jnp.concatenate([digits, obs_high], axis=2).reshape(tiles, -1).astype(BF)
    low = (obs - obs_high).astype(BF).reshape(tiles, -1)
    low = jnp.pad(low, ((0, 0), (0, described.shape[1] - low.shape[1])))
    bands_of = [
        lax.ppermute(described, "lat", down), described, lax.ppermute(described, "lat", up), low
    ]
    sens = jnp.stack([x.reshape(2, tiles // 2, -1) for x in bands_of], axis=1)
    sens = sens.reshape(-1, described.shape[1])

    def block(h):
        part = coefs[:, :, h * half : (h + 1) * half]
        blank = jnp.zeros_like(part[0])
        return jnp.concatenate(
            [jnp.concatenate([part[0], part[2]], axis=1), jnp.concatenate([part[1], blank], axis=1)],
            axis=0,
        )

    def edge_fields(fields_4d, depth, bottom):
        first = rows - depth if bottom else 0
        return fields_4d[:, :, first : first + depth].reshape(-1, lon)

    def edge_coefs(h, bottom):
        first = rows - CROWS if bottom else 0
        part = coefs[:, first : first + CROWS, h * half : (h + 1) * half]
        part = jnp.pad(part.reshape(3 * CROWS, half), ((0, 16 - 3 * CROWS), (0, 0)))
        return jnp.concatenate([part[:8], part[8:]], axis=1)

    received = []
    for bottom, pairs in ((False, up), (True, down)):
        message = [edge_fields(background, HALO, bottom), edge_coefs(0, bottom)]
        message = lax.ppermute(jnp.concatenate(message, axis=0), "lat", pairs)
        diagonal = lax.ppermute(edge_fields(around, 1, bottom), "lat", pairs)
        received.append((message, diagonal, lax.ppermute(edge_coefs(1, bottom), "lat", pairs)))
    (near, dnear, c_near), (far, dfar, c_far) = received
    r_e = jnp.concatenate([c_near, c_far], axis=0)
    p_bg, r_bg = background.reshape(-1, lon), around.reshape(-1, lon)
    return p_bg, r_bg, block(0), block(1), r_e, near, far, dnear, dfar, sens


def shards(
    background, conv_weight, conv_bias, mix_weight, mix_bias, out_weight, out_bias,
    drift_east, drift_north, diffusivity, sensors, observations,
):
    frames, variables, rows, lon = background.shape
    tiles, bands = lax.axis_size("tm"), lax.axis_size("lat")
    paired = tiles == 2 and bands % 2 == 0
    group = rows // 2
    hid = mix_weight.shape[0]
    fields = frames * variables
    arrays = (background, drift_east, drift_north, diffusivity, sensors, observations)
    if paired:
        p_bg, r_bg, p_c, near, far, dnear, dfar = exchange_pairs(*arrays)
        offsets = [[*range(2 * frames)], [*range(frames), *range(-frames, 0)]]
        i_of = lambda: lax.axis_index("tm")
        parity_of = lambda: lax.axis_index("lat") % 2
        sens = ()
    else:
        p_bg, r_bg, p_c, r_c, r_e, near, far, dnear, dfar, sens = exchange_gathered(*arrays)
        offsets = [[*range(frames), *range(-frames, 0), *range(frames, 2 * frames)]]
        i_of = lambda: 0
        parity_of = lambda: 0
        sens = (sens,)
    others = len(offsets[0]) - frames

    channels = (frames + others) * variables
    depth = -(-(3 * round16((group + 2) * channels) + 3) // 128) * 128
    quarters = 8 // variables
    width = lon // 8
    taps = jnp.asarray(np.stack([tap_table(o, frames, variables, group, depth) for o in offsets]))
    own, coef, back, halo, chalo, ohalo = model_tables(rows, frames, variables, quarters)
    gather = conv_table(rows, frames, others, variables, group)
    index = np.stack(
        [index_rows([gather[c], *halo[c], chalo[c], own, coef, back, ohalo[c]], 256) for c in range(5)]
    )
    tables = [gather[0], own, coef, back, halo[0], chalo[0], ohalo[0]]
    small = [conv_weight, conv_bias.reshape(1, -1), mix_weight, mix_bias.reshape(1, -1)]
    small += [out_weight, out_bias.reshape(1, -1)]
    with jax.named_scope("weights"):
        weights = call(
            functools.partial(
                prep_kernel, group=group, channels=channels, i_of=i_of, parity_of=parity_of
            ),
            [
                struct((frames * group * hid, depth), BF),
                struct((group * hid, group * hid), BF),
                struct((variables * group, group * hid), BF),
                struct((group * hid, 128), F32),
                struct((variables * group, 128), F32),
            ]
            + [struct(x.shape, BF) for x in tables],
            [pltpu.VMEM(x.shape, x.dtype) for x in small]
            + [pltpu.VMEM(taps.shape[1:], jnp.int32), pltpu.VMEM(index.shape[1:], jnp.int32)]
            + [pltpu.SemaphoreType.DMA((8,))],
            *small, taps, jnp.asarray(index), fetched=range(8),
        )
    if paired:
        *weights, near, far, r_bg = lax.optimization_barrier((*weights, near, far, r_bg))
        with jax.named_scope("relay"):
            edges = call(relay_kernel, struct((16, lon), BF), [], near, far)
        pairs = swap_pairs(tiles, bands)[0]
        late, edges, dnear, dfar = lax.optimization_barrier((p_c, edges, dnear, dfar))
        r_c = lax.ppermute(late, ("tm", "lat"), pairs)
        r_e = lax.ppermute(edges, ("tm", "lat"), pairs)
    *w_conv, p_conv = weights[:6]
    p_model = weights[6:]
    with jax.named_scope("prior"):
        prior = call(
            functools.partial(
                conv_kernel, frames=frames, variables=variables, group=group, chunk=256
            ),
            struct(background.shape, F32),
            [pltpu.VMEM((rows // group, depth, lon), BF)],
            p_bg, r_bg, near, far, dnear, dfar, *w_conv, p_conv,
            cost=COST,
        )
    tall, ctall = rows + 2 * HALO, rows + 2 * CROWS
    with jax.named_scope("model"):
        return call(
            functools.partial(
                model_kernel, rows=rows, frames=frames, variables=variables,
                tile_cols=drift_east.shape[1], n_sens=sensors.shape[3],
                paired=paired, i_of=i_of, parity_of=parity_of,
            ),
            struct(background.shape, F32),
            [
                pltpu.VMEM((2 * frames, tall, 8, width), F32),
                pltpu.VMEM((2 * frames, tall, 8, width), F32),
                pltpu.VMEM((2, 5, ctall, 8, width), F32),
            ],
            p_bg, p_c, r_c, r_e, near, far, dnear, dfar, *sens, prior, *p_model,
        )


def solution(mesh):
    placed = (
        P("tm", None, "lat", None),
        P(),
        P(),
        P(),
        P(),
        P(),
        P(),
        P("lat", "tm"),
        P("lat", "tm"),
        P("lat", "tm"),
        P(None, "lat", "tm", None),
        P(None, "lat", "tm", None, None),
    )
    return jax.shard_map(
        shards, mesh=mesh, in_specs=placed, out_specs=P("tm", None, "lat", None), check_vma=False
    )
```

```python
import functools

import jax
import jax.numpy as jnp
import numpy as np
from jax import lax
from jax.experimental import pallas as pl
from jax.experimental.pallas import tpu as pltpu
from jax.sharding import PartitionSpec as P

KT = 5
SUB = 3
K_MID = 0.17
HALO = 2 * SUB
CROWS = 2 * SUB - 1
BF = jnp.bfloat16
F32 = jnp.float32
VMEM_BYTES = 48 * 1024 * 1024
COST = 60 * 10**6
PACK_BYTES = 64 * 1024 * 1024 - 1024 * 1024
GELU_1 = 2.0 * float(np.sqrt(2.0 / np.pi))
GELU_2 = 8.0 * 0.044715 * float(np.sqrt(2.0 / np.pi))


def dot(a, b):
    return jnp.dot(a, b, preferred_element_type=F32)


def dot_t(a, b):
    return lax.dot_general(a, b, (((1,), (1,)), ((), ())), preferred_element_type=F32)


def split2(x):
    high = x.astype(BF)
    return high, (x - high.astype(F32)).astype(BF)


def fetch(pairs, sems):
    copies = [pltpu.make_async_copy(source, target, sems.at[n]) for n, (source, target) in enumerate(pairs)]
    for copy in copies:
        copy.start()
    for copy in copies:
        copy.wait()


def pack_table(rows, fields):
    table = np.zeros((2, 2, 80, 128), np.float32)
    coef_row = fields * rows
    for parity in range(2):
        for side in range(2):
            for message in range(4):
                far, diagonal = message % 2, message // 2
                bottom = (far == 0) == (parity == 0)
                out = table[parity, side]
                if diagonal:
                    base = 64 + 8 * far
                    for field in range(fields):
                        out[base + field, field * rows + (rows - 1 if bottom else 0)] = 1
                    if side == 0:
                        out[base + fields, coef_row + 3 * rows + 15] = 1
                    continue
                base = 32 * far
                for field in range(fields):
                    for e in range(HALO):
                        row = rows - HALO + e if bottom else e
                        out[base + field * HALO + e, field * rows + row] = 1
                for slot in range(8):
                    j = side * 8 + slot
                    target = base + 24 + slot
                    if j < 3 * CROWS:
                        c, e = divmod(j, CROWS)
                        row = rows - CROWS + e if bottom else e
                        out[target, coef_row + c * rows + row] = 1
                    else:
                        out[target, coef_row + 3 * rows + 14] = 1
    return table


def near_far(case):
    parity = case in (1, 3)
    top_ok = case != 2
    bottom_ok = case not in (3, 4)
    top_slot = 0 if parity else 1
    return top_slot, 1 - top_slot, top_ok, bottom_ok


def model_tables(rows, frames, variables, quarters):
    lanes = quarters * variables
    own = np.zeros((rows * lanes, quarters * variables * rows), np.float32)
    coef = np.zeros((rows * lanes, quarters * rows), np.float32)
    out = np.zeros((lanes * rows, rows * lanes), np.float32)
    for r in range(rows):
        for q in range(quarters):
            for v in range(variables):
                own[r * lanes + q * variables + v, (q * variables + v) * rows + r] = 1
                coef[r * lanes + q * variables + v, q * rows + r] = 1
                out[(q * variables + v) * rows + r, r * lanes + q * variables + v] = 1
    halo = np.zeros((5, frames, 2 * HALO * lanes, quarters * 64), np.float32)
    chalo = np.zeros((5, 3 * 2 * CROWS * lanes, quarters * 64), np.float32)
    ohalo = np.zeros((5, 3 * 2 * CROWS * lanes, quarters * 32), np.float32)
    for case in range(5):
        top_slot, bottom_slot, top_ok, bottom_ok = near_far(case)
        for q in range(quarters):
            for v in range(variables):
                lane = q * variables + v
                for half, slot, ok in ((0, top_slot, top_ok), (1, bottom_slot, bottom_ok)):
                    if not ok:
                        continue
                    for t in range(frames):
                        for e in range(HALO):
                            local = (t * variables + v) * HALO + e
                            halo[case, t, (half * HALO + e) * lanes + lane, q * 64 + slot * 32 + local] = 1
                    for c in range(3):
                        for e in range(CROWS):
                            j = c * CROWS + e
                            column = q * 64 + slot * 32 + (j // 8) * 16 + 8 + j % 8
                            row = ((c * 2 + half) * CROWS + e) * lanes + lane
                            chalo[case, row, column] = 1
                            column = q * 32 + (j // 8) * 16 + slot * 8 + j % 8
                            ohalo[case, row, column] = 1
    return own, coef, out, halo, chalo, ohalo


def round16(n):
    return -(-n // 16) * 16


def conv_table(rows, frames, others, variables, group):
    channels = (frames + others) * variables
    tall = round16((group + 2) * channels)
    own_rows = frames * variables * rows
    oth_rows = others * variables * rows
    table = np.zeros((5, rows // group * tall, own_rows + oth_rows + 80), np.float32)
    for case in range(5):
        top_slot, bottom_slot, top_ok, bottom_ok = near_far(case)
        for g in range(rows // group):
            for yy in range(group + 2):
                y = g * group + yy - 1
                for f in range(frames + others):
                    for v in range(variables):
                        target = g * tall + yy * channels + f * variables + v
                        own = f < frames
                        field = (f if own else f - frames) * variables + v
                        if 0 <= y < rows:
                            table[case, target, (0 if own else own_rows) + field * rows + y] = 1
                            continue
                        slot, ok = (top_slot, top_ok) if y < 0 else (bottom_slot, bottom_ok)
                        if not ok:
                            continue
                        column = own_rows + oth_rows
                        if own:
                            column += slot * 32 + field * HALO + (HALO - 1 if y < 0 else 0)
                        else:
                            column += 64 + slot * 8 + field
                        table[case, target, column] = 1
    return table


def tap_table(offsets, frames, variables, group, depth):
    channels = len(offsets) * variables
    tall = round16((group + 2) * channels)
    table = np.full((8, depth), -1, np.int32)
    for t in range(frames):
        for s in range(3):
            for i in range(3):
                for f, offset in enumerate(offsets):
                    lag = offset - t + KT // 2
                    for v in range(variables):
                        if 0 <= lag < KT:
                            k = s * tall + i * channels + f * variables + v
                            table[t, k] = ((v * KT + lag) * 3 + i) * 3 + s
    table[frames, 3 * tall : 3 * tall + 3] = 3 * 3 * KT * variables + np.arange(3)
    return table


def index_rows(tables, lanes):
    out = np.full((8, lanes), -1, np.int32)
    for n, table in enumerate(tables):
        out[n, : table.shape[0]] = np.where(table.any(1), table.argmax(1), -1)
    return out


def case_of(parity, index, count):
    return jnp.where(index == 0, 2, jnp.where(index == count - 1, jnp.where(parity == 1, 3, 4), parity))


def pack_kernel(
    bg_in, east_in, north_in, diff_in, sensors_in, obs_in, table_in, p_c, near, far, dnear, dfar,
    bg, east, north, diff, sensors, obs, table, sems, *, frames,
):
    me_t = lax.axis_index("tm")
    parity = lax.axis_index("lat") % 2
    fetch(
        [
            (bg_in, bg), (east_in, east), (north_in, north), (diff_in, diff),
            (sensors_in, sensors), (obs_in, obs), (table_in.at[parity], table),
        ],
        sems,
    )
    fields = bg.shape[0] * bg.shape[1]
    rows, lon = bg.shape[2], bg.shape[3]
    half = lon // 2
    fields_2d = bg[...].reshape(fields * rows, lon)
    a, b = east[...].astype(BF), north[...].astype(BF)
    k = (diff[...] - K_MID).astype(BF)

    def described(first, low):
        pieces = []
        for t in range(frames):
            cells = sensors[first + t, 0]
            if not low:
                pieces += [(cells >> 8).astype(F32), (cells & 255).astype(F32)]
            for v in range(obs.shape[3]):
                value = obs[first + t, 0, 0, v : v + 1]
                high = value.astype(BF).astype(F32)
                pieces.append(value - high if low else high)
        row = jnp.concatenate(pieces, axis=1)
        if row.shape[1] < half:
            row = jnp.concatenate([row, jnp.zeros((1, half - row.shape[1]), F32)], axis=1)
        return row

    mine, theirs = me_t * frames, (1 - me_t) * frames
    extra = jnp.concatenate(
        [
            jnp.zeros((12, half), F32),
            described(mine, True),
            described(theirs, True),
            described(mine, False),
            described(theirs, False),
        ],
        axis=0,
    ).astype(BF)
    p_c[0:rows, 0:half] = a
    p_c[rows : 2 * rows, 0:half] = b
    p_c[0:rows, half:lon] = k
    p_c[rows : 2 * rows, half:lon] = extra
    for side in range(2):
        cut = slice(side * half, (side + 1) * half)
        source = jnp.concatenate([fields_2d[:, cut], a, b, k, extra], axis=0)
        message = dot(table[side], source).astype(BF)
        near[:, cut] = message[0:32]
        far[:, cut] = message[32:64]
        dnear[:, cut] = message[64:72]
        dfar[:, cut] = message[72:80]


def relay_kernel(far, near, out):
    edge = near.shape[0] - 8
    out[0:8, :] = near[edge : edge + 8, :]
    out[8:16, :] = far[edge : edge + 8, :]


def prep_kernel(*refs, group, channels, i_of, parity_of):
    sources, rest = refs[:8], refs[8:]
    w1, w2, w3, b2, b3, p_conv, p_own, p_coef, p_out, p_halo, p_chalo, p_ohalo = rest[:12]
    conv_w, conv_b, mix_w, mix_b, out_w, out_b, taps, index, sems = rest[12:]
    hid = mix_w.shape[0]
    case = case_of(parity_of(), lax.axis_index("lat"), lax.axis_size("lat"))
    moves = [*zip(sources[:6], (conv_w, conv_b, mix_w, mix_b, out_w, out_b))]
    moves += [(sources[6].at[i_of()], taps), (sources[7].at[case], index)]
    fetch(moves, sems)
    columns = index[...].astype(F32).T

    def select(n, shape):
        lanes = lax.broadcasted_iota(jnp.int32, shape, 1).astype(F32)
        return jnp.where(lanes == columns[0 : shape[0], n : n + 1], 1.0, 0.0)

    frames = p_halo.shape[0]
    p_conv[...] = select(0, p_conv.shape).astype(BF)
    for t in range(frames):
        p_halo[t] = select(1 + t, p_halo.shape[1:]).astype(BF)
    for n, target in ((1 + frames, p_chalo), (5 + frames, p_ohalo)):
        halved = lax.broadcasted_iota(jnp.int32, target.shape, 0) < target.shape[0] // 3 * 2
        target[...] = (select(n, target.shape) * jnp.where(halved, 0.5, 1.0)).astype(BF)
    p_own[...] = select(2 + frames, p_own.shape).astype(BF)
    p_coef[...] = select(3 + frames, p_coef.shape).astype(BF)
    p_out[...] = select(4 + frames, p_out.shape).astype(BF)
    table = taps[...]

    def column(row):
        n = row.shape[1]
        here = lax.broadcasted_iota(jnp.int32, (n, n), 0) == lax.broadcasted_iota(jnp.int32, (n, n), 1)
        return jnp.sum(jnp.where(here, jnp.broadcast_to(row, (n, n)), 0.0), axis=1, keepdims=True)

    bias = 0.5 * column(conv_b[...])
    pieces = []
    for _ in range(3):
        piece = bias.astype(BF)
        bias = bias - piece.astype(F32)
        pieces.append(piece.astype(F32))
    ntap = conv_w.shape[1]
    padded = 128
    weights = jnp.concatenate(
        [0.5 * conv_w[...].astype(F32)] + pieces + [jnp.zeros((hid, padded - ntap - 3), F32)], axis=1
    ).astype(BF)
    tap_id = lax.broadcasted_iota(jnp.int32, (padded, table.shape[1]), 0)

    def chosen(n):
        return dot(weights, jnp.where(tap_id == table[n : n + 1, :], 1.0, 0.0).astype(BF))

    biased = chosen(frames)
    for t in range(frames):
        first = chosen(t)
        for y in range(group):
            start = (t * group + y) * hid
            moved = pltpu.roll(first, y * channels, 1) if y else first
            w1[start : start + hid, :] = (moved + biased).astype(BF)
    tall = group * hid
    row = lax.broadcasted_iota(jnp.int32, (tall, hid), 0) & (hid - 1)
    up = jnp.where(row == lax.broadcasted_iota(jnp.int32, (tall, hid), 1), 1.0, 0.0).astype(BF)
    mixed = dot_t(dot(up, (0.5 * mix_w[...].astype(F32)).astype(BF)).astype(BF), up)
    shift = hid.bit_length() - 1
    rows2 = lax.broadcasted_iota(jnp.int32, (tall, tall), 0) >> shift
    cols2 = lax.broadcasted_iota(jnp.int32, (tall, tall), 1) >> shift
    w2[...] = jnp.where(rows2 == cols2, mixed, 0.0).astype(BF)
    variables = out_w.shape[0]
    wide = dot_t(out_w[...], up)
    y = lax.broadcasted_iota(jnp.int32, (group, tall), 0)
    here = y == lax.broadcasted_iota(jnp.int32, (group, tall), 1) >> shift
    w3[...] = jnp.concatenate(
        [jnp.where(here, jnp.broadcast_to(wide[v : v + 1], (group, tall)), 0.0) for v in range(variables)],
        axis=0,
    ).astype(BF)
    b3[...] = jnp.concatenate(
        [jnp.broadcast_to(out_b[:, v : v + 1], (group, 128)) for v in range(variables)], axis=0
    )
    mixed_bias = jnp.broadcast_to(0.5 * column(mix_b[...]), (hid, 128))
    b2[...] = jnp.concatenate([mixed_bias] * group, axis=0)


def model_kernel(
    p_bg, p_c, r_c, r_e, near, far, dnear, dfar, *rest,
    rows, frames, variables, tile_cols, n_sens, paired, i_of, parity_of,
):
    sens = None if paired else rest[0]
    first = 0 if paired else 1
    prior, p_own, p_coef, p_out, p_halo, p_chalo, p_ohalo = rest[first : first + 7]
    out, field_a, field_b, coefs = rest[first + 7 :]
    lon = p_bg.shape[1]
    half = lon // 2
    quarters = 8 // variables
    width = half // quarters
    me_l, count = lax.axis_index("lat"), lax.axis_size("lat")
    parity = parity_of()
    me_t = i_of()
    top_ok, bottom_ok = me_l > 0, me_l < count - 1
    tall = rows + 2 * HALO

    for t in range(frames):
        for h in range(2):
            g = t * 2 + h
            body, rim = [], []
            for q in range(quarters):
                cut = slice(h * half + q * width, h * half + (q + 1) * width)
                body.append(p_bg[t * variables * rows : (t + 1) * variables * rows, cut])
                rim += [near[:, cut], far[:, cut]]
            field_a[g, HALO : HALO + rows] = dot(p_own[...], jnp.concatenate(body, axis=0)).reshape(rows, 8, width)
            edges = dot(p_halo[t], jnp.concatenate(rim, axis=0)).reshape(2 * HALO, 8, width)
            field_a[g, 0:HALO] = edges[0:HALO]
            field_a[g, HALO + rows : tall] = edges[HALO:]

    ctall = rows + 2 * CROWS
    for source in range(2):
        big = p_c if source == 0 else r_c
        spot = me_t if source == 0 else 1 - me_t
        pieces = []
        for side in range(2):
            for c_row in range(2):
                stack = []
                for q in range(quarters):
                    cut = slice(side * half + q * width, side * half + (q + 1) * width)
                    stack.append(big[c_row * rows : (c_row + 1) * rows, cut])
                pieces.append(jnp.concatenate(stack, axis=0))
        scaled = p_coef[...]
        ha = (0.5 * dot(scaled, pieces[0])).reshape(rows, 8, width)
        hb = (0.5 * dot(scaled, pieces[1])).reshape(rows, 8, width)
        kk = dot(scaled, pieces[2]).reshape(rows, 8, width) + K_MID
        rim = []
        for q in range(quarters):
            for message in (near[16:32], far[16:32]) if source == 0 else (r_e,):
                for side in range(2):
                    cut = slice(side * half + q * width, side * half + (q + 1) * width)
                    rim.append(message[:, cut])
        edges = dot((p_ohalo if source else p_chalo)[...], jnp.concatenate(rim, axis=0))
        edges = edges.reshape(3, 2, CROWS, 8, width)
        k_top = edges[2, 0] + jnp.where(top_ok, K_MID, 0.0)
        k_bottom = edges[2, 1] + jnp.where(bottom_ok, K_MID, 0.0)
        for start, size, xa, xb, xk in (
            (0, CROWS, edges[0, 0], edges[1, 0], k_top),
            (CROWS, rows, ha, hb, kk),
            (CROWS + rows, CROWS, edges[0, 1], edges[1, 1], k_bottom),
        ):
            span = slice(start, start + size)
            coefs[spot, 0, span] = xk - xa
            coefs[spot, 1, span] = xk + xa
            coefs[spot, 2, span] = xk - xb
            coefs[spot, 3, span] = xk + xb
            coefs[spot, 4, span] = 1.0 - 4.0 * xk

    lane = lax.broadcasted_iota(jnp.int32, (8, 128), 1)
    sub_q = lax.broadcasted_iota(jnp.int32, (8, 128), 0) >> (variables.bit_length() - 1)
    first_lane, last_lane = lane == 0, lane == 127
    first_q, last_q = sub_q == 0, sub_q == quarters - 1
    tiles = width // 128

    def cut_tiles(x):
        return [x[:, n * 128 : (n + 1) * 128] for n in range(tiles)]

    def from_west(x0, x1):
        both = [[pltpu.roll(part, 1, 1) for part in cut_tiles(x)] for x in (x0, x1)]
        result = []
        for h in range(2):
            wrapped = jnp.where(last_q, both[1 - h][-1], both[h][-1])
            carry = pltpu.roll(wrapped, variables, 0)
            parts = []
            for n in range(tiles):
                parts.append(jnp.where(first_lane, carry if n == 0 else both[h][n - 1], both[h][n]))
            result.append(jnp.concatenate(parts, axis=1))
        return result

    def from_east(x0, x1):
        both = [[pltpu.roll(part, 127, 1) for part in cut_tiles(x)] for x in (x0, x1)]
        result = []
        for h in range(2):
            wrapped = jnp.where(first_q, both[1 - h][0], both[h][0])
            carry = pltpu.roll(wrapped, 8 - variables, 0)
            parts = []
            for n in range(tiles):
                parts.append(
                    jnp.where(last_lane, carry if n == tiles - 1 else both[h][n + 1], both[h][n])
                )
            result.append(jnp.concatenate(parts, axis=1))
        return result

    def forward(source, target, low, high):
        for r in range(low, high):
            cr = r - (HALO - CROWS)
            for t in range(frames):
                center = [source[t * 2 + h, r] for h in range(2)]
                west, east = from_west(*center), from_east(*center)
                for h in range(2):
                    g = t * 2 + h
                    target[g, r] = (
                        (coefs[h, 4, cr] * center[h] + coefs[h, 0, cr] * east[h])
                        + (coefs[h, 1, cr] * west[h] + coefs[h, 2, cr] * source[g, r + 1])
                        + coefs[h, 3, cr] * source[g, r - 1]
                    )

    def backward(source, target, low, high):
        for r in range(low, high):
            cr = r - (HALO - CROWS)
            for t in range(frames):
                center = [source[t * 2 + h, r] for h in range(2)]
                west = from_west(*[coefs[h, 0, cr] * center[h] for h in range(2)])
                east = from_east(*[coefs[h, 1, cr] * center[h] for h in range(2)])
                for h in range(2):
                    g = t * 2 + h
                    target[g, r] = (
                        (coefs[h, 4, cr] * center[h] + west[h])
                        + (east[h] + coefs[h, 2, cr - 1] * source[g, r - 1])
                        + coefs[h, 3, cr + 1] * source[g, r + 1]
                    )

    buffers = [field_a, field_b]
    for step in range(SUB):
        forward(buffers[step % 2], buffers[(step + 1) % 2], step + 1, tall - step - 1)
    forecast, spread = buffers[SUB % 2], buffers[(SUB + 1) % 2]

    def kinds(row, t):
        base = t * (2 + variables) * n_sens
        return [row[:, base + n * n_sens : base + (n + 1) * n_sens] for n in range(2 + variables)]

    def sensor_rows(h, band):
        if not paired:
            count = sens.shape[0] // 8
            first = (h * 4 + band) * count
            return [sens[...].astype(F32)[first + n : first + n + 1] for n in range(count)]
        if band in (1, 3):
            at = slice(rows, rows + 16)
            mine, other = p_c[at, half:lon].astype(F32), r_c[at, half:lon].astype(F32)
            n = 14 if band == 1 else 12
            return [jnp.where(me_t == h, mine[n : n + 1], other[n + 1 : n + 2])]
        from_far = parity == (0 if band == 0 else 1)
        pair = [m[16:32, half:lon].astype(F32)[15:16] for m in (near, far)]
        row = frames * variables
        pair += [m[:, 0:half].astype(F32)[row : row + 1] for m in (dnear, dfar)]
        found = [jnp.where(from_far, pair[n + 1], pair[n]) for n in (0, 2)]
        return [jnp.where(me_t == h, found[0], found[1])]

    row_bits = tile_cols.bit_length() - 1
    width_bits = width.bit_length() - 1

    def located(h, band, t):
        found = []
        for n, row in enumerate(sensor_rows(h, band)):
            high, low, *values = kinds(row, t)
            cell = (high * 256.0 + low).astype(jnp.int32)
            column = (cell & (tile_cols - 1)) + n * tile_cols
            found.append([cell >> row_bits, column >> width_bits, column & (width - 1)] + list(values))
        if band == 1:
            for n, row in enumerate(sensor_rows(h, 3)):
                for v in range(variables):
                    found[n][3 + v] = found[n][3 + v] + row[:, (t * variables + v) * n_sens : (t * variables + v + 1) * n_sens]
        return [jnp.concatenate([f[n] for f in found], axis=1) for n in range(3 + variables)]

    def assimilate(g, row_list, where_row, quarter, lane_of, values):
        total = where_row.shape[1]
        lanes_bf = lax.broadcasted_iota(jnp.int32, (width, total), 0).astype(F32).astype(BF)
        apart = jnp.abs(lanes_bf - lane_of.astype(F32).astype(BF))
        onehot = jnp.maximum(BF(1) - apart, BF(0))
        stack = jnp.concatenate([forecast[g, HALO + r] for r in row_list], axis=0)
        size = 8 * len(row_list)
        picked = dot(jnp.concatenate(split2(stack), axis=0), onehot)
        picked = picked[:size] + picked[size:]
        shape = (8, total)
        here_q = (lax.broadcasted_iota(jnp.int32, shape, 0) >> (variables.bit_length() - 1)) == quarter
        variable = lax.broadcasted_iota(jnp.int32, shape, 0) & (variables - 1)
        misfit = jnp.zeros(shape, F32)
        for n, r in enumerate(row_list):
            misfit = misfit + jnp.where(where_row == r, picked[n * 8 : (n + 1) * 8], 0.0)
        target = jnp.broadcast_to(values[0], shape)
        for v in range(1, variables):
            target = jnp.where(variable == v, values[v], target)
        misfit = jnp.where(here_q, misfit - target, 0.0)
        row_f = where_row.astype(F32)
        weighted = jnp.concatenate([jnp.where(row_f == float(r), misfit, 0.0) for r in row_list], axis=0)
        sums = dot_t(jnp.concatenate(split2(weighted), axis=0), onehot)
        return (sums[:size] + sums[size:]).reshape(len(row_list), 8, width)

    far_away = -(1 << 20)
    for t in range(frames):
        for h in range(2):
            g = t * 2 + h
            row, quarter, lane_of, *values = located(h, 1, t)
            spread[g, HALO : HALO + rows] = assimilate(g, list(range(rows)), row, quarter, lane_of, values)
            above, below = located(h, 0, t), located(h, 2, t)
            above[0] = jnp.where(top_ok, above[0] - rows, far_away)
            below[0] = jnp.where(bottom_ok, below[0] + rows, far_away)
            merged = [jnp.concatenate([x, y], axis=1) for x, y in zip(above, below)]
            rim_rows = list(range(-SUB, 0)) + list(range(rows, rows + SUB))
            rim = assimilate(g, rim_rows, merged[0], merged[1], merged[2], merged[3:])
            spread[g, HALO - SUB : HALO] = rim[0:SUB]
            spread[g, HALO + rows : HALO + rows + SUB] = rim[SUB:]

    buffers = [spread, forecast]
    for step in range(SUB):
        low = HALO - SUB + step + 1
        backward(buffers[step % 2], buffers[(step + 1) % 2], low, tall - low)
    result = buffers[SUB % 2]
    twice = jnp.concatenate([p_out[...], p_out[...]], axis=1)

    for t in range(frames):
        for h in range(2):
            parts = split2(result[t * 2 + h, HALO : HALO + rows].reshape(rows * 8, width))
            back = dot(twice, jnp.concatenate(parts, axis=0))
            for q in range(quarters):
                cut = slice(h * half + q * width, h * half + (q + 1) * width)
                for v in range(variables):
                    base = (q * variables + v) * rows
                    out[t, v, :, cut] = prior[t, v, :, cut] - back[base : base + rows]


def gelu(y):
    inner = y * (GELU_1 + GELU_2 * (y * y))
    return (y + y * jnp.tanh(inner)).astype(BF)


def shifted(chosen, window, depth):
    tall, lon = chosen.shape
    packed = chosen.astype(BF)
    window[0:tall] = pltpu.roll(packed, 1, 1)
    window[tall : 2 * tall] = packed
    window[2 * tall : 3 * tall] = pltpu.roll(packed, lon - 1, 1)
    ones = lax.broadcasted_iota(jnp.int32, (depth - 3 * tall, lon), 0) < 3
    window[3 * tall : depth] = jnp.where(ones, 1.0, 0.0).astype(BF)


def widen(column, chunk):
    return jnp.concatenate([column] * (chunk // 128), axis=1)


def conv_kernel(
    p_bg, r_bg, near, far, dnear, dfar, w1, w2, w3, b2, b3, select, out, window,
    *, frames, variables, group, chunk,
):
    groups, depth, lon = window.shape
    fields = jnp.concatenate([x[...] for x in (p_bg, r_bg, near, far, dnear, dfar)], axis=0)
    chosen = dot(select[...], fields)
    tall = chosen.shape[0] // groups
    for g in range(groups):
        shifted(chosen[g * tall : (g + 1) * tall], window.at[g], depth)
    hidden = w2.shape[0]
    bias2, bias3 = widen(b2[...], chunk), widen(b3[...], chunk)
    pending = []
    wide2 = jnp.concatenate([bias2] * frames, axis=1)
    for n in range(lon // chunk):
        cut = slice(n * chunk, (n + 1) * chunk)
        for g in range(groups):
            first = dot(w1[...], window[g, :, cut])
            one = [gelu(first[t * hidden : (t + 1) * hidden]) for t in range(frames)]
            pending.append((g, cut, gelu(dot(w2[...], jnp.concatenate(one, axis=1)) + wide2)))
    for g, cut, two in pending:
        scores = dot(w3[...], two)
        for t in range(frames):
            score = scores[:, t * chunk : (t + 1) * chunk] + bias3
            for v in range(variables):
                out[t, v, g * group : (g + 1) * group, cut] = score[v * group : (v + 1) * group]


def call(body, out_shape, scratch, *args, fetched=(), limit=VMEM_BYTES, cost=None):
    whole = pl.BlockSpec(memory_space=pltpu.VMEM)
    given = pl.BlockSpec(memory_space=pltpu.HBM)
    several = isinstance(out_shape, (list, tuple))
    if cost is not None:
        cost = pl.CostEstimate(flops=10**8, bytes_accessed=cost, transcendentals=0)
    return pl.pallas_call(
        body,
        out_shape=out_shape,
        in_specs=[given if n in fetched else whole for n in range(len(args))],
        out_specs=[whole] * len(out_shape) if several else whole,
        scratch_shapes=scratch,
        compiler_params=pltpu.CompilerParams(vmem_limit_bytes=limit),
        cost_estimate=cost,
    )(*args)


def struct(shape, dtype):
    return jax.ShapeDtypeStruct(shape, dtype)


def swap_pairs(tiles, bands):
    def at(t, j):
        return t * bands + j

    def far(j):
        return j + 1 if j % 2 else j - 1

    cells = [(t, j) for t in range(tiles) for j in range(bands)]
    inner = lambda j: 0 <= far(j) < bands
    return (
        [(at(t, j), at(1 - t, j)) for t, j in cells],
        [(at(t, j), at(t, j ^ 1)) for t, j in cells],
        [(at(t, j), at(t, far(j)) if inner(j) else at(1 - t, j)) for t, j in cells],
        [(at(t, j), at(1 - t, j ^ 1)) for t, j in cells],
        [(at(t, j), at(1 - t, far(j)) if inner(j) else at(1 - t, j)) for t, j in cells],
    )


def exchange_pairs(background, east, north, diff, sensors, observations):
    frames, variables, rows, lon = background.shape
    fields = frames * variables
    bands = lax.axis_size("lat")
    table = jnp.asarray(pack_table(rows, fields), BF)
    arrays = (background, east, north, diff, sensors, observations)
    lat_message, diagonal = struct((32, lon), BF), struct((8, lon), BF)
    with jax.named_scope("pack"):
        p_c, near, far, dnear, dfar = call(
            functools.partial(pack_kernel, frames=frames),
            [struct((2 * rows, lon), BF), lat_message, lat_message, diagonal, diagonal],
            [pltpu.VMEM(x.shape, x.dtype) for x in arrays]
            + [pltpu.VMEM(table.shape[1:], BF), pltpu.SemaphoreType.DMA((7,))],
            *arrays, table, fetched=range(7), limit=PACK_BYTES,
        )
    axes = ("tm", "lat")
    across, on_chip, next_chip, diag_near, diag_far = swap_pairs(lax.axis_size("tm"), bands)
    p_bg = background.reshape(fields * rows, lon)
    r_bg = lax.ppermute(p_bg, axes, across)
    r_dfar = lax.ppermute(dfar, axes, diag_far)
    r_far = lax.ppermute(far, axes, next_chip)
    r_dnear = lax.ppermute(dnear, axes, diag_near)
    r_near = lax.ppermute(near, axes, on_chip)
    return p_bg, r_bg, p_c, r_near, r_far, r_dnear, r_dfar


def exchange_gathered(background, east, north, diff, sensors, observations):
    frames, variables, rows, lon = background.shape
    fields = frames * variables
    half = lon // 2
    tiles, bands = lax.axis_size("tm"), lax.axis_size("lat")
    down = [(j, j + 1) for j in range(bands - 1)]
    up = [(j + 1, j) for j in range(bands - 1)]
    later = [(t, t + 1) for t in range(tiles - 1)]
    earlier = [(t + 1, t) for t in range(tiles - 1)]
    coefs = jnp.stack([east, north, diff - K_MID]).astype(BF)
    coefs = lax.all_gather(coefs, "tm", axis=2, tiled=True)
    around = jnp.concatenate(
        [lax.ppermute(background, "tm", later), lax.ppermute(background, "tm", earlier)], axis=0
    )
    cells = lax.all_to_all(sensors, "tm", split_axis=0, concat_axis=2, tiled=True)[:, 0]
    obs = lax.all_to_all(observations, "tm", split_axis=0, concat_axis=2, tiled=True)[:, 0]
    cells = jnp.moveaxis(cells, 1, 0)
    obs = jnp.transpose(obs, (1, 0, 2, 3))
    obs_high = obs.astype(BF).astype(F32)
    digits = jnp.stack([(cells >> 8).astype(F32), (cells & 255).astype(F32)], axis=2)
    described = jnp.concatenate([digits, obs_high], axis=2).reshape(tiles, -1).astype(BF)
    low = (obs - obs_high).astype(BF).reshape(tiles, -1)
    low = jnp.pad(low, ((0, 0), (0, described.shape[1] - low.shape[1])))
    bands_of = [
        lax.ppermute(described, "lat", down), described, lax.ppermute(described, "lat", up), low
    ]
    sens = jnp.stack([x.reshape(2, tiles // 2, -1) for x in bands_of], axis=1)
    sens = sens.reshape(-1, described.shape[1])

    def block(h):
        part = coefs[:, :, h * half : (h + 1) * half]
        blank = jnp.zeros_like(part[0])
        return jnp.concatenate(
            [jnp.concatenate([part[0], part[2]], axis=1), jnp.concatenate([part[1], blank], axis=1)],
            axis=0,
        )

    def edge_fields(fields_4d, depth, bottom):
        first = rows - depth if bottom else 0
        return fields_4d[:, :, first : first + depth].reshape(-1, lon)

    def edge_coefs(h, bottom):
        first = rows - CROWS if bottom else 0
        part = coefs[:, first : first + CROWS, h * half : (h + 1) * half]
        part = jnp.pad(part.reshape(3 * CROWS, half), ((0, 16 - 3 * CROWS), (0, 0)))
        return jnp.concatenate([part[:8], part[8:]], axis=1)

    received = []
    for bottom, pairs in ((False, up), (True, down)):
        message = [edge_fields(background, HALO, bottom), edge_coefs(0, bottom)]
        message = lax.ppermute(jnp.concatenate(message, axis=0), "lat", pairs)
        diagonal = lax.ppermute(edge_fields(around, 1, bottom), "lat", pairs)
        received.append((message, diagonal, lax.ppermute(edge_coefs(1, bottom), "lat", pairs)))
    (near, dnear, c_near), (far, dfar, c_far) = received
    r_e = jnp.concatenate([c_near, c_far], axis=0)
    p_bg, r_bg = background.reshape(-1, lon), around.reshape(-1, lon)
    return p_bg, r_bg, block(0), block(1), r_e, near, far, dnear, dfar, sens


def shards(
    background, conv_weight, conv_bias, mix_weight, mix_bias, out_weight, out_bias,
    drift_east, drift_north, diffusivity, sensors, observations,
):
    frames, variables, rows, lon = background.shape
    tiles, bands = lax.axis_size("tm"), lax.axis_size("lat")
    paired = tiles == 2 and bands % 2 == 0
    group = rows // 2
    hid = mix_weight.shape[0]
    fields = frames * variables
    arrays = (background, drift_east, drift_north, diffusivity, sensors, observations)
    if paired:
        p_bg, r_bg, p_c, near, far, dnear, dfar = exchange_pairs(*arrays)
        offsets = [[*range(2 * frames)], [*range(frames), *range(-frames, 0)]]
        i_of = lambda: lax.axis_index("tm")
        parity_of = lambda: lax.axis_index("lat") % 2
        sens = ()
    else:
        p_bg, r_bg, p_c, r_c, r_e, near, far, dnear, dfar, sens = exchange_gathered(*arrays)
        offsets = [[*range(frames), *range(-frames, 0), *range(frames, 2 * frames)]]
        i_of = lambda: 0
        parity_of = lambda: 0
        sens = (sens,)
    others = len(offsets[0]) - frames

    channels = (frames + others) * variables
    depth = -(-(3 * round16((group + 2) * channels) + 3) // 128) * 128
    quarters = 8 // variables
    width = lon // 8
    taps = jnp.asarray(np.stack([tap_table(o, frames, variables, group, depth) for o in offsets]))
    own, coef, back, halo, chalo, ohalo = model_tables(rows, frames, variables, quarters)
    gather = conv_table(rows, frames, others, variables, group)
    index = np.stack(
        [index_rows([gather[c], *halo[c], chalo[c], own, coef, back, ohalo[c]], 256) for c in range(5)]
    )
    tables = [gather[0], own, coef, back, halo[0], chalo[0], ohalo[0]]
    small = [conv_weight, conv_bias.reshape(1, -1), mix_weight, mix_bias.reshape(1, -1)]
    small += [out_weight, out_bias.reshape(1, -1)]
    with jax.named_scope("weights"):
        weights = call(
            functools.partial(
                prep_kernel, group=group, channels=channels, i_of=i_of, parity_of=parity_of
            ),
            [
                struct((frames * group * hid, depth), BF),
                struct((group * hid, group * hid), BF),
                struct((variables * group, group * hid), BF),
                struct((group * hid, 128), F32),
                struct((variables * group, 128), F32),
            ]
            + [struct(x.shape, BF) for x in tables],
            [pltpu.VMEM(x.shape, x.dtype) for x in small]
            + [pltpu.VMEM(taps.shape[1:], jnp.int32), pltpu.VMEM(index.shape[1:], jnp.int32)]
            + [pltpu.SemaphoreType.DMA((8,))],
            *small, taps, jnp.asarray(index), fetched=range(8),
        )
    if paired:
        far, near, r_bg, *weights = lax.optimization_barrier((far, near, r_bg, *weights))
        with jax.named_scope("relay"):
            edges = call(relay_kernel, struct((16, lon), BF), [], far, near)
        pairs = swap_pairs(tiles, bands)[0]
        dfar, dnear, late, edges = lax.optimization_barrier((dfar, dnear, p_c, edges))
        r_c = lax.ppermute(late, ("tm", "lat"), pairs)
        r_e = lax.ppermute(edges, ("tm", "lat"), pairs)
    *w_conv, p_conv = weights[:6]
    p_model = weights[6:]
    with jax.named_scope("prior"):
        prior = call(
            functools.partial(
                conv_kernel, frames=frames, variables=variables, group=group, chunk=256
            ),
            struct(background.shape, F32),
            [pltpu.VMEM((rows // group, depth, lon), BF)],
            p_bg, r_bg, near, far, dnear, dfar, *w_conv, p_conv,
            cost=COST,
        )
    tall, ctall = rows + 2 * HALO, rows + 2 * CROWS
    with jax.named_scope("model"):
        return call(
            functools.partial(
                model_kernel, rows=rows, frames=frames, variables=variables,
                tile_cols=drift_east.shape[1], n_sens=sensors.shape[3],
                paired=paired, i_of=i_of, parity_of=parity_of,
            ),
            struct(background.shape, F32),
            [
                pltpu.VMEM((2 * frames, tall, 8, width), F32),
                pltpu.VMEM((2 * frames, tall, 8, width), F32),
                pltpu.VMEM((2, 5, ctall, 8, width), F32),
            ],
            p_bg, p_c, r_c, r_e, near, far, dnear, dfar, *sens, prior, *p_model,
        )


def solution(mesh):
    placed = (
        P("tm", None, "lat", None),
        P(),
        P(),
        P(),
        P(),
        P(),
        P(),
        P("lat", "tm"),
        P("lat", "tm"),
        P("lat", "tm"),
        P(None, "lat", "tm", None),
        P(None, "lat", "tm", None, None),
    )
    return jax.shard_map(
        shards, mesh=mesh, in_specs=placed, out_specs=P("tm", None, "lat", None), check_vma=False
    )
```

```python
import functools

import jax
import jax.numpy as jnp
import numpy as np
from jax import lax
from jax.experimental import pallas as pl
from jax.experimental.pallas import tpu as pltpu
from jax.sharding import PartitionSpec as P

KT = 5
SUB = 3
K_MID = 0.17
HALO = 2 * SUB
CROWS = 2 * SUB - 1
BF = jnp.bfloat16
F32 = jnp.float32
VMEM_BYTES = 48 * 1024 * 1024
COST = 60 * 10**6
PACK_BYTES = 64 * 1024 * 1024 - 1024 * 1024
GELU_1 = 2.0 * float(np.sqrt(2.0 / np.pi))
GELU_2 = 8.0 * 0.044715 * float(np.sqrt(2.0 / np.pi))


def dot(a, b):
    return jnp.dot(a, b, preferred_element_type=F32)


def dot_t(a, b):
    return lax.dot_general(a, b, (((1,), (1,)), ((), ())), preferred_element_type=F32)


def split2(x):
    high = x.astype(BF)
    return high, (x - high.astype(F32)).astype(BF)


def fetch(pairs, sems):
    copies = [pltpu.make_async_copy(source, target, sems.at[n]) for n, (source, target) in enumerate(pairs)]
    for copy in copies:
        copy.start()
    for copy in copies:
        copy.wait()


def pack_table(rows, fields):
    table = np.zeros((2, 2, 80, 128), np.float32)
    coef_row = fields * rows
    for parity in range(2):
        for side in range(2):
            for message in range(4):
                far, diagonal = message % 2, message // 2
                bottom = (far == 0) == (parity == 0)
                out = table[parity, side]
                if diagonal:
                    base = 64 + 8 * far
                    for field in range(fields):
                        out[base + field, field * rows + (rows - 1 if bottom else 0)] = 1
                    if side == 0:
                        out[base + fields, coef_row + 3 * rows + 15] = 1
                    continue
                base = 32 * far
                for field in range(fields):
                    for e in range(HALO):
                        row = rows - HALO + e if bottom else e
                        out[base + field * HALO + e, field * rows + row] = 1
                for slot in range(8):
                    j = side * 8 + slot
                    target = base + 24 + slot
                    if j < 3 * CROWS:
                        c, e = divmod(j, CROWS)
                        row = rows - CROWS + e if bottom else e
                        out[target, coef_row + c * rows + row] = 1
                    else:
                        out[target, coef_row + 3 * rows + 14] = 1
    return table


def near_far(case):
    parity = case in (1, 3)
    top_ok = case != 2
    bottom_ok = case not in (3, 4)
    top_slot = 0 if parity else 1
    return top_slot, 1 - top_slot, top_ok, bottom_ok


def model_tables(rows, frames, variables, quarters):
    lanes = quarters * variables
    own = np.zeros((rows * lanes, quarters * variables * rows), np.float32)
    coef = np.zeros((rows * lanes, quarters * rows), np.float32)
    out = np.zeros((lanes * rows, rows * lanes), np.float32)
    for r in range(rows):
        for q in range(quarters):
            for v in range(variables):
                own[r * lanes + q * variables + v, (q * variables + v) * rows + r] = 1
                coef[r * lanes + q * variables + v, q * rows + r] = 1
                out[(q * variables + v) * rows + r, r * lanes + q * variables + v] = 1
    halo = np.zeros((5, frames, 2 * HALO * lanes, quarters * 64), np.float32)
    chalo = np.zeros((5, 3 * 2 * CROWS * lanes, quarters * 64), np.float32)
    ohalo = np.zeros((5, 3 * 2 * CROWS * lanes, quarters * 32), np.float32)
    for case in range(5):
        top_slot, bottom_slot, top_ok, bottom_ok = near_far(case)
        for q in range(quarters):
            for v in range(variables):
                lane = q * variables + v
                for half, slot, ok in ((0, top_slot, top_ok), (1, bottom_slot, bottom_ok)):
                    if not ok:
                        continue
                    for t in range(frames):
                        for e in range(HALO):
                            local = (t * variables + v) * HALO + e
                            halo[case, t, (half * HALO + e) * lanes + lane, q * 64 + slot * 32 + local] = 1
                    for c in range(3):
                        for e in range(CROWS):
                            j = c * CROWS + e
                            column = q * 64 + slot * 32 + (j // 8) * 16 + 8 + j % 8
                            row = ((c * 2 + half) * CROWS + e) * lanes + lane
                            chalo[case, row, column] = 1
                            column = q * 32 + (j // 8) * 16 + slot * 8 + j % 8
                            ohalo[case, row, column] = 1
    return own, coef, out, halo, chalo, ohalo


def round16(n):
    return -(-n // 16) * 16


def conv_table(rows, frames, others, variables, group):
    channels = (frames + others) * variables
    tall = round16((group + 2) * channels)
    own_rows = frames * variables * rows
    oth_rows = others * variables * rows
    table = np.zeros((5, rows // group * tall, own_rows + oth_rows + 80), np.float32)
    for case in range(5):
        top_slot, bottom_slot, top_ok, bottom_ok = near_far(case)
        for g in range(rows // group):
            for yy in range(group + 2):
                y = g * group + yy - 1
                for f in range(frames + others):
                    for v in range(variables):
                        target = g * tall + yy * channels + f * variables + v
                        own = f < frames
                        field = (f if own else f - frames) * variables + v
                        if 0 <= y < rows:
                            table[case, target, (0 if own else own_rows) + field * rows + y] = 1
                            continue
                        slot, ok = (top_slot, top_ok) if y < 0 else (bottom_slot, bottom_ok)
                        if not ok:
                            continue
                        column = own_rows + oth_rows
                        if own:
                            column += slot * 32 + field * HALO + (HALO - 1 if y < 0 else 0)
                        else:
                            column += 64 + slot * 8 + field
                        table[case, target, column] = 1
    return table


def tap_table(offsets, frames, variables, group, depth):
    channels = len(offsets) * variables
    tall = round16((group + 2) * channels)
    table = np.full((8, depth), -1, np.int32)
    for t in range(frames):
        for s in range(3):
            for i in range(3):
                for f, offset in enumerate(offsets):
                    lag = offset - t + KT // 2
                    for v in range(variables):
                        if 0 <= lag < KT:
                            k = s * tall + i * channels + f * variables + v
                            table[t, k] = ((v * KT + lag) * 3 + i) * 3 + s
    table[frames, 3 * tall : 3 * tall + 3] = 3 * 3 * KT * variables + np.arange(3)
    return table


def index_rows(tables, lanes):
    out = np.full((8, lanes), -1, np.int32)
    for n, table in enumerate(tables):
        out[n, : table.shape[0]] = np.where(table.any(1), table.argmax(1), -1)
    return out


def case_of(parity, index, count):
    return jnp.where(index == 0, 2, jnp.where(index == count - 1, jnp.where(parity == 1, 3, 4), parity))


def pack_kernel(
    bg_in, east_in, north_in, diff_in, sensors_in, obs_in, table_in, p_c, near, far, dnear, dfar,
    bg, east, north, diff, sensors, obs, table, sems, *, frames,
):
    me_t = lax.axis_index("tm")
    parity = lax.axis_index("lat") % 2
    fetch(
        [
            (bg_in, bg), (east_in, east), (north_in, north), (diff_in, diff),
            (sensors_in, sensors), (obs_in, obs), (table_in.at[parity], table),
        ],
        sems,
    )
    fields = bg.shape[0] * bg.shape[1]
    rows, lon = bg.shape[2], bg.shape[3]
    half = lon // 2
    fields_2d = bg[...].reshape(fields * rows, lon)
    a, b = east[...].astype(BF), north[...].astype(BF)
    k = (diff[...] - K_MID).astype(BF)

    def described(first, low):
        pieces = []
        for t in range(frames):
            cells = sensors[first + t, 0]
            if not low:
                pieces += [(cells >> 8).astype(F32), (cells & 255).astype(F32)]
            for v in range(obs.shape[3]):
                value = obs[first + t, 0, 0, v : v + 1]
                high = value.astype(BF).astype(F32)
                pieces.append(value - high if low else high)
        row = jnp.concatenate(pieces, axis=1)
        if row.shape[1] < half:
            row = jnp.concatenate([row, jnp.zeros((1, half - row.shape[1]), F32)], axis=1)
        return row

    mine, theirs = me_t * frames, (1 - me_t) * frames
    extra = jnp.concatenate(
        [
            jnp.zeros((12, half), F32),
            described(mine, True),
            described(theirs, True),
            described(mine, False),
            described(theirs, False),
        ],
        axis=0,
    ).astype(BF)
    p_c[0:rows, 0:half] = a
    p_c[rows : 2 * rows, 0:half] = b
    p_c[0:rows, half:lon] = k
    p_c[rows : 2 * rows, half:lon] = extra
    for side in range(2):
        cut = slice(side * half, (side + 1) * half)
        source = jnp.concatenate([fields_2d[:, cut], a, b, k, extra], axis=0)
        message = dot(table[side], source).astype(BF)
        near[:, cut] = message[0:32]
        far[:, cut] = message[32:64]
        dnear[:, cut] = message[64:72]
        dfar[:, cut] = message[72:80]


def hold_kernel(source, out):
    out[...] = source[...]


def relay_kernel(far, near, p_c, out):
    own, edge = p_c.shape[0], near.shape[0] - 8
    out[0:own, :] = p_c[...]
    out[own : own + 8, :] = near[edge : edge + 8, :]
    out[own + 8 : own + 16, :] = far[edge : edge + 8, :]


def prep_kernel(*refs, group, channels, i_of, parity_of):
    sources, rest = refs[:8], refs[8:]
    w1, w2, w3, b2, b3, p_conv, p_own, p_coef, p_out, p_halo, p_chalo, p_ohalo = rest[:12]
    conv_w, conv_b, mix_w, mix_b, out_w, out_b, taps, index, sems = rest[12:]
    hid = mix_w.shape[0]
    case = case_of(parity_of(), lax.axis_index("lat"), lax.axis_size("lat"))
    moves = [*zip(sources[:6], (conv_w, conv_b, mix_w, mix_b, out_w, out_b))]
    moves += [(sources[6].at[i_of()], taps), (sources[7].at[case], index)]
    fetch(moves, sems)
    columns = index[...].astype(F32).T

    def select(n, shape):
        lanes = lax.broadcasted_iota(jnp.int32, shape, 1).astype(F32)
        return jnp.where(lanes == columns[0 : shape[0], n : n + 1], 1.0, 0.0)

    frames = p_halo.shape[0]
    p_conv[...] = select(0, p_conv.shape).astype(BF)
    for t in range(frames):
        p_halo[t] = select(1 + t, p_halo.shape[1:]).astype(BF)
    for n, target in ((1 + frames, p_chalo), (5 + frames, p_ohalo)):
        halved = lax.broadcasted_iota(jnp.int32, target.shape, 0) < target.shape[0] // 3 * 2
        target[...] = (select(n, target.shape) * jnp.where(halved, 0.5, 1.0)).astype(BF)
    p_own[...] = select(2 + frames, p_own.shape).astype(BF)
    p_coef[...] = select(3 + frames, p_coef.shape).astype(BF)
    p_out[...] = select(4 + frames, p_out.shape).astype(BF)
    table = taps[...]

    def column(row):
        n = row.shape[1]
        here = lax.broadcasted_iota(jnp.int32, (n, n), 0) == lax.broadcasted_iota(jnp.int32, (n, n), 1)
        return jnp.sum(jnp.where(here, jnp.broadcast_to(row, (n, n)), 0.0), axis=1, keepdims=True)

    bias = 0.5 * column(conv_b[...])
    pieces = []
    for _ in range(3):
        piece = bias.astype(BF)
        bias = bias - piece.astype(F32)
        pieces.append(piece.astype(F32))
    ntap = conv_w.shape[1]
    padded = 128
    weights = jnp.concatenate(
        [0.5 * conv_w[...].astype(F32)] + pieces + [jnp.zeros((hid, padded - ntap - 3), F32)], axis=1
    ).astype(BF)
    tap_id = lax.broadcasted_iota(jnp.int32, (padded, table.shape[1]), 0)

    def chosen(n):
        return dot(weights, jnp.where(tap_id == table[n : n + 1, :], 1.0, 0.0).astype(BF))

    biased = chosen(frames)
    for t in range(frames):
        first = chosen(t)
        for y in range(group):
            start = (t * group + y) * hid
            moved = pltpu.roll(first, y * channels, 1) if y else first
            w1[start : start + hid, :] = (moved + biased).astype(BF)
    tall = group * hid
    row = lax.broadcasted_iota(jnp.int32, (tall, hid), 0) & (hid - 1)
    up = jnp.where(row == lax.broadcasted_iota(jnp.int32, (tall, hid), 1), 1.0, 0.0).astype(BF)
    mixed = dot_t(dot(up, (0.5 * mix_w[...].astype(F32)).astype(BF)).astype(BF), up)
    shift = hid.bit_length() - 1
    rows2 = lax.broadcasted_iota(jnp.int32, (tall, tall), 0) >> shift
    cols2 = lax.broadcasted_iota(jnp.int32, (tall, tall), 1) >> shift
    w2[...] = jnp.where(rows2 == cols2, mixed, 0.0).astype(BF)
    variables = out_w.shape[0]
    wide = dot_t(out_w[...], up)
    y = lax.broadcasted_iota(jnp.int32, (group, tall), 0)
    here = y == lax.broadcasted_iota(jnp.int32, (group, tall), 1) >> shift
    w3[...] = jnp.concatenate(
        [jnp.where(here, jnp.broadcast_to(wide[v : v + 1], (group, tall)), 0.0) for v in range(variables)],
        axis=0,
    ).astype(BF)
    b3[...] = jnp.concatenate(
        [jnp.broadcast_to(out_b[:, v : v + 1], (group, 128)) for v in range(variables)], axis=0
    )
    mixed_bias = jnp.broadcast_to(0.5 * column(mix_b[...]), (hid, 128))
    b2[...] = jnp.concatenate([mixed_bias] * group, axis=0)


def model_kernel(
    p_bg, p_c, r_c, near, far, dnear, dfar, *rest,
    rows, frames, variables, tile_cols, n_sens, paired, i_of, parity_of,
):
    sens = None if paired else rest[0]
    first = 0 if paired else 1
    prior, p_own, p_coef, p_out, p_halo, p_chalo, p_ohalo = rest[first : first + 7]
    out, field_a, field_b, coefs = rest[first + 7 :]
    lon = p_bg.shape[1]
    half = lon // 2
    quarters = 8 // variables
    width = half // quarters
    me_l, count = lax.axis_index("lat"), lax.axis_size("lat")
    parity = parity_of()
    me_t = i_of()
    top_ok, bottom_ok = me_l > 0, me_l < count - 1
    tall = rows + 2 * HALO

    for t in range(frames):
        for h in range(2):
            g = t * 2 + h
            body, rim = [], []
            for q in range(quarters):
                cut = slice(h * half + q * width, h * half + (q + 1) * width)
                body.append(p_bg[t * variables * rows : (t + 1) * variables * rows, cut])
                rim += [near[:, cut], far[:, cut]]
            field_a[g, HALO : HALO + rows] = dot(p_own[...], jnp.concatenate(body, axis=0)).reshape(rows, 8, width)
            edges = dot(p_halo[t], jnp.concatenate(rim, axis=0)).reshape(2 * HALO, 8, width)
            field_a[g, 0:HALO] = edges[0:HALO]
            field_a[g, HALO + rows : tall] = edges[HALO:]

    ctall = rows + 2 * CROWS
    for source in range(2):
        big = p_c if source == 0 else r_c
        spot = me_t if source == 0 else 1 - me_t
        pieces = []
        for side in range(2):
            for c_row in range(2):
                stack = []
                for q in range(quarters):
                    cut = slice(side * half + q * width, side * half + (q + 1) * width)
                    stack.append(big[c_row * rows : (c_row + 1) * rows, cut])
                pieces.append(jnp.concatenate(stack, axis=0))
        scaled = p_coef[...]
        ha = (0.5 * dot(scaled, pieces[0])).reshape(rows, 8, width)
        hb = (0.5 * dot(scaled, pieces[1])).reshape(rows, 8, width)
        kk = dot(scaled, pieces[2]).reshape(rows, 8, width) + K_MID
        rim = []
        for q in range(quarters):
            for message in (near[16:32], far[16:32]) if source == 0 else (r_c[2 * rows : 2 * rows + 16],):
                for side in range(2):
                    cut = slice(side * half + q * width, side * half + (q + 1) * width)
                    rim.append(message[:, cut])
        edges = dot((p_ohalo if source else p_chalo)[...], jnp.concatenate(rim, axis=0))
        edges = edges.reshape(3, 2, CROWS, 8, width)
        k_top = edges[2, 0] + jnp.where(top_ok, K_MID, 0.0)
        k_bottom = edges[2, 1] + jnp.where(bottom_ok, K_MID, 0.0)
        for start, size, xa, xb, xk in (
            (0, CROWS, edges[0, 0], edges[1, 0], k_top),
            (CROWS, rows, ha, hb, kk),
            (CROWS + rows, CROWS, edges[0, 1], edges[1, 1], k_bottom),
        ):
            span = slice(start, start + size)
            coefs[spot, 0, span] = xk - xa
            coefs[spot, 1, span] = xk + xa
            coefs[spot, 2, span] = xk - xb
            coefs[spot, 3, span] = xk + xb
            coefs[spot, 4, span] = 1.0 - 4.0 * xk

    lane = lax.broadcasted_iota(jnp.int32, (8, 128), 1)
    sub_q = lax.broadcasted_iota(jnp.int32, (8, 128), 0) >> (variables.bit_length() - 1)
    first_lane, last_lane = lane == 0, lane == 127
    first_q, last_q = sub_q == 0, sub_q == quarters - 1
    tiles = width // 128

    def cut_tiles(x):
        return [x[:, n * 128 : (n + 1) * 128] for n in range(tiles)]

    def from_west(x0, x1):
        both = [[pltpu.roll(part, 1, 1) for part in cut_tiles(x)] for x in (x0, x1)]
        result = []
        for h in range(2):
            wrapped = jnp.where(last_q, both[1 - h][-1], both[h][-1])
            carry = pltpu.roll(wrapped, variables, 0)
            parts = []
            for n in range(tiles):
                parts.append(jnp.where(first_lane, carry if n == 0 else both[h][n - 1], both[h][n]))
            result.append(jnp.concatenate(parts, axis=1))
        return result

    def from_east(x0, x1):
        both = [[pltpu.roll(part, 127, 1) for part in cut_tiles(x)] for x in (x0, x1)]
        result = []
        for h in range(2):
            wrapped = jnp.where(first_q, both[1 - h][0], both[h][0])
            carry = pltpu.roll(wrapped, 8 - variables, 0)
            parts = []
            for n in range(tiles):
                parts.append(
                    jnp.where(last_lane, carry if n == tiles - 1 else both[h][n + 1], both[h][n])
                )
            result.append(jnp.concatenate(parts, axis=1))
        return result

    def forward(source, target, low, high):
        for r in range(low, high):
            cr = r - (HALO - CROWS)
            for t in range(frames):
                center = [source[t * 2 + h, r] for h in range(2)]
                west, east = from_west(*center), from_east(*center)
                for h in range(2):
                    g = t * 2 + h
                    target[g, r] = (
                        (coefs[h, 4, cr] * center[h] + coefs[h, 0, cr] * east[h])
                        + (coefs[h, 1, cr] * west[h] + coefs[h, 2, cr] * source[g, r + 1])
                        + coefs[h, 3, cr] * source[g, r - 1]
                    )

    def backward(source, target, low, high):
        for r in range(low, high):
            cr = r - (HALO - CROWS)
            for t in range(frames):
                center = [source[t * 2 + h, r] for h in range(2)]
                west = from_west(*[coefs[h, 0, cr] * center[h] for h in range(2)])
                east = from_east(*[coefs[h, 1, cr] * center[h] for h in range(2)])
                for h in range(2):
                    g = t * 2 + h
                    target[g, r] = (
                        (coefs[h, 4, cr] * center[h] + west[h])
                        + (east[h] + coefs[h, 2, cr - 1] * source[g, r - 1])
                        + coefs[h, 3, cr + 1] * source[g, r + 1]
                    )

    buffers = [field_a, field_b]
    for step in range(SUB):
        forward(buffers[step % 2], buffers[(step + 1) % 2], step + 1, tall - step - 1)
    forecast, spread = buffers[SUB % 2], buffers[(SUB + 1) % 2]

    def kinds(row, t):
        base = t * (2 + variables) * n_sens
        return [row[:, base + n * n_sens : base + (n + 1) * n_sens] for n in range(2 + variables)]

    def sensor_rows(h, band):
        if not paired:
            count = sens.shape[0] // 8
            first = (h * 4 + band) * count
            return [sens[...].astype(F32)[first + n : first + n + 1] for n in range(count)]
        if band in (1, 3):
            at = slice(rows, rows + 16)
            mine, other = p_c[at, half:lon].astype(F32), r_c[at, half:lon].astype(F32)
            n = 14 if band == 1 else 12
            return [jnp.where(me_t == h, mine[n : n + 1], other[n + 1 : n + 2])]
        from_far = parity == (0 if band == 0 else 1)
        pair = [m[16:32, half:lon].astype(F32)[15:16] for m in (near, far)]
        row = frames * variables
        pair += [m[:, 0:half].astype(F32)[row : row + 1] for m in (dnear, dfar)]
        found = [jnp.where(from_far, pair[n + 1], pair[n]) for n in (0, 2)]
        return [jnp.where(me_t == h, found[0], found[1])]

    row_bits = tile_cols.bit_length() - 1
    width_bits = width.bit_length() - 1

    def located(h, band, t):
        found = []
        for n, row in enumerate(sensor_rows(h, band)):
            high, low, *values = kinds(row, t)
            cell = (high * 256.0 + low).astype(jnp.int32)
            column = (cell & (tile_cols - 1)) + n * tile_cols
            found.append([cell >> row_bits, column >> width_bits, column & (width - 1)] + list(values))
        if band == 1:
            for n, row in enumerate(sensor_rows(h, 3)):
                for v in range(variables):
                    found[n][3 + v] = found[n][3 + v] + row[:, (t * variables + v) * n_sens : (t * variables + v + 1) * n_sens]
        return [jnp.concatenate([f[n] for f in found], axis=1) for n in range(3 + variables)]

    def assimilate(g, row_list, where_row, quarter, lane_of, values):
        total = where_row.shape[1]
        lanes_bf = lax.broadcasted_iota(jnp.int32, (width, total), 0).astype(F32).astype(BF)
        apart = jnp.abs(lanes_bf - lane_of.astype(F32).astype(BF))
        onehot = jnp.maximum(BF(1) - apart, BF(0))
        stack = jnp.concatenate([forecast[g, HALO + r] for r in row_list], axis=0)
        size = 8 * len(row_list)
        picked = dot(jnp.concatenate(split2(stack), axis=0), onehot)
        picked = picked[:size] + picked[size:]
        shape = (8, total)
        here_q = (lax.broadcasted_iota(jnp.int32, shape, 0) >> (variables.bit_length() - 1)) == quarter
        variable = lax.broadcasted_iota(jnp.int32, shape, 0) & (variables - 1)
        misfit = jnp.zeros(shape, F32)
        for n, r in enumerate(row_list):
            misfit = misfit + jnp.where(where_row == r, picked[n * 8 : (n + 1) * 8], 0.0)
        target = jnp.broadcast_to(values[0], shape)
        for v in range(1, variables):
            target = jnp.where(variable == v, values[v], target)
        misfit = jnp.where(here_q, misfit - target, 0.0)
        row_f = where_row.astype(F32)
        weighted = jnp.concatenate([jnp.where(row_f == float(r), misfit, 0.0) for r in row_list], axis=0)
        sums = dot_t(jnp.concatenate(split2(weighted), axis=0), onehot)
        return (sums[:size] + sums[size:]).reshape(len(row_list), 8, width)

    far_away = -(1 << 20)
    for t in range(frames):
        for h in range(2):
            g = t * 2 + h
            row, quarter, lane_of, *values = located(h, 1, t)
            spread[g, HALO : HALO + rows] = assimilate(g, list(range(rows)), row, quarter, lane_of, values)
            above, below = located(h, 0, t), located(h, 2, t)
            above[0] = jnp.where(top_ok, above[0] - rows, far_away)
            below[0] = jnp.where(bottom_ok, below[0] + rows, far_away)
            merged = [jnp.concatenate([x, y], axis=1) for x, y in zip(above, below)]
            rim_rows = list(range(-SUB, 0)) + list(range(rows, rows + SUB))
            rim = assimilate(g, rim_rows, merged[0], merged[1], merged[2], merged[3:])
            spread[g, HALO - SUB : HALO] = rim[0:SUB]
            spread[g, HALO + rows : HALO + rows + SUB] = rim[SUB:]

    buffers = [spread, forecast]
    for step in range(SUB):
        low = HALO - SUB + step + 1
        backward(buffers[step % 2], buffers[(step + 1) % 2], low, tall - low)
    result = buffers[SUB % 2]
    twice = jnp.concatenate([p_out[...], p_out[...]], axis=1)

    for t in range(frames):
        for h in range(2):
            parts = split2(result[t * 2 + h, HALO : HALO + rows].reshape(rows * 8, width))
            back = dot(twice, jnp.concatenate(parts, axis=0))
            for q in range(quarters):
                cut = slice(h * half + q * width, h * half + (q + 1) * width)
                for v in range(variables):
                    base = (q * variables + v) * rows
                    out[t, v, :, cut] = prior[t, v, :, cut] - back[base : base + rows]


def gelu(y):
    inner = y * (GELU_1 + GELU_2 * (y * y))
    return (y + y * jnp.tanh(inner)).astype(BF)


def shifted(chosen, window, depth):
    tall, lon = chosen.shape
    packed = chosen.astype(BF)
    window[0:tall] = pltpu.roll(packed, 1, 1)
    window[tall : 2 * tall] = packed
    window[2 * tall : 3 * tall] = pltpu.roll(packed, lon - 1, 1)
    ones = lax.broadcasted_iota(jnp.int32, (depth - 3 * tall, lon), 0) < 3
    window[3 * tall : depth] = jnp.where(ones, 1.0, 0.0).astype(BF)


def widen(column, chunk):
    return jnp.concatenate([column] * (chunk // 128), axis=1)


def conv_kernel(
    p_bg, r_bg, near, far, dnear, dfar, w1, w2, w3, b2, b3, select, out, window,
    *, frames, variables, group, chunk,
):
    groups, depth, lon = window.shape
    fields = jnp.concatenate([x[...] for x in (p_bg, r_bg, near, far, dnear, dfar)], axis=0)
    chosen = dot(select[...], fields)
    tall = chosen.shape[0] // groups
    for g in range(groups):
        shifted(chosen[g * tall : (g + 1) * tall], window.at[g], depth)
    hidden = w2.shape[0]
    bias2, bias3 = widen(b2[...], chunk), widen(b3[...], chunk)
    pending = []
    wide2 = jnp.concatenate([bias2] * frames, axis=1)
    for n in range(lon // chunk):
        cut = slice(n * chunk, (n + 1) * chunk)
        for g in range(groups):
            first = dot(w1[...], window[g, :, cut])
            one = [gelu(first[t * hidden : (t + 1) * hidden]) for t in range(frames)]
            pending.append((g, cut, gelu(dot(w2[...], jnp.concatenate(one, axis=1)) + wide2)))
    for g, cut, two in pending:
        scores = dot(w3[...], two)
        for t in range(frames):
            score = scores[:, t * chunk : (t + 1) * chunk] + bias3
            for v in range(variables):
                out[t, v, g * group : (g + 1) * group, cut] = score[v * group : (v + 1) * group]


def call(body, out_shape, scratch, *args, fetched=(), limit=VMEM_BYTES, cost=None):
    whole = pl.BlockSpec(memory_space=pltpu.VMEM)
    given = pl.BlockSpec(memory_space=pltpu.HBM)
    several = isinstance(out_shape, (list, tuple))
    if cost is not None:
        cost = pl.CostEstimate(flops=10**8, bytes_accessed=cost, transcendentals=0)
    return pl.pallas_call(
        body,
        out_shape=out_shape,
        in_specs=[given if n in fetched else whole for n in range(len(args))],
        out_specs=[whole] * len(out_shape) if several else whole,
        scratch_shapes=scratch,
        compiler_params=pltpu.CompilerParams(vmem_limit_bytes=limit),
        cost_estimate=cost,
    )(*args)


def struct(shape, dtype):
    return jax.ShapeDtypeStruct(shape, dtype)


def swap_pairs(tiles, bands):
    def at(t, j):
        return t * bands + j

    def far(j):
        return j + 1 if j % 2 else j - 1

    cells = [(t, j) for t in range(tiles) for j in range(bands)]
    inner = lambda j: 0 <= far(j) < bands
    return (
        [(at(t, j), at(1 - t, j)) for t, j in cells],
        [(at(t, j), at(t, j ^ 1)) for t, j in cells],
        [(at(t, j), at(t, far(j)) if inner(j) else at(1 - t, j)) for t, j in cells],
        [(at(t, j), at(1 - t, j ^ 1)) for t, j in cells],
        [(at(t, j), at(1 - t, far(j)) if inner(j) else at(1 - t, j)) for t, j in cells],
    )


def exchange_pairs(background, east, north, diff, sensors, observations):
    frames, variables, rows, lon = background.shape
    fields = frames * variables
    bands = lax.axis_size("lat")
    table = jnp.asarray(pack_table(rows, fields), BF)
    arrays = (background, east, north, diff, sensors, observations)
    lat_message, diagonal = struct((32, lon), BF), struct((8, lon), BF)
    with jax.named_scope("pack"):
        p_c, near, far, dnear, dfar = call(
            functools.partial(pack_kernel, frames=frames),
            [struct((2 * rows, lon), BF), lat_message, lat_message, diagonal, diagonal],
            [pltpu.VMEM(x.shape, x.dtype) for x in arrays]
            + [pltpu.VMEM(table.shape[1:], BF), pltpu.SemaphoreType.DMA((7,))],
            *arrays, table, fetched=range(7), limit=PACK_BYTES,
        )
    axes = ("tm", "lat")
    across, on_chip, next_chip, diag_near, diag_far = swap_pairs(lax.axis_size("tm"), bands)
    p_bg = background.reshape(fields * rows, lon)
    r_bg = lax.ppermute(p_bg, axes, across)
    r_dfar = lax.ppermute(dfar, axes, diag_far)
    r_far = lax.ppermute(far, axes, next_chip)
    r_dnear = lax.ppermute(dnear, axes, diag_near)
    r_near = lax.ppermute(near, axes, on_chip)
    return p_bg, r_bg, p_c, r_near, r_far, r_dnear, r_dfar


def exchange_gathered(background, east, north, diff, sensors, observations):
    frames, variables, rows, lon = background.shape
    fields = frames * variables
    half = lon // 2
    tiles, bands = lax.axis_size("tm"), lax.axis_size("lat")
    down = [(j, j + 1) for j in range(bands - 1)]
    up = [(j + 1, j) for j in range(bands - 1)]
    later = [(t, t + 1) for t in range(tiles - 1)]
    earlier = [(t + 1, t) for t in range(tiles - 1)]
    coefs = jnp.stack([east, north, diff - K_MID]).astype(BF)
    coefs = lax.all_gather(coefs, "tm", axis=2, tiled=True)
    around = jnp.concatenate(
        [lax.ppermute(background, "tm", later), lax.ppermute(background, "tm", earlier)], axis=0
    )
    cells = lax.all_to_all(sensors, "tm", split_axis=0, concat_axis=2, tiled=True)[:, 0]
    obs = lax.all_to_all(observations, "tm", split_axis=0, concat_axis=2, tiled=True)[:, 0]
    cells = jnp.moveaxis(cells, 1, 0)
    obs = jnp.transpose(obs, (1, 0, 2, 3))
    obs_high = obs.astype(BF).astype(F32)
    digits = jnp.stack([(cells >> 8).astype(F32), (cells & 255).astype(F32)], axis=2)
    described = jnp.concatenate([digits, obs_high], axis=2).reshape(tiles, -1).astype(BF)
    low = (obs - obs_high).astype(BF).reshape(tiles, -1)
    low = jnp.pad(low, ((0, 0), (0, described.shape[1] - low.shape[1])))
    bands_of = [
        lax.ppermute(described, "lat", down), described, lax.ppermute(described, "lat", up), low
    ]
    sens = jnp.stack([x.reshape(2, tiles // 2, -1) for x in bands_of], axis=1)
    sens = sens.reshape(-1, described.shape[1])

    def block(h):
        part = coefs[:, :, h * half : (h + 1) * half]
        blank = jnp.zeros_like(part[0])
        return jnp.concatenate(
            [jnp.concatenate([part[0], part[2]], axis=1), jnp.concatenate([part[1], blank], axis=1)],
            axis=0,
        )

    def edge_fields(fields_4d, depth, bottom):
        first = rows - depth if bottom else 0
        return fields_4d[:, :, first : first + depth].reshape(-1, lon)

    def edge_coefs(h, bottom):
        first = rows - CROWS if bottom else 0
        part = coefs[:, first : first + CROWS, h * half : (h + 1) * half]
        part = jnp.pad(part.reshape(3 * CROWS, half), ((0, 16 - 3 * CROWS), (0, 0)))
        return jnp.concatenate([part[:8], part[8:]], axis=1)

    received = []
    for bottom, pairs in ((False, up), (True, down)):
        message = [edge_fields(background, HALO, bottom), edge_coefs(0, bottom)]
        message = lax.ppermute(jnp.concatenate(message, axis=0), "lat", pairs)
        diagonal = lax.ppermute(edge_fields(around, 1, bottom), "lat", pairs)
        received.append((message, diagonal, lax.ppermute(edge_coefs(1, bottom), "lat", pairs)))
    (near, dnear, c_near), (far, dfar, c_far) = received
    p_bg, r_bg = background.reshape(-1, lon), around.reshape(-1, lon)
    r_c = jnp.concatenate([block(1), c_near, c_far], axis=0)
    return p_bg, r_bg, block(0), r_c, near, far, dnear, dfar, sens


def shards(
    background, conv_weight, conv_bias, mix_weight, mix_bias, out_weight, out_bias,
    drift_east, drift_north, diffusivity, sensors, observations,
):
    frames, variables, rows, lon = background.shape
    tiles, bands = lax.axis_size("tm"), lax.axis_size("lat")
    paired = tiles == 2 and bands % 2 == 0
    group = rows // 2
    hid = mix_weight.shape[0]
    fields = frames * variables
    arrays = (background, drift_east, drift_north, diffusivity, sensors, observations)
    if paired:
        p_bg, r_bg, p_c, near, far, dnear, dfar = exchange_pairs(*arrays)
        offsets = [[*range(2 * frames)], [*range(frames), *range(-frames, 0)]]
        i_of = lambda: lax.axis_index("tm")
        parity_of = lambda: lax.axis_index("lat") % 2
        sens = ()
    else:
        p_bg, r_bg, p_c, r_c, near, far, dnear, dfar, sens = exchange_gathered(*arrays)
        offsets = [[*range(frames), *range(-frames, 0), *range(frames, 2 * frames)]]
        i_of = lambda: 0
        parity_of = lambda: 0
        sens = (sens,)
    others = len(offsets[0]) - frames

    channels = (frames + others) * variables
    depth = -(-(3 * round16((group + 2) * channels) + 3) // 128) * 128
    quarters = 8 // variables
    width = lon // 8
    taps = jnp.asarray(np.stack([tap_table(o, frames, variables, group, depth) for o in offsets]))
    own, coef, back, halo, chalo, ohalo = model_tables(rows, frames, variables, quarters)
    gather = conv_table(rows, frames, others, variables, group)
    index = np.stack(
        [index_rows([gather[c], *halo[c], chalo[c], own, coef, back, ohalo[c]], 256) for c in range(5)]
    )
    tables = [gather[0], own, coef, back, halo[0], chalo[0], ohalo[0]]
    small = [conv_weight, conv_bias.reshape(1, -1), mix_weight, mix_bias.reshape(1, -1)]
    small += [out_weight, out_bias.reshape(1, -1)]
    with jax.named_scope("weights"):
        weights = call(
            functools.partial(
                prep_kernel, group=group, channels=channels, i_of=i_of, parity_of=parity_of
            ),
            [
                struct((frames * group * hid, depth), BF),
                struct((group * hid, group * hid), BF),
                struct((variables * group, group * hid), BF),
                struct((group * hid, 128), F32),
                struct((variables * group, 128), F32),
            ]
            + [struct(x.shape, BF) for x in tables],
            [pltpu.VMEM(x.shape, x.dtype) for x in small]
            + [pltpu.VMEM(taps.shape[1:], jnp.int32), pltpu.VMEM(index.shape[1:], jnp.int32)]
            + [pltpu.SemaphoreType.DMA((8,))],
            *small, taps, jnp.asarray(index), fetched=range(8),
        )
    if paired:
        with jax.named_scope("own_coefs"):
            p_c = call(hold_kernel, struct(p_c.shape, BF), [], p_c)
        held = (far, near, r_bg, p_c, *weights)
        far, near, r_bg, p_c, *weights = lax.optimization_barrier(held)
        with jax.named_scope("relay"):
            late = call(relay_kernel, struct((2 * rows + 16, lon), BF), [], far, near, p_c)
        dfar, dnear, late = lax.optimization_barrier((dfar, dnear, late))
        r_c = lax.ppermute(late, ("tm", "lat"), swap_pairs(tiles, bands)[0])
    *w_conv, p_conv = weights[:6]
    p_model = weights[6:]
    with jax.named_scope("prior"):
        prior = call(
            functools.partial(
                conv_kernel, frames=frames, variables=variables, group=group, chunk=256
            ),
            struct(background.shape, F32),
            [pltpu.VMEM((rows // group, depth, lon), BF)],
            p_bg, r_bg, near, far, dnear, dfar, *w_conv, p_conv,
            cost=COST,
        )
    tall, ctall = rows + 2 * HALO, rows + 2 * CROWS
    with jax.named_scope("model"):
        return call(
            functools.partial(
                model_kernel, rows=rows, frames=frames, variables=variables,
                tile_cols=drift_east.shape[1], n_sens=sensors.shape[3],
                paired=paired, i_of=i_of, parity_of=parity_of,
            ),
            struct(background.shape, F32),
            [
                pltpu.VMEM((2 * frames, tall, 8, width), F32),
                pltpu.VMEM((2 * frames, tall, 8, width), F32),
                pltpu.VMEM((2, 5, ctall, 8, width), F32),
            ],
            p_bg, p_c, r_c, near, far, dnear, dfar, *sens, prior, *p_model,
        )


def solution(mesh):
    placed = (
        P("tm", None, "lat", None),
        P(),
        P(),
        P(),
        P(),
        P(),
        P(),
        P("lat", "tm"),
        P("lat", "tm"),
        P("lat", "tm"),
        P(None, "lat", "tm", None),
        P(None, "lat", "tm", None, None),
    )
    return jax.shard_map(
        shards, mesh=mesh, in_specs=placed, out_specs=P("tm", None, "lat", None), check_vma=False
    )
```

```python
import functools

import jax
import jax.numpy as jnp
import numpy as np
from jax import lax
from jax.experimental import pallas as pl
from jax.experimental.pallas import tpu as pltpu
from jax.sharding import PartitionSpec as P

KT = 5
SUB = 3
K_MID = 0.17
HALO = 2 * SUB
CROWS = 2 * SUB - 1
BF = jnp.bfloat16
F32 = jnp.float32
VMEM_BYTES = 48 * 1024 * 1024
COST = 60 * 10**6
PACK_BYTES = 64 * 1024 * 1024 - 1024 * 1024
GELU_1 = 2.0 * float(np.sqrt(2.0 / np.pi))
GELU_2 = 8.0 * 0.044715 * float(np.sqrt(2.0 / np.pi))


def dot(a, b):
    return jnp.dot(a, b, preferred_element_type=F32)


def dot_t(a, b):
    return lax.dot_general(a, b, (((1,), (1,)), ((), ())), preferred_element_type=F32)


def split2(x):
    high = x.astype(BF)
    return high, (x - high.astype(F32)).astype(BF)


def fetch(pairs, sems):
    copies = [pltpu.make_async_copy(source, target, sems.at[n]) for n, (source, target) in enumerate(pairs)]
    for copy in copies:
        copy.start()
    for copy in copies:
        copy.wait()


def pack_table(rows, fields):
    table = np.zeros((2, 2, 80, 128), np.float32)
    coef_row = fields * rows
    for parity in range(2):
        for side in range(2):
            for message in range(4):
                far, diagonal = message % 2, message // 2
                bottom = (far == 0) == (parity == 0)
                out = table[parity, side]
                if diagonal:
                    base = 64 + 8 * far
                    for field in range(fields):
                        out[base + field, field * rows + (rows - 1 if bottom else 0)] = 1
                    if side == 0:
                        out[base + fields, coef_row + 3 * rows + 15] = 1
                    continue
                base = 32 * far
                for field in range(fields):
                    for e in range(HALO):
                        row = rows - HALO + e if bottom else e
                        out[base + field * HALO + e, field * rows + row] = 1
                for slot in range(8):
                    j = side * 8 + slot
                    target = base + 24 + slot
                    if j < 3 * CROWS:
                        c, e = divmod(j, CROWS)
                        row = rows - CROWS + e if bottom else e
                        out[target, coef_row + c * rows + row] = 1
                    else:
                        out[target, coef_row + 3 * rows + 14] = 1
    return table


def near_far(case):
    parity = case in (1, 3)
    top_ok = case != 2
    bottom_ok = case not in (3, 4)
    top_slot = 0 if parity else 1
    return top_slot, 1 - top_slot, top_ok, bottom_ok


def model_tables(rows, frames, variables, quarters):
    lanes = quarters * variables
    own = np.zeros((rows * lanes, quarters * variables * rows), np.float32)
    coef = np.zeros((rows * lanes, quarters * rows), np.float32)
    out = np.zeros((lanes * rows, rows * lanes), np.float32)
    for r in range(rows):
        for q in range(quarters):
            for v in range(variables):
                own[r * lanes + q * variables + v, (q * variables + v) * rows + r] = 1
                coef[r * lanes + q * variables + v, q * rows + r] = 1
                out[(q * variables + v) * rows + r, r * lanes + q * variables + v] = 1
    halo = np.zeros((5, frames, 2 * HALO * lanes, quarters * 64), np.float32)
    chalo = np.zeros((5, 3 * 2 * CROWS * lanes, quarters * 64), np.float32)
    ohalo = np.zeros((5, 3 * 2 * CROWS * lanes, quarters * 32), np.float32)
    for case in range(5):
        top_slot, bottom_slot, top_ok, bottom_ok = near_far(case)
        for q in range(quarters):
            for v in range(variables):
                lane = q * variables + v
                for half, slot, ok in ((0, top_slot, top_ok), (1, bottom_slot, bottom_ok)):
                    if not ok:
                        continue
                    for t in range(frames):
                        for e in range(HALO):
                            local = (t * variables + v) * HALO + e
                            halo[case, t, (half * HALO + e) * lanes + lane, q * 64 + slot * 32 + local] = 1
                    for c in range(3):
                        for e in range(CROWS):
                            j = c * CROWS + e
                            column = q * 64 + slot * 32 + (j // 8) * 16 + 8 + j % 8
                            row = ((c * 2 + half) * CROWS + e) * lanes + lane
                            chalo[case, row, column] = 1
                            column = q * 32 + (j // 8) * 16 + slot * 8 + j % 8
                            ohalo[case, row, column] = 1
    return own, coef, out, halo, chalo, ohalo


def round16(n):
    return -(-n // 16) * 16


def conv_table(rows, frames, others, variables, group):
    channels = (frames + others) * variables
    tall = round16((group + 2) * channels)
    own_rows = frames * variables * rows
    oth_rows = others * variables * rows
    table = np.zeros((5, rows // group * tall, own_rows + oth_rows + 80), np.float32)
    for case in range(5):
        top_slot, bottom_slot, top_ok, bottom_ok = near_far(case)
        for g in range(rows // group):
            for yy in range(group + 2):
                y = g * group + yy - 1
                for f in range(frames + others):
                    for v in range(variables):
                        target = g * tall + yy * channels + f * variables + v
                        own = f < frames
                        field = (f if own else f - frames) * variables + v
                        if 0 <= y < rows:
                            table[case, target, (0 if own else own_rows) + field * rows + y] = 1
                            continue
                        slot, ok = (top_slot, top_ok) if y < 0 else (bottom_slot, bottom_ok)
                        if not ok:
                            continue
                        column = own_rows + oth_rows
                        if own:
                            column += slot * 32 + field * HALO + (HALO - 1 if y < 0 else 0)
                        else:
                            column += 64 + slot * 8 + field
                        table[case, target, column] = 1
    return table


def tap_table(offsets, frames, variables, group, depth):
    channels = len(offsets) * variables
    tall = round16((group + 2) * channels)
    table = np.full((8, depth), -1, np.int32)
    for t in range(frames):
        for s in range(3):
            for i in range(3):
                for f, offset in enumerate(offsets):
                    lag = offset - t + KT // 2
                    for v in range(variables):
                        if 0 <= lag < KT:
                            k = s * tall + i * channels + f * variables + v
                            table[t, k] = ((v * KT + lag) * 3 + i) * 3 + s
    table[frames, 3 * tall : 3 * tall + 3] = 3 * 3 * KT * variables + np.arange(3)
    return table


def index_rows(tables, lanes):
    out = np.full((8, lanes), -1, np.int32)
    for n, table in enumerate(tables):
        out[n, : table.shape[0]] = np.where(table.any(1), table.argmax(1), -1)
    return out


def case_of(parity, index, count):
    return jnp.where(index == 0, 2, jnp.where(index == count - 1, jnp.where(parity == 1, 3, 4), parity))


def pack_kernel(
    bg_in, east_in, north_in, diff_in, sensors_in, obs_in, table_in, p_c, near, far, dnear, dfar,
    bg, east, north, diff, sensors, obs, table, sems, *, frames,
):
    me_t = lax.axis_index("tm")
    parity = lax.axis_index("lat") % 2
    fetch(
        [
            (bg_in, bg), (east_in, east), (north_in, north), (diff_in, diff),
            (sensors_in, sensors), (obs_in, obs), (table_in.at[parity], table),
        ],
        sems,
    )
    fields = bg.shape[0] * bg.shape[1]
    rows, lon = bg.shape[2], bg.shape[3]
    half = lon // 2
    fields_2d = bg[...].reshape(fields * rows, lon)
    a, b = east[...].astype(BF), north[...].astype(BF)
    k = (diff[...] - K_MID).astype(BF)

    def described(first, low):
        pieces = []
        for t in range(frames):
            cells = sensors[first + t, 0]
            if not low:
                pieces += [(cells >> 8).astype(F32), (cells & 255).astype(F32)]
            for v in range(obs.shape[3]):
                value = obs[first + t, 0, 0, v : v + 1]
                high = value.astype(BF).astype(F32)
                pieces.append(value - high if low else high)
        row = jnp.concatenate(pieces, axis=1)
        if row.shape[1] < half:
            row = jnp.concatenate([row, jnp.zeros((1, half - row.shape[1]), F32)], axis=1)
        return row

    mine, theirs = me_t * frames, (1 - me_t) * frames
    extra = jnp.concatenate(
        [
            jnp.zeros((12, half), F32),
            described(mine, True),
            described(theirs, True),
            described(mine, False),
            described(theirs, False),
        ],
        axis=0,
    ).astype(BF)
    p_c[0:rows, 0:half] = a
    p_c[rows : 2 * rows, 0:half] = b
    p_c[0:rows, half:lon] = k
    p_c[rows : 2 * rows, half:lon] = extra
    for side in range(2):
        cut = slice(side * half, (side + 1) * half)
        source = jnp.concatenate([fields_2d[:, cut], a, b, k, extra], axis=0)
        message = dot(table[side], source).astype(BF)
        near[:, cut] = message[0:32]
        far[:, cut] = message[32:64]
        dnear[:, cut] = message[64:72]
        dfar[:, cut] = message[72:80]


def hold_kernel(source, out):
    out[...] = source[...]


def relay_kernel(far, near, p_c, out):
    own, edge = p_c.shape[0], near.shape[0] - 8
    out[0:own, :] = p_c[...]
    out[own : own + 8, :] = near[edge : edge + 8, :]
    out[own + 8 : own + 16, :] = far[edge : edge + 8, :]


def prep_kernel(*refs, group, channels, i_of, parity_of):
    sources, rest = refs[:8], refs[8:]
    w1, w2, w3, b2, b3, p_conv, p_own, p_coef, p_out, p_halo, p_chalo, p_ohalo = rest[:12]
    conv_w, conv_b, mix_w, mix_b, out_w, out_b, taps, index, sems = rest[12:]
    hid = mix_w.shape[0]
    case = case_of(parity_of(), lax.axis_index("lat"), lax.axis_size("lat"))
    moves = [*zip(sources[:6], (conv_w, conv_b, mix_w, mix_b, out_w, out_b))]
    moves += [(sources[6].at[i_of()], taps), (sources[7].at[case], index)]
    fetch(moves, sems)
    columns = index[...].astype(F32).T

    def select(n, shape):
        lanes = lax.broadcasted_iota(jnp.int32, shape, 1).astype(F32)
        return jnp.where(lanes == columns[0 : shape[0], n : n + 1], 1.0, 0.0)

    frames = p_halo.shape[0]
    p_conv[...] = select(0, p_conv.shape).astype(BF)
    for t in range(frames):
        p_halo[t] = select(1 + t, p_halo.shape[1:]).astype(BF)
    for n, target in ((1 + frames, p_chalo), (5 + frames, p_ohalo)):
        halved = lax.broadcasted_iota(jnp.int32, target.shape, 0) < target.shape[0] // 3 * 2
        target[...] = (select(n, target.shape) * jnp.where(halved, 0.5, 1.0)).astype(BF)
    p_own[...] = select(2 + frames, p_own.shape).astype(BF)
    p_coef[...] = select(3 + frames, p_coef.shape).astype(BF)
    p_out[...] = select(4 + frames, p_out.shape).astype(BF)
    table = taps[...]

    def column(row):
        n = row.shape[1]
        here = lax.broadcasted_iota(jnp.int32, (n, n), 0) == lax.broadcasted_iota(jnp.int32, (n, n), 1)
        return jnp.sum(jnp.where(here, jnp.broadcast_to(row, (n, n)), 0.0), axis=1, keepdims=True)

    bias = 0.5 * column(conv_b[...])
    pieces = []
    for _ in range(3):
        piece = bias.astype(BF)
        bias = bias - piece.astype(F32)
        pieces.append(piece.astype(F32))
    ntap = conv_w.shape[1]
    padded = 128
    weights = jnp.concatenate(
        [0.5 * conv_w[...].astype(F32)] + pieces + [jnp.zeros((hid, padded - ntap - 3), F32)], axis=1
    ).astype(BF)
    tap_id = lax.broadcasted_iota(jnp.int32, (padded, table.shape[1]), 0)

    def chosen(n):
        return dot(weights, jnp.where(tap_id == table[n : n + 1, :], 1.0, 0.0).astype(BF))

    biased = chosen(frames)
    for t in range(frames):
        first = chosen(t)
        for y in range(group):
            start = (t * group + y) * hid
            moved = pltpu.roll(first, y * channels, 1) if y else first
            w1[start : start + hid, :] = (moved + biased).astype(BF)
    tall = group * hid
    row = lax.broadcasted_iota(jnp.int32, (tall, hid), 0) & (hid - 1)
    up = jnp.where(row == lax.broadcasted_iota(jnp.int32, (tall, hid), 1), 1.0, 0.0).astype(BF)
    mixed = dot_t(dot(up, (0.5 * mix_w[...].astype(F32)).astype(BF)).astype(BF), up)
    shift = hid.bit_length() - 1
    rows2 = lax.broadcasted_iota(jnp.int32, (tall, tall), 0) >> shift
    cols2 = lax.broadcasted_iota(jnp.int32, (tall, tall), 1) >> shift
    w2[...] = jnp.where(rows2 == cols2, mixed, 0.0).astype(BF)
    variables = out_w.shape[0]
    wide = dot_t(out_w[...], up)
    y = lax.broadcasted_iota(jnp.int32, (group, tall), 0)
    here = y == lax.broadcasted_iota(jnp.int32, (group, tall), 1) >> shift
    w3[...] = jnp.concatenate(
        [jnp.where(here, jnp.broadcast_to(wide[v : v + 1], (group, tall)), 0.0) for v in range(variables)],
        axis=0,
    ).astype(BF)
    b3[...] = jnp.concatenate(
        [jnp.broadcast_to(out_b[:, v : v + 1], (group, 128)) for v in range(variables)], axis=0
    )
    mixed_bias = jnp.broadcast_to(0.5 * column(mix_b[...]), (hid, 128))
    b2[...] = jnp.concatenate([mixed_bias] * group, axis=0)


def model_kernel(
    p_bg, p_c, r_c, near, far, dnear, dfar, *rest,
    rows, frames, variables, tile_cols, n_sens, paired, i_of, parity_of,
):
    sens = None if paired else rest[0]
    first = 0 if paired else 1
    prior, p_own, p_coef, p_out, p_halo, p_chalo, p_ohalo = rest[first : first + 7]
    out, field_a, field_b, coefs = rest[first + 7 :]
    lon = p_bg.shape[1]
    half = lon // 2
    quarters = 8 // variables
    width = half // quarters
    me_l, count = lax.axis_index("lat"), lax.axis_size("lat")
    parity = parity_of()
    me_t = i_of()
    top_ok, bottom_ok = me_l > 0, me_l < count - 1
    tall = rows + 2 * HALO

    for t in range(frames):
        for h in range(2):
            g = t * 2 + h
            body, rim = [], []
            for q in range(quarters):
                cut = slice(h * half + q * width, h * half + (q + 1) * width)
                body.append(p_bg[t * variables * rows : (t + 1) * variables * rows, cut])
                rim += [near[:, cut], far[:, cut]]
            field_a[g, HALO : HALO + rows] = dot(p_own[...], jnp.concatenate(body, axis=0)).reshape(rows, 8, width)
            edges = dot(p_halo[t], jnp.concatenate(rim, axis=0)).reshape(2 * HALO, 8, width)
            field_a[g, 0:HALO] = edges[0:HALO]
            field_a[g, HALO + rows : tall] = edges[HALO:]

    ctall = rows + 2 * CROWS
    for source in range(2):
        big = p_c if source == 0 else r_c
        spot = me_t if source == 0 else 1 - me_t
        pieces = []
        for side in range(2):
            for c_row in range(2):
                stack = []
                for q in range(quarters):
                    cut = slice(side * half + q * width, side * half + (q + 1) * width)
                    stack.append(big[c_row * rows : (c_row + 1) * rows, cut])
                pieces.append(jnp.concatenate(stack, axis=0))
        scaled = p_coef[...]
        ha = (0.5 * dot(scaled, pieces[0])).reshape(rows, 8, width)
        hb = (0.5 * dot(scaled, pieces[1])).reshape(rows, 8, width)
        kk = dot(scaled, pieces[2]).reshape(rows, 8, width) + K_MID
        rim = []
        for q in range(quarters):
            for message in (near[16:32], far[16:32]) if source == 0 else (r_c[2 * rows : 2 * rows + 16],):
                for side in range(2):
                    cut = slice(side * half + q * width, side * half + (q + 1) * width)
                    rim.append(message[:, cut])
        edges = dot((p_ohalo if source else p_chalo)[...], jnp.concatenate(rim, axis=0))
        edges = edges.reshape(3, 2, CROWS, 8, width)
        k_top = edges[2, 0] + jnp.where(top_ok, K_MID, 0.0)
        k_bottom = edges[2, 1] + jnp.where(bottom_ok, K_MID, 0.0)
        for start, size, xa, xb, xk in (
            (0, CROWS, edges[0, 0], edges[1, 0], k_top),
            (CROWS, rows, ha, hb, kk),
            (CROWS + rows, CROWS, edges[0, 1], edges[1, 1], k_bottom),
        ):
            span = slice(start, start + size)
            coefs[spot, 0, span] = xk - xa
            coefs[spot, 1, span] = xk + xa
            coefs[spot, 2, span] = xk - xb
            coefs[spot, 3, span] = xk + xb
            coefs[spot, 4, span] = 1.0 - 4.0 * xk

    lane = lax.broadcasted_iota(jnp.int32, (8, 128), 1)
    sub_q = lax.broadcasted_iota(jnp.int32, (8, 128), 0) >> (variables.bit_length() - 1)
    first_lane, last_lane = lane == 0, lane == 127
    first_q, last_q = sub_q == 0, sub_q == quarters - 1
    tiles = width // 128

    def cut_tiles(x):
        return [x[:, n * 128 : (n + 1) * 128] for n in range(tiles)]

    def from_west(x0, x1):
        both = [[pltpu.roll(part, 1, 1) for part in cut_tiles(x)] for x in (x0, x1)]
        result = []
        for h in range(2):
            wrapped = jnp.where(last_q, both[1 - h][-1], both[h][-1])
            carry = pltpu.roll(wrapped, variables, 0)
            parts = []
            for n in range(tiles):
                parts.append(jnp.where(first_lane, carry if n == 0 else both[h][n - 1], both[h][n]))
            result.append(jnp.concatenate(parts, axis=1))
        return result

    def from_east(x0, x1):
        both = [[pltpu.roll(part, 127, 1) for part in cut_tiles(x)] for x in (x0, x1)]
        result = []
        for h in range(2):
            wrapped = jnp.where(first_q, both[1 - h][0], both[h][0])
            carry = pltpu.roll(wrapped, 8 - variables, 0)
            parts = []
            for n in range(tiles):
                parts.append(
                    jnp.where(last_lane, carry if n == tiles - 1 else both[h][n + 1], both[h][n])
                )
            result.append(jnp.concatenate(parts, axis=1))
        return result

    def forward(source, target, low, high):
        for r in range(low, high):
            cr = r - (HALO - CROWS)
            for t in range(frames):
                center = [source[t * 2 + h, r] for h in range(2)]
                west, east = from_west(*center), from_east(*center)
                for h in range(2):
                    g = t * 2 + h
                    target[g, r] = (
                        (coefs[h, 4, cr] * center[h] + coefs[h, 0, cr] * east[h])
                        + (coefs[h, 1, cr] * west[h] + coefs[h, 2, cr] * source[g, r + 1])
                        + coefs[h, 3, cr] * source[g, r - 1]
                    )

    def backward(source, target, low, high):
        for r in range(low, high):
            cr = r - (HALO - CROWS)
            for t in range(frames):
                center = [source[t * 2 + h, r] for h in range(2)]
                west = from_west(*[coefs[h, 0, cr] * center[h] for h in range(2)])
                east = from_east(*[coefs[h, 1, cr] * center[h] for h in range(2)])
                for h in range(2):
                    g = t * 2 + h
                    target[g, r] = (
                        (coefs[h, 4, cr] * center[h] + west[h])
                        + (east[h] + coefs[h, 2, cr - 1] * source[g, r - 1])
                        + coefs[h, 3, cr + 1] * source[g, r + 1]
                    )

    buffers = [field_a, field_b]
    for step in range(SUB):
        forward(buffers[step % 2], buffers[(step + 1) % 2], step + 1, tall - step - 1)
    forecast, spread = buffers[SUB % 2], buffers[(SUB + 1) % 2]

    def kinds(row, t):
        base = t * (2 + variables) * n_sens
        return [row[:, base + n * n_sens : base + (n + 1) * n_sens] for n in range(2 + variables)]

    def sensor_rows(h, band):
        if not paired:
            count = sens.shape[0] // 8
            first = (h * 4 + band) * count
            return [sens[...].astype(F32)[first + n : first + n + 1] for n in range(count)]
        if band in (1, 3):
            at = slice(rows, rows + 16)
            mine, other = p_c[at, half:lon].astype(F32), r_c[at, half:lon].astype(F32)
            n = 14 if band == 1 else 12
            return [jnp.where(me_t == h, mine[n : n + 1], other[n + 1 : n + 2])]
        from_far = parity == (0 if band == 0 else 1)
        pair = [m[16:32, half:lon].astype(F32)[15:16] for m in (near, far)]
        row = frames * variables
        pair += [m[:, 0:half].astype(F32)[row : row + 1] for m in (dnear, dfar)]
        found = [jnp.where(from_far, pair[n + 1], pair[n]) for n in (0, 2)]
        return [jnp.where(me_t == h, found[0], found[1])]

    row_bits = tile_cols.bit_length() - 1
    width_bits = width.bit_length() - 1

    def located(h, band, t):
        found = []
        for n, row in enumerate(sensor_rows(h, band)):
            high, low, *values = kinds(row, t)
            cell = (high * 256.0 + low).astype(jnp.int32)
            column = (cell & (tile_cols - 1)) + n * tile_cols
            found.append([cell >> row_bits, column >> width_bits, column & (width - 1)] + list(values))
        if band == 1:
            for n, row in enumerate(sensor_rows(h, 3)):
                for v in range(variables):
                    found[n][3 + v] = found[n][3 + v] + row[:, (t * variables + v) * n_sens : (t * variables + v + 1) * n_sens]
        return [jnp.concatenate([f[n] for f in found], axis=1) for n in range(3 + variables)]

    def assimilate(g, row_list, where_row, quarter, lane_of, values):
        total = where_row.shape[1]
        lanes_bf = lax.broadcasted_iota(jnp.int32, (width, total), 0).astype(F32).astype(BF)
        apart = jnp.abs(lanes_bf - lane_of.astype(F32).astype(BF))
        onehot = jnp.maximum(BF(1) - apart, BF(0))
        stack = jnp.concatenate([forecast[g, HALO + r] for r in row_list], axis=0)
        size = 8 * len(row_list)
        picked = dot(jnp.concatenate(split2(stack), axis=0), onehot)
        picked = picked[:size] + picked[size:]
        shape = (8, total)
        here_q = (lax.broadcasted_iota(jnp.int32, shape, 0) >> (variables.bit_length() - 1)) == quarter
        variable = lax.broadcasted_iota(jnp.int32, shape, 0) & (variables - 1)
        misfit = jnp.zeros(shape, F32)
        for n, r in enumerate(row_list):
            misfit = misfit + jnp.where(where_row == r, picked[n * 8 : (n + 1) * 8], 0.0)
        target = jnp.broadcast_to(values[0], shape)
        for v in range(1, variables):
            target = jnp.where(variable == v, values[v], target)
        misfit = jnp.where(here_q, misfit - target, 0.0)
        row_f = where_row.astype(F32)
        weighted = jnp.concatenate([jnp.where(row_f == float(r), misfit, 0.0) for r in row_list], axis=0)
        sums = dot_t(jnp.concatenate(split2(weighted), axis=0), onehot)
        return (sums[:size] + sums[size:]).reshape(len(row_list), 8, width)

    far_away = -(1 << 20)
    for t in range(frames):
        for h in range(2):
            g = t * 2 + h
            row, quarter, lane_of, *values = located(h, 1, t)
            spread[g, HALO : HALO + rows] = assimilate(g, list(range(rows)), row, quarter, lane_of, values)
            above, below = located(h, 0, t), located(h, 2, t)
            above[0] = jnp.where(top_ok, above[0] - rows, far_away)
            below[0] = jnp.where(bottom_ok, below[0] + rows, far_away)
            merged = [jnp.concatenate([x, y], axis=1) for x, y in zip(above, below)]
            rim_rows = list(range(-SUB, 0)) + list(range(rows, rows + SUB))
            rim = assimilate(g, rim_rows, merged[0], merged[1], merged[2], merged[3:])
            spread[g, HALO - SUB : HALO] = rim[0:SUB]
            spread[g, HALO + rows : HALO + rows + SUB] = rim[SUB:]

    buffers = [spread, forecast]
    for step in range(SUB):
        low = HALO - SUB + step + 1
        backward(buffers[step % 2], buffers[(step + 1) % 2], low, tall - low)
    result = buffers[SUB % 2]
    twice = jnp.concatenate([p_out[...], p_out[...]], axis=1)

    for t in range(frames):
        for h in range(2):
            parts = split2(result[t * 2 + h, HALO : HALO + rows].reshape(rows * 8, width))
            back = dot(twice, jnp.concatenate(parts, axis=0))
            for q in range(quarters):
                cut = slice(h * half + q * width, h * half + (q + 1) * width)
                for v in range(variables):
                    base = (q * variables + v) * rows
                    out[t, v, :, cut] = prior[t, v, :, cut] - back[base : base + rows]


def gelu(y):
    inner = y * (GELU_1 + GELU_2 * (y * y))
    return (y + y * jnp.tanh(inner)).astype(BF)


def shifted(chosen, window, depth):
    tall, lon = chosen.shape
    packed = chosen.astype(BF)
    window[0:tall] = pltpu.roll(packed, 1, 1)
    window[tall : 2 * tall] = packed
    window[2 * tall : 3 * tall] = pltpu.roll(packed, lon - 1, 1)
    ones = lax.broadcasted_iota(jnp.int32, (depth - 3 * tall, lon), 0) < 3
    window[3 * tall : depth] = jnp.where(ones, 1.0, 0.0).astype(BF)


def widen(column, chunk):
    return jnp.concatenate([column] * (chunk // 128), axis=1)


def conv_kernel(
    p_bg, r_bg, near, far, dnear, dfar, w1, w2, w3, b2, b3, select, out, window,
    *, frames, variables, group, chunk,
):
    groups, depth, lon = window.shape
    fields = jnp.concatenate([x[...] for x in (p_bg, r_bg, near, far, dnear, dfar)], axis=0)
    chosen = dot(select[...], fields)
    tall = chosen.shape[0] // groups
    for g in range(groups):
        shifted(chosen[g * tall : (g + 1) * tall], window.at[g], depth)
    hidden = w2.shape[0]
    bias2, bias3 = widen(b2[...], chunk), widen(b3[...], chunk)
    pending = []
    wide2 = jnp.concatenate([bias2] * frames, axis=1)
    for n in range(lon // chunk):
        cut = slice(n * chunk, (n + 1) * chunk)
        for g in range(groups):
            first = dot(w1[...], window[g, :, cut])
            one = [gelu(first[t * hidden : (t + 1) * hidden]) for t in range(frames)]
            pending.append((g, cut, gelu(dot(w2[...], jnp.concatenate(one, axis=1)) + wide2)))
    for g, cut, two in pending:
        scores = dot(w3[...], two)
        for t in range(frames):
            score = scores[:, t * chunk : (t + 1) * chunk] + bias3
            for v in range(variables):
                out[t, v, g * group : (g + 1) * group, cut] = score[v * group : (v + 1) * group]


def call(body, out_shape, scratch, *args, fetched=(), limit=VMEM_BYTES, cost=None):
    whole = pl.BlockSpec(memory_space=pltpu.VMEM)
    given = pl.BlockSpec(memory_space=pltpu.HBM)
    several = isinstance(out_shape, (list, tuple))
    if cost is not None:
        cost = pl.CostEstimate(flops=10**8, bytes_accessed=cost, transcendentals=0)
    return pl.pallas_call(
        body,
        out_shape=out_shape,
        in_specs=[given if n in fetched else whole for n in range(len(args))],
        out_specs=[whole] * len(out_shape) if several else whole,
        scratch_shapes=scratch,
        compiler_params=pltpu.CompilerParams(vmem_limit_bytes=limit),
        cost_estimate=cost,
    )(*args)


def struct(shape, dtype):
    return jax.ShapeDtypeStruct(shape, dtype)


def swap_pairs(tiles, bands):
    def at(t, j):
        return t * bands + j

    def far(j):
        return j + 1 if j % 2 else j - 1

    cells = [(t, j) for t in range(tiles) for j in range(bands)]
    inner = lambda j: 0 <= far(j) < bands
    return (
        [(at(t, j), at(1 - t, j)) for t, j in cells],
        [(at(t, j), at(t, j ^ 1)) for t, j in cells],
        [(at(t, j), at(t, far(j)) if inner(j) else at(1 - t, j)) for t, j in cells],
        [(at(t, j), at(1 - t, j ^ 1)) for t, j in cells],
        [(at(t, j), at(1 - t, far(j)) if inner(j) else at(1 - t, j)) for t, j in cells],
    )


def exchange_pairs(background, east, north, diff, sensors, observations):
    frames, variables, rows, lon = background.shape
    fields = frames * variables
    bands = lax.axis_size("lat")
    table = jnp.asarray(pack_table(rows, fields), BF)
    arrays = (background, east, north, diff, sensors, observations)
    lat_message, diagonal = struct((32, lon), BF), struct((8, lon), BF)
    with jax.named_scope("pack"):
        p_c, near, far, dnear, dfar = call(
            functools.partial(pack_kernel, frames=frames),
            [struct((2 * rows, lon), BF), lat_message, lat_message, diagonal, diagonal],
            [pltpu.VMEM(x.shape, x.dtype) for x in arrays]
            + [pltpu.VMEM(table.shape[1:], BF), pltpu.SemaphoreType.DMA((7,))],
            *arrays, table, fetched=range(7), limit=PACK_BYTES,
        )
    axes = ("tm", "lat")
    across, on_chip, next_chip, diag_near, diag_far = swap_pairs(lax.axis_size("tm"), bands)
    p_bg = background.reshape(fields * rows, lon)
    r_bg = lax.ppermute(p_bg, axes, across)
    r_dfar = lax.ppermute(dfar, axes, diag_far)
    r_far = lax.ppermute(far, axes, next_chip)
    r_dnear = lax.ppermute(dnear, axes, diag_near)
    r_near = lax.ppermute(near, axes, on_chip)
    return p_bg, r_bg, p_c, r_near, r_far, r_dnear, r_dfar


def exchange_gathered(background, east, north, diff, sensors, observations):
    frames, variables, rows, lon = background.shape
    fields = frames * variables
    half = lon // 2
    tiles, bands = lax.axis_size("tm"), lax.axis_size("lat")
    down = [(j, j + 1) for j in range(bands - 1)]
    up = [(j + 1, j) for j in range(bands - 1)]
    later = [(t, t + 1) for t in range(tiles - 1)]
    earlier = [(t + 1, t) for t in range(tiles - 1)]
    coefs = jnp.stack([east, north, diff - K_MID]).astype(BF)
    coefs = lax.all_gather(coefs, "tm", axis=2, tiled=True)
    around = jnp.concatenate(
        [lax.ppermute(background, "tm", later), lax.ppermute(background, "tm", earlier)], axis=0
    )
    cells = lax.all_to_all(sensors, "tm", split_axis=0, concat_axis=2, tiled=True)[:, 0]
    obs = lax.all_to_all(observations, "tm", split_axis=0, concat_axis=2, tiled=True)[:, 0]
    cells = jnp.moveaxis(cells, 1, 0)
    obs = jnp.transpose(obs, (1, 0, 2, 3))
    obs_high = obs.astype(BF).astype(F32)
    digits = jnp.stack([(cells >> 8).astype(F32), (cells & 255).astype(F32)], axis=2)
    described = jnp.concatenate([digits, obs_high], axis=2).reshape(tiles, -1).astype(BF)
    low = (obs - obs_high).astype(BF).reshape(tiles, -1)
    low = jnp.pad(low, ((0, 0), (0, described.shape[1] - low.shape[1])))
    bands_of = [
        lax.ppermute(described, "lat", down), described, lax.ppermute(described, "lat", up), low
    ]
    sens = jnp.stack([x.reshape(2, tiles // 2, -1) for x in bands_of], axis=1)
    sens = sens.reshape(-1, described.shape[1])

    def block(h):
        part = coefs[:, :, h * half : (h + 1) * half]
        blank = jnp.zeros_like(part[0])
        return jnp.concatenate(
            [jnp.concatenate([part[0], part[2]], axis=1), jnp.concatenate([part[1], blank], axis=1)],
            axis=0,
        )

    def edge_fields(fields_4d, depth, bottom):
        first = rows - depth if bottom else 0
        return fields_4d[:, :, first : first + depth].reshape(-1, lon)

    def edge_coefs(h, bottom):
        first = rows - CROWS if bottom else 0
        part = coefs[:, first : first + CROWS, h * half : (h + 1) * half]
        part = jnp.pad(part.reshape(3 * CROWS, half), ((0, 16 - 3 * CROWS), (0, 0)))
        return jnp.concatenate([part[:8], part[8:]], axis=1)

    received = []
    for bottom, pairs in ((False, up), (True, down)):
        message = [edge_fields(background, HALO, bottom), edge_coefs(0, bottom)]
        message = lax.ppermute(jnp.concatenate(message, axis=0), "lat", pairs)
        diagonal = lax.ppermute(edge_fields(around, 1, bottom), "lat", pairs)
        received.append((message, diagonal, lax.ppermute(edge_coefs(1, bottom), "lat", pairs)))
    (near, dnear, c_near), (far, dfar, c_far) = received
    p_bg, r_bg = background.reshape(-1, lon), around.reshape(-1, lon)
    r_c = jnp.concatenate([block(1), c_near, c_far], axis=0)
    return p_bg, r_bg, block(0), r_c, near, far, dnear, dfar, sens


def shards(
    background, conv_weight, conv_bias, mix_weight, mix_bias, out_weight, out_bias,
    drift_east, drift_north, diffusivity, sensors, observations,
):
    frames, variables, rows, lon = background.shape
    tiles, bands = lax.axis_size("tm"), lax.axis_size("lat")
    paired = tiles == 2 and bands % 2 == 0
    group = rows // 2
    hid = mix_weight.shape[0]
    fields = frames * variables
    arrays = (background, drift_east, drift_north, diffusivity, sensors, observations)
    if paired:
        p_bg, r_bg, p_c, near, far, dnear, dfar = exchange_pairs(*arrays)
        offsets = [[*range(2 * frames)], [*range(frames), *range(-frames, 0)]]
        i_of = lambda: lax.axis_index("tm")
        parity_of = lambda: lax.axis_index("lat") % 2
        sens = ()
    else:
        p_bg, r_bg, p_c, r_c, near, far, dnear, dfar, sens = exchange_gathered(*arrays)
        offsets = [[*range(frames), *range(-frames, 0), *range(frames, 2 * frames)]]
        i_of = lambda: 0
        parity_of = lambda: 0
        sens = (sens,)
    others = len(offsets[0]) - frames

    channels = (frames + others) * variables
    depth = -(-(3 * round16((group + 2) * channels) + 3) // 128) * 128
    quarters = 8 // variables
    width = lon // 8
    taps = jnp.asarray(np.stack([tap_table(o, frames, variables, group, depth) for o in offsets]))
    own, coef, back, halo, chalo, ohalo = model_tables(rows, frames, variables, quarters)
    gather = conv_table(rows, frames, others, variables, group)
    index = np.stack(
        [index_rows([gather[c], *halo[c], chalo[c], own, coef, back, ohalo[c]], 256) for c in range(5)]
    )
    tables = [gather[0], own, coef, back, halo[0], chalo[0], ohalo[0]]
    small = [conv_weight, conv_bias.reshape(1, -1), mix_weight, mix_bias.reshape(1, -1)]
    small += [out_weight, out_bias.reshape(1, -1)]
    with jax.named_scope("weights"):
        weights = call(
            functools.partial(
                prep_kernel, group=group, channels=channels, i_of=i_of, parity_of=parity_of
            ),
            [
                struct((frames * group * hid, depth), BF),
                struct((group * hid, group * hid), BF),
                struct((variables * group, group * hid), BF),
                struct((group * hid, 128), F32),
                struct((variables * group, 128), F32),
            ]
            + [struct(x.shape, BF) for x in tables],
            [pltpu.VMEM(x.shape, x.dtype) for x in small]
            + [pltpu.VMEM(taps.shape[1:], jnp.int32), pltpu.VMEM(index.shape[1:], jnp.int32)]
            + [pltpu.SemaphoreType.DMA((8,))],
            *small, taps, jnp.asarray(index), fetched=range(8),
        )
    if paired:
        with jax.named_scope("own_coefs"):
            p_c = call(hold_kernel, struct(p_c.shape, BF), [], p_c)
        held = (far, near, r_bg, p_c, *weights)
        far, near, r_bg, p_c, *weights = lax.optimization_barrier(held)
        with jax.named_scope("relay"):
            late = call(relay_kernel, struct((2 * rows + 16, lon), BF), [], far, near, p_c)
        dnear, dfar, late = lax.optimization_barrier((dnear, dfar, late))
        r_c = lax.ppermute(late, ("tm", "lat"), swap_pairs(tiles, bands)[0])
    *w_conv, p_conv = weights[:6]
    p_model = weights[6:]
    with jax.named_scope("prior"):
        prior = call(
            functools.partial(
                conv_kernel, frames=frames, variables=variables, group=group, chunk=256
            ),
            struct(background.shape, F32),
            [pltpu.VMEM((rows // group, depth, lon), BF)],
            p_bg, r_bg, near, far, dnear, dfar, *w_conv, p_conv,
            cost=COST,
        )
    tall, ctall = rows + 2 * HALO, rows + 2 * CROWS
    with jax.named_scope("model"):
        return call(
            functools.partial(
                model_kernel, rows=rows, frames=frames, variables=variables,
                tile_cols=drift_east.shape[1], n_sens=sensors.shape[3],
                paired=paired, i_of=i_of, parity_of=parity_of,
            ),
            struct(background.shape, F32),
            [
                pltpu.VMEM((2 * frames, tall, 8, width), F32),
                pltpu.VMEM((2 * frames, tall, 8, width), F32),
                pltpu.VMEM((2, 5, ctall, 8, width), F32),
            ],
            p_bg, p_c, r_c, near, far, dnear, dfar, *sens, prior, *p_model,
        )


def solution(mesh):
    placed = (
        P("tm", None, "lat", None),
        P(),
        P(),
        P(),
        P(),
        P(),
        P(),
        P("lat", "tm"),
        P("lat", "tm"),
        P("lat", "tm"),
        P(None, "lat", "tm", None),
        P(None, "lat", "tm", None, None),
    )
    return jax.shard_map(
        shards, mesh=mesh, in_specs=placed, out_specs=P("tm", None, "lat", None), check_vma=False
    )
```
